128 devices in a mesh: ctx: 16 (over x, y_hi, core), dp: 2 (over y_lo), fsdp: 4 (over z).
Axes of the slice: x: 4, y: 4 (y_hi: 2, y_lo: 2; y = y_hi * 2 + y_lo), z: 4, core: 2. Of those that a mesh axis runs over, the one named last changes fastest.
Arguments:
- hidden_in: bfloat16 [2, 8192, 1024], P('dp', ('ctx', 'fsdp')), may hold values from -6 to 6
- positions: int32 [2, 8192], P('dp', ('ctx', 'fsdp')), may hold values from 0 to 8191, as said below
- attn_gain: bfloat16 [1024], P(('dp', 'fsdp')), may hold values from 0.5 to 1.5
- query_weight: bfloat16 [1024, 2048], P(('dp', 'fsdp')), may hold values from -0.1875 to 0.1875
- key_matrix: bfloat16 [1024, 1024], P(('dp', 'fsdp')), may hold values from -0.1875 to 0.1875
- value_matrix: bfloat16 [1024, 1024], P(('dp', 'fsdp')), may hold values from -0.1875 to 0.1875
- output_weight: bfloat16 [2048, 1024], P(('dp', 'fsdp')), may hold values from -6 to 6
- query_norm_gain: bfloat16 [128], P(('dp', 'fsdp')), may hold values from 0.5 to 1.5
- key_gain: bfloat16 [128], P(('dp', 'fsdp')), may hold values from 0.5 to 1.5
- mlp_gain: bfloat16 [1024], P(('dp', 'fsdp')), may hold values from 0.5 to 1.5
- gate_weight: bfloat16 [1024, 3072], P(('dp', 'fsdp')), may hold values from -0.1875 to 0.1875
- up_weight: bfloat16 [1024, 3072], P(('dp', 'fsdp')), may hold values from -0.1875 to 0.1875
- down_weight: bfloat16 [3072, 1024], P(('dp', 'fsdp')), may hold values from -0.109375 to 0.109375
- cotangent: bfloat16 [2, 8192, 1024], P('dp', ('ctx', 'fsdp')), may hold values from -6 to 6
Outputs:
- layer_out: bfloat16 [2, 8192, 1024], P('dp', ('ctx', 'fsdp'))
- input_grad: float32 [2, 8192, 1024], P('dp', ('ctx', 'fsdp'))
- attn_gain_grad: float32 [1024], P(('dp', 'fsdp'))
- query_weight_grad: float32 [1024, 2048], P(('dp', 'fsdp'))
- key_weight_grad: float32 [1024, 1024], P(('dp', 'fsdp'))
- value_weight_grad: float32 [1024, 1024], P(('dp', 'fsdp'))
- output_weight_grad: float32 [2048, 1024], P(('dp', 'fsdp'))
- query_gain_grad: float32 [128], P(('dp', 'fsdp'))
- key_gain_grad: float32 [128], P(('dp', 'fsdp'))
- mlp_gain_grad: float32 [1024], P(('dp', 'fsdp'))
- gate_weight_grad: float32 [1024, 3072], P(('dp', 'fsdp'))
- up_weight_grad: float32 [1024, 3072], P(('dp', 'fsdp'))
- down_weight_grad: float32 [3072, 1024], P(('dp', 'fsdp'))
The draws below stay inside these ranges and needn't reach their ends.
Inputs may be any that keep to these rules, and one draw needn't show every extreme that they name: In each sequence the positions take every value 0 to 8191 once; they come in runs of 128 consecutive rising positions that start at multiples of 128, one run to each device, in an order drawn at random.
All inputs are finite; a program needn't handle non-finite values.
Results may differ from the reference program's by a relative error of at most 0.025.
Values may be sent and summed in bfloat16 or wider, within the bound.
A program may use at most 448 MiB of HBM per device.

```python
import math
import jax
import jax.numpy as jnp
from jax import lax

MODEL_WIDTH = 1024
QUERY_HEADS = 16
KEY_VALUE_HEADS = 8
HEAD_SIZE = 128
FF = 3072
TOK_DEV = 128
SEQS = 2
LEN = 8192


def draw_positions(key, part):
    key = jax.random.fold_in(key, 11)
    runs = LEN // TOK_DEV
    seeds = jax.random.split(key, SEQS)
    order = jax.vmap(lambda single: jax.random.permutation(single, runs))(seeds)
    offsets = jnp.arange(TOK_DEV, dtype=jnp.int32)
    places = order.astype(jnp.int32)[:, :, None] * TOK_DEV + offsets[None, None, :]
    return places.reshape(SEQS, LEN)


def shard_levels(rng, shape, cuts, low, high):
    level = 1.0
    for dim, blocks in cuts:
        heights = jax.random.uniform(jax.random.fold_in(jax.random.fold_in(rng, 6), dim), (blocks,), jnp.float32, low / len(cuts), high / len(cuts))
        level = level * jnp.repeat(jnp.exp(heights), shape[dim] // blocks).reshape((-1,) + (1,) * (len(shape) - 1 - dim))
    return level


def gaussian(key, shape, spread, bound, pieces=(), held_as=jnp.bfloat16):
    level = shard_levels(key, shape, pieces, -0.22, 0.18) if pieces else 1.0
    entries = jax.random.normal(key, shape, jnp.float32) * spread * level
    return jnp.minimum(jnp.maximum(entries, -bound), bound).astype(held_as)


def setup_inputs(seed: int = 0) -> dict:
    key_list = jax.random.split(jax.random.key(seed), 15)
    hidden_in = gaussian(key_list[0], (SEQS, LEN, MODEL_WIDTH), 1.0, 6.0, ((0, 2), (1, 64)))
    positions = draw_positions(jax.random.fold_in(key_list[14], 71), 0)
    attn_gain = jnp.clip(1.0 + 0.1 * jax.random.normal(key_list[2], (MODEL_WIDTH,), jnp.float32), 0.5, 1.5).astype(jnp.bfloat16)
    query_weight = gaussian(key_list[3], (MODEL_WIDTH, QUERY_HEADS * HEAD_SIZE), MODEL_WIDTH ** -0.5, 0.1875, ((0, 8),))
    key_matrix = gaussian(key_list[4], (MODEL_WIDTH, KEY_VALUE_HEADS * HEAD_SIZE), MODEL_WIDTH ** -0.5, 0.1875, ((0, 8),))
    value_matrix = gaussian(key_list[5], (MODEL_WIDTH, KEY_VALUE_HEADS * HEAD_SIZE), MODEL_WIDTH ** -0.5, 0.1875, ((0, 8),))
    output_weight = gaussian(key_list[6], (QUERY_HEADS * HEAD_SIZE, MODEL_WIDTH), (max(1, 4 * QUERY_HEADS * HEAD_SIZE // LEN)) ** -0.5, 6.0, ((0, 8),))
    query_norm_gain = jnp.clip(1.0 + 0.1 * jax.random.normal(key_list[7], (HEAD_SIZE,), jnp.float32), 0.5, 1.5).astype(jnp.bfloat16)
    key_gain = jnp.clip(1.0 + 0.1 * jax.random.normal(key_list[8], (HEAD_SIZE,), jnp.float32), 0.5, 1.5).astype(jnp.bfloat16)
    mlp_gain = jnp.clip(1.0 + 0.1 * jax.random.normal(key_list[9], (MODEL_WIDTH,), jnp.float32), 0.5, 1.5).astype(jnp.bfloat16)
    gate_weight = gaussian(key_list[10], (MODEL_WIDTH, FF), MODEL_WIDTH ** -0.5, 0.1875, ((0, 8),))
    up_weight = gaussian(key_list[11], (MODEL_WIDTH, FF), MODEL_WIDTH ** -0.5, 0.1875, ((0, 8),))
    down_weight = gaussian(key_list[12], (FF, MODEL_WIDTH), FF ** -0.5, 0.109375, ((0, 8),))
    cotangent = gaussian(key_list[13], (SEQS, LEN, MODEL_WIDTH), 1.0, 6.0, ((0, 2), (1, 64)))
    return {"hidden_in": hidden_in, "positions": positions, "attn_gain": attn_gain, "query_weight": query_weight, "key_matrix": key_matrix, "value_matrix": value_matrix, "output_weight": output_weight, "query_norm_gain": query_norm_gain, "key_gain": key_gain, "mlp_gain": mlp_gain, "gate_weight": gate_weight, "up_weight": up_weight, "down_weight": down_weight, "cotangent": cotangent}


@jax.custom_vjp
def reduced_precision(v):
    return lax.optimization_barrier(v.astype(jnp.bfloat16)).astype(jnp.float32)

@jax.custom_vjp
def reduced_reverse(v):
    return v

def low_keep(v):
    return (reduced_precision(v), None)

def low_pass(kept, grad):
    return (grad,)

def back_keep(v):
    return (v, None)

def back_low(kept, grad):
    return (reduced_precision(grad),)
reduced_precision.defvjp(low_keep, low_pass)
reduced_reverse.defvjp(back_keep, back_low)
EPS = 1e-06
THETA = 1000000.0
NEGATIVE_LIMIT = -1e+30
HIGH_PRECISION = lax.Precision.HIGHEST

def root_mean_square_norm(value, gain):
    return value * lax.rsqrt(lax.optimization_barrier(jnp.mean(value * value, axis=-1, keepdims=True)) + EPS) * gain

def rotary_tables(places, width):
    inverse = 1.0 / THETA ** (jnp.arange(0, width, 2, dtype=jnp.float32) / width)
    angle = places.astype(jnp.float32)[:, None] * inverse[None, :]
    return (jnp.cos(angle)[:, None, :], jnp.sin(angle)[:, None, :])

def apply_rotary(value, cosine_table, sine_table):
    half = value.shape[-1] // 2
    first, second = (value[..., :half], value[..., half:])
    return jnp.concatenate([first * cosine_table - second * sine_table, second * cosine_table + first * sine_table], axis=-1)

def attention(query_rows, key_tensor, value_tensor, places):
    length_total = query_rows.shape[0]
    block_tile = math.gcd(length_total, 512)
    count_total = length_total // block_tile
    scale = HEAD_SIZE ** (-0.5)
    query_tile_blocks = query_rows.reshape(count_total, block_tile, KEY_VALUE_HEADS, QUERY_HEADS // KEY_VALUE_HEADS, HEAD_SIZE)
    place_blocks = places.reshape(count_total, block_tile)

    def one_block(inputs):
        row_count, row_places = inputs
        scores = reduced_reverse(jnp.einsum('tkgd,rkd->kgtr', row_count, key_tensor, precision=HIGH_PRECISION) * scale)
        allowed = row_places[:, None] >= places[None, :]
        peak = lax.optimization_barrier(jnp.max(jnp.where(allowed, scores, NEGATIVE_LIMIT), axis=-1, keepdims=True))
        weights = jnp.where(allowed, jnp.exp(scores - peak), 0.0)
        total = lax.optimization_barrier(jnp.sum(weights, axis=-1, keepdims=True))
        summed = jnp.einsum('kgtr,rkd->kgtd', reduced_precision(weights), value_tensor, precision=HIGH_PRECISION)
        return jnp.transpose(summed / total, (2, 0, 1, 3))
    result = lax.map(jax.checkpoint(one_block), (query_tile_blocks, place_blocks))
    return result.reshape(length_total, QUERY_HEADS * HEAD_SIZE)

def layer(hidden, places, attn_gain, query_weight, key_matrix, value_matrix, output_weight, query_norm_gain, key_gain, mlp_gain, gate_weight, up_weight, down_weight):
    length_total = hidden.shape[0]
    cosine_table, sine_table = rotary_tables(places, HEAD_SIZE)
    first_norm = reduced_precision(root_mean_square_norm(hidden, attn_gain))
    query_prenorm = reduced_reverse(jnp.dot(first_norm, query_weight, precision=HIGH_PRECISION)).reshape(length_total, QUERY_HEADS, HEAD_SIZE)
    key_prenorm = reduced_reverse(jnp.dot(first_norm, key_matrix, precision=HIGH_PRECISION)).reshape(length_total, KEY_VALUE_HEADS, HEAD_SIZE)
    value_tensor = reduced_precision(reduced_reverse(jnp.dot(first_norm, value_matrix, precision=HIGH_PRECISION))).reshape(length_total, KEY_VALUE_HEADS, HEAD_SIZE)
    query_rows = reduced_precision(apply_rotary(root_mean_square_norm(query_prenorm, query_norm_gain), cosine_table, sine_table)).reshape(length_total, KEY_VALUE_HEADS, QUERY_HEADS // KEY_VALUE_HEADS, HEAD_SIZE)
    key_tensor = reduced_precision(apply_rotary(root_mean_square_norm(key_prenorm, key_gain), cosine_table, sine_table))
    mixed = reduced_precision(reduced_reverse(attention(query_rows, key_tensor, value_tensor, places)))
    middle = hidden + reduced_reverse(jnp.dot(mixed, output_weight, precision=HIGH_PRECISION))
    norm_two = reduced_precision(root_mean_square_norm(middle, mlp_gain))
    gate = reduced_reverse(jnp.dot(norm_two, gate_weight, precision=HIGH_PRECISION))
    up = reduced_reverse(jnp.dot(norm_two, up_weight, precision=HIGH_PRECISION))
    inner = reduced_precision(jax.nn.silu(gate) * up)
    return middle + reduced_reverse(jnp.dot(inner, down_weight, precision=HIGH_PRECISION))

def reference(hidden_in, positions, attn_gain, query_weight, key_matrix, value_matrix, output_weight, query_norm_gain, key_gain, mlp_gain, gate_weight, up_weight, down_weight, cotangent):
    params = tuple((w.astype(jnp.float32) for w in (attn_gain, query_weight, key_matrix, value_matrix, output_weight, query_norm_gain, key_gain, mlp_gain, gate_weight, up_weight, down_weight)))
    outputs = []
    input_grads = []
    sums = None
    for index in range(SEQS):
        places = positions[index]

        def forward(hidden, *weights):
            return layer(hidden, places, *weights)
        result, pullback = jax.vjp(forward, hidden_in[index].astype(jnp.float32), *params)
        grads = pullback(cotangent[index].astype(jnp.float32))
        outputs.append(result.astype(jnp.bfloat16))
        input_grads.append(grads[0])
        if sums is None:
            sums = tuple(grads[1:])
        else:
            sums = tuple((a + b for a, b in zip(sums, grads[1:])))
    return (jnp.stack(outputs), jnp.stack(input_grads), sums[0], sums[1], sums[2], sums[3], sums[4], sums[5], sums[6], sums[7], sums[8], sums[9], sums[10])
```

```python
import functools

import jax
import jax.numpy as jnp
from jax import lax
from jax.experimental import pallas as pl
from jax.experimental.pallas import tpu as pltpu
from jax.sharding import PartitionSpec as P

HEAD = 128
EPS = 1e-06
THETA = 1000000.0
SCALE = HEAD ** (-0.5)
LOG2E = 1.4426950408889634
RUN = 128
CHUNK = 512
BF = jnp.bfloat16
F32 = jnp.float32
MESH = pl.DeviceIdType.MESH


class Place:
    def __init__(self):
        self.ctx = lax.axis_index("ctx")
        self.dp = lax.axis_index("dp")
        self.fsdp = lax.axis_index("fsdp")
        self.chip = self.ctx // 2
        self.core = self.ctx % 2


def spread_tokens(me, k):
    head = me.dp * 4 + me.fsdp
    mine = me.core * 4 + me.fsdp
    n = (head + k) % 8
    slot = (mine + k) % 8
    dest = (me.chip * 2 + me.dp, n // 4, n % 4)
    source = (me.chip * 2 + slot // 4, me.core, slot % 4)
    return dest, n, source, slot, mine, me.core == me.dp


def return_tokens(me, k):
    head = me.dp * 4 + me.fsdp
    mine = me.core * 4 + me.fsdp
    n = (mine + k) % 8
    slot = (head + k) % 8
    dest = (me.chip * 2 + n // 4, me.core, n % 4)
    source = (me.chip * 2 + me.dp, slot // 4, slot % 4)
    return dest, n, source, slot, head, me.core == me.dp


def weight_group(me, k):
    head = me.dp * 4 + me.fsdp
    n = (head + k) % 8
    slot = (head + 8 - k) % 8
    dest = (me.ctx, n // 4, n % 4)
    source = (me.ctx, slot // 4, slot % 4)
    return dest, n, source, slot, head, True


def chips(me, k):
    n = (me.chip + k) % 8
    slot = (me.chip + 8 - k) % 8
    dest = (n * 2 + me.core, me.dp, me.fsdp)
    source = (slot * 2 + me.core, me.dp, me.fsdp)
    return dest, n, source, slot, me.chip, True


def exchange(moves, collective_id, out_shapes, *arrays):
    n_in, n_out = len(arrays), len(out_shapes)
    patterns = []
    for move in moves:
        if move[0] not in patterns:
            patterns.append(move[0])

    def kernel(*refs):
        ins, outs = refs[:n_in], refs[n_in : n_in + n_out]
        send_sem, recv_sem = refs[n_in + n_out :]
        me = Place()
        barrier = pltpu.get_barrier_semaphore()
        count = 0
        for pattern in patterns:
            for k in range(8):
                _, _, source, _, _, stays = pattern(me, k)
                if k == 0:
                    if stays is True:
                        continue

                    @pl.when(jnp.logical_not(stays))
                    def _():
                        pl.semaphore_signal(barrier, inc=1, device_id=source, device_id_type=MESH)

                    count = count + jnp.where(stays, 0, 1)
                else:
                    pl.semaphore_signal(barrier, inc=1, device_id=source, device_id_type=MESH)
                    count = count + 1
        pl.semaphore_wait(barrier, count)

        def remote(t, k):
            pattern, a, b, block, landing = moves[t]
            dest, n, _, slot, mine, _ = pattern(me, k)
            return pltpu.make_async_remote_copy(
                src_ref=block(ins[a], n),
                dst_ref=landing(outs[b], mine),
                send_sem=send_sem.at[t, k],
                recv_sem=recv_sem.at[t, mine],
                device_id=dest,
                device_id_type=MESH,
            )

        def arrival(t, k):
            pattern, a, b, block, landing = moves[t]
            dest, n, _, slot, mine, _ = pattern(me, k)
            return pltpu.make_async_remote_copy(
                src_ref=block(ins[a], n),
                dst_ref=landing(outs[b], slot),
                send_sem=send_sem.at[t, k],
                recv_sem=recv_sem.at[t, slot],
                device_id=dest,
                device_id_type=MESH,
            )

        def local(t):
            pattern, a, b, block, landing = moves[t]
            _, n, _, _, mine, _ = pattern(me, 0)
            return pltpu.make_async_copy(
                block(ins[a], n), landing(outs[b], mine), send_sem.at[t, 0]
            )

        def split(t, here, there):
            stays = moves[t][0](me, 0)[-1]
            if stays is True:
                here()
            else:
                pl.when(stays)(here)
                pl.when(jnp.logical_not(stays))(there)

        for k in range(1, 8):
            for t in range(len(moves)):
                remote(t, k).start()
        for t in range(len(moves)):
            split(t, lambda: local(t).start(), lambda: remote(t, 0).start())
        for t in range(len(moves)):
            split(t, lambda: local(t).wait(), lambda: remote(t, 0).wait_send())
            split(t, lambda: None, lambda: arrival(t, 0).wait_recv())
            for k in range(1, 8):
                remote(t, k).wait_send()
                arrival(t, k).wait_recv()

    return pl.pallas_call(
        kernel,
        out_shape=tuple(jax.ShapeDtypeStruct(s, d) for s, d in out_shapes),
        in_specs=[pl.BlockSpec(memory_space=pl.ANY)] * n_in,
        out_specs=tuple([pl.BlockSpec(memory_space=pl.ANY)] * n_out),
        scratch_shapes=[
            pltpu.SemaphoreType.DMA((len(moves), 8)),
            pltpu.SemaphoreType.DMA((len(moves), 8)),
        ],
        compiler_params=pltpu.CompilerParams(collective_id=collective_id, has_side_effects=True),
        name="exchange_%d" % collective_id,
    )(*arrays)


def whole(ref, n):
    return ref


def rows(size):
    def pick(ref, n):
        return ref.at[pl.ds(pl.multiple_of(n * size, size), size)]

    return pick


def columns(size):
    def pick(ref, n):
        return ref.at[:, pl.ds(pl.multiple_of(n * size, size), size)]

    return pick


def rows_at(size, start, width):
    def pick(ref, n):
        return ref.at[pl.ds(pl.multiple_of(n * size, size), size), pl.ds(start, width)]

    return pick


NT = (((1,), (1,)), ((), ()))
NN = (((1,), (0,)), ((), ()))


def mm(a, b, dims=NN):
    return lax.dot_general(a, b, dims, preferred_element_type=F32)


def stacked(ref):
    return jnp.concatenate([ref[:, :HEAD], ref[:, HEAD:]], axis=0)


def forward_kernel(order, own, q_ref, kv_ref, o_ref, l_ref, keys, vals, acc):
    step = pl.program_id(0)
    n_runs = order.shape[0]

    @pl.when(step == 0)
    def _():
        def place(r, _):
            src = pl.ds(pl.multiple_of(r * RUN, RUN), RUN)
            dst = pl.ds(pl.multiple_of(order[r] * RUN, RUN), RUN)
            keys[dst, :] = kv_ref[src, :HEAD]
            vals[dst, :HEAD] = kv_ref[src, HEAD:]
            vals[dst, HEAD:] = jnp.ones((RUN, HEAD), BF)
            return 0

        lax.fori_loop(0, n_runs, place, 0)

    run = own[step]
    query = stacked(q_ref)
    acc[...] = jnp.zeros_like(acc)

    def visit(j, masked):
        at = pl.ds(pl.multiple_of(j * CHUNK, CHUNK), CHUNK)
        s = mm(query, keys[at, :], NT)
        p = jnp.exp2(s * (SCALE * LOG2E))
        if masked:
            row = lax.broadcasted_iota(jnp.int32, p.shape, 0) % RUN + run * RUN
            col = lax.broadcasted_iota(jnp.int32, p.shape, 1) + j * CHUNK
            p = jnp.where(col <= row, p, 0.0)
        acc[...] += mm(p.astype(BF), vals[at, :])

    last = run // (CHUNK // RUN)

    def plain(j, _):
        visit(j, False)
        return 0

    lax.fori_loop(0, last, plain, 0)
    visit(last, True)
    total = acc[:, HEAD:]
    out = acc[:, :HEAD] / total
    log = jnp.log2(total)
    o_ref[:, :HEAD] = out[:RUN]
    o_ref[:, HEAD:] = out[RUN:]
    l_ref[:, :HEAD] = log[:RUN]
    l_ref[:, HEAD:] = log[RUN:]


def attention_forward(order, own, q, kv):
    length = kv.shape[0]
    tokens = q.shape[0]
    block = pl.BlockSpec((RUN, 2 * HEAD), lambda i, *_: (i, 0))
    return pl.pallas_call(
        forward_kernel,
        grid_spec=pltpu.PrefetchScalarGridSpec(
            num_scalar_prefetch=2,
            grid=(tokens // RUN,),
            in_specs=[block, pl.BlockSpec((length, 2 * HEAD), lambda i, *_: (0, 0))],
            out_specs=[block, block],
            scratch_shapes=[
                pltpu.VMEM((length, HEAD), BF),
                pltpu.VMEM((length, 2 * HEAD), BF),
                pltpu.VMEM((2 * RUN, 2 * HEAD), F32),
            ],
        ),
        out_shape=(jax.ShapeDtypeStruct(q.shape, F32), jax.ShapeDtypeStruct(q.shape, F32)),
        compiler_params=pltpu.CompilerParams(
            dimension_semantics=("arbitrary",), vmem_limit_bytes=48 * 2**20
        ),
        name="attention_forward",
    )(order, own, q, kv)


def backward_kernel(
    order, own, q_ref, g_ref, o_ref, l_ref, kv_ref, dq_ref, dkv_ref,
    keys, keys_t, vals, dk, dv, dq_t, q_t, g_t,
):
    step = pl.program_id(0)
    n_runs = order.shape[0]

    @pl.when(step == 0)
    def _():
        dk[...] = jnp.zeros_like(dk)
        dv[...] = jnp.zeros_like(dv)

        def place(r, _):
            src = pl.ds(pl.multiple_of(r * RUN, RUN), RUN)
            dst = pl.ds(pl.multiple_of(order[r] * RUN, RUN), RUN)
            k = kv_ref[src, :HEAD]
            keys[dst, :] = k
            keys_t[:, dst] = k.T
            vals[dst, :] = kv_ref[src, HEAD:]
            return 0

        lax.fori_loop(0, n_runs, place, 0)

    run = own[step]
    query = stacked(q_ref)
    grad = stacked(g_ref)
    q_t[...] = query.T
    g_t[...] = grad.T
    delta = jnp.sum((grad.astype(F32) * stacked(o_ref)).T, axis=0, keepdims=True)
    log = stacked(l_ref).T[:1]
    dq_t[...] = jnp.zeros_like(dq_t)

    def visit(j, masked):
        at = pl.ds(pl.multiple_of(j * CHUNK, CHUNK), CHUNK)
        s = mm(keys[at, :], q_t[...])
        p = jnp.exp2(s * (SCALE * LOG2E) - log)
        if masked:
            row = lax.broadcasted_iota(jnp.int32, p.shape, 1) % RUN + run * RUN
            col = lax.broadcasted_iota(jnp.int32, p.shape, 0) + j * CHUNK
            p = jnp.where(col <= row, p, 0.0)
        dp = mm(vals[at, :], g_t[...])
        ds = (p * (dp - delta)).astype(BF)
        dv[at, :] += mm(p.astype(BF), grad)
        dk[at, :] += mm(ds, query)
        dq_t[...] += mm(keys_t[:, at], ds)

    last = run // (CHUNK // RUN)

    def plain(j, _):
        visit(j, False)
        return 0

    lax.fori_loop(0, last, plain, 0)
    visit(last, True)
    out = dq_t[...].T * SCALE
    dq_ref[:, :HEAD] = out[:RUN]
    dq_ref[:, HEAD:] = out[RUN:]

    @pl.when(step == pl.num_programs(0) - 1)
    def _():
        def give(r, _):
            dst = pl.ds(pl.multiple_of(r * RUN, RUN), RUN)
            src = pl.ds(pl.multiple_of(order[r] * RUN, RUN), RUN)
            dkv_ref[dst, :HEAD] = (dk[src, :] * SCALE).astype(BF)
            dkv_ref[dst, HEAD:] = dv[src, :].astype(BF)
            return 0

        lax.fori_loop(0, n_runs, give, 0)


def attention_backward(order, own, q, g, o, log, kv):
    length = kv.shape[0]
    tokens = q.shape[0]
    block = pl.BlockSpec((RUN, 2 * HEAD), lambda i, *_: (i, 0))
    all_rows = pl.BlockSpec((length, 2 * HEAD), lambda i, *_: (0, 0))
    return pl.pallas_call(
        backward_kernel,
        grid_spec=pltpu.PrefetchScalarGridSpec(
            num_scalar_prefetch=2,
            grid=(tokens // RUN,),
            in_specs=[block, block, block, block, all_rows],
            out_specs=[block, all_rows],
            scratch_shapes=[
                pltpu.VMEM((length, HEAD), BF),
                pltpu.VMEM((HEAD, length), BF),
                pltpu.VMEM((length, HEAD), BF),
                pltpu.VMEM((length, HEAD), F32),
                pltpu.VMEM((length, HEAD), F32),
                pltpu.VMEM((HEAD, 2 * RUN), F32),
                pltpu.VMEM((HEAD, 2 * RUN), BF),
                pltpu.VMEM((HEAD, 2 * RUN), BF),
            ],
        ),
        out_shape=(jax.ShapeDtypeStruct(q.shape, F32), jax.ShapeDtypeStruct(kv.shape, BF)),
        compiler_params=pltpu.CompilerParams(
            dimension_semantics=("arbitrary",), vmem_limit_bytes=48 * 2**20
        ),
        name="attention_backward",
    )(order, own, q, g, o, log, kv)


def rotate(value, cos, sin):
    a, b = value[..., : HEAD // 2], value[..., HEAD // 2 :]
    return jnp.concatenate([a * cos - b * sin, b * cos + a * sin], axis=-1)


def rotate_back(grad, cos, sin):
    a, b = grad[..., : HEAD // 2], grad[..., HEAD // 2 :]
    return jnp.concatenate([a * cos + b * sin, b * cos - a * sin], axis=-1)


def inverse_rms(value):
    return lax.rsqrt(jnp.mean(value * value, axis=-1, keepdims=True) + EPS)


def norm_back(value, inverse, gain, grad):
    scaled = grad * gain
    inner = jnp.sum(scaled * value, axis=-1, keepdims=True)
    return inverse * scaled - value * inverse * inverse * inverse * inner / value.shape[-1]


def dot(a, b):
    return jnp.dot(a, b, preferred_element_type=F32)


def dot_t(a, b):
    return lax.dot_general(a, b, (((0,), (0,)), ((), ())), preferred_element_type=F32)


def summed(parts, count):
    return jnp.sum(parts.reshape((count, -1) + parts.shape[1:]).astype(F32), axis=0)


def row_of(vector):
    return jnp.pad(vector.reshape(1, -1), ((0, 0), (0, 128 - vector.shape[-1])))


def local(
    hidden_in, positions, attn_gain, query_weight, key_matrix, value_matrix, output_weight,
    query_norm_gain, key_gain, mlp_gain, gate_weight, up_weight, down_weight, cotangent,
):
    hidden = hidden_in[0]
    cot = cotangent[0]
    tokens, width = hidden.shape
    group = 8 * tokens
    ff = gate_weight.shape[1] // 8
    part = width // 8

    place_tile = jnp.broadcast_to(positions, (8, tokens))
    gain_tile = jnp.concatenate(
        [row_of(g.astype(F32)) for g in (attn_gain, mlp_gain, query_norm_gain, key_gain)]
        + [jnp.zeros((4, 128), F32)],
        axis=0,
    )
    x_all, places, gains, w_qkv = exchange(
        (
            (spread_tokens, 0, 0, whole, rows(tokens)),
            (spread_tokens, 1, 1, whole, rows(8)),
            (weight_group, 2, 2, whole, rows(8)),
            (weight_group, 3, 3, columns(256), rows_at(part, 0, 256)),
            (weight_group, 4, 3, columns(128), rows_at(part, 256, 128)),
            (weight_group, 5, 3, columns(128), rows_at(part, 384, 128)),
        ),
        1,
        (((group, width), BF), ((64, tokens), jnp.int32), ((64, 128), F32), ((width, 512), BF)),
        hidden, place_tile, gain_tile, query_weight, key_matrix, value_matrix,
    )
    gains = gains.reshape(8, 8, 128)
    attn_scale = gains[:, 0].reshape(1, width)
    mlp_scale = gains[:, 1].reshape(1, width)
    query_scale = gains[:, 2, :16].reshape(1, HEAD)
    key_scale = gains[:, 3, :16].reshape(1, HEAD)

    x_wide = x_all.astype(F32)
    attn_inverse_all = inverse_rms(x_wide)
    norm_one = (x_wide * attn_inverse_all * attn_scale).astype(BF)
    qkv = dot(norm_one, w_qkv)
    pre = qkv[:, :384].reshape(group, 3, HEAD)
    head_scale = jnp.stack([query_scale, query_scale, key_scale], axis=1)
    head_inverse = inverse_rms(pre)
    place_rows = places.reshape(8, 8, tokens)[:, 0].reshape(group)
    frequency = 1.0 / THETA ** (jnp.arange(0, HEAD, 2, dtype=F32) / HEAD)
    angle = place_rows.astype(F32)[:, None] * frequency[None, :]
    cos, sin = jnp.cos(angle)[:, None, :], jnp.sin(angle)[:, None, :]
    turned = rotate(pre * head_inverse * head_scale, cos, sin).astype(BF).reshape(group, 384)
    queries = turned[:, :256]
    kv = jnp.concatenate([turned[:, 256:], qkv[:, 384:].astype(BF)], axis=1)

    kv_all, all_places, cot_all, w_gu = exchange(
        (
            (chips, 0, 0, whole, rows(group)),
            (chips, 1, 1, whole, rows(64)),
            (spread_tokens, 2, 2, whole, rows(tokens)),
            (weight_group, 3, 3, columns(ff), rows_at(part, 0, ff)),
            (weight_group, 4, 3, columns(ff), rows_at(part, ff, ff)),
        ),
        2,
        (((8 * group, 256), BF), ((512, tokens), jnp.int32), ((group, width), BF), ((width, 2 * ff), BF)),
        kv, places, cot, gate_weight, up_weight,
    )
    order = all_places.reshape(64, 8, tokens)[:, 0, 0] // RUN
    own = places.reshape(8, 8, tokens)[:, 0, 0] // RUN
    attention, log_total = attention_forward(order, own, queries, kv_all)
    mixed = attention.astype(BF)
    branch_part = dot(mixed, output_weight).astype(BF)

    (branch,) = exchange(
        ((return_tokens, 0, 0, rows(tokens), rows(tokens)),), 3, (((group, width), BF),), branch_part
    )
    residual = hidden.astype(F32)
    middle = residual + summed(branch, 8)
    mlp_inverse = inverse_rms(middle)
    norm_two_own = (middle * mlp_inverse * mlp_scale).astype(BF)

    (norm_two,) = exchange(
        ((spread_tokens, 0, 0, whole, rows(tokens)),), 4, (((group, width), BF),), norm_two_own
    )
    gate_up = dot(norm_two, w_gu)
    gate, up = gate_up[:, :ff], gate_up[:, ff:]
    sigma = jax.nn.sigmoid(gate)
    swish = gate * sigma
    inner = (swish * up).astype(BF)
    inner_grad = lax.dot_general(cot_all, down_weight, NT, preferred_element_type=F32)
    gate_up_grad = jnp.concatenate(
        [
            (inner_grad * up * sigma * (1.0 + gate * (1.0 - sigma))).astype(BF),
            (inner_grad * swish).astype(BF),
        ],
        axis=1,
    )
    norm_two_part = lax.dot_general(gate_up_grad, w_gu, NT, preferred_element_type=F32).astype(BF)

    (norm_two_parts,) = exchange(
        ((return_tokens, 0, 0, rows(tokens), rows(tokens)),), 5, (((group, width), BF),), norm_two_part
    )
    norm_two_grad = summed(norm_two_parts, 8)
    middle_grad = cot.astype(F32) + norm_back(middle, mlp_inverse, mlp_scale, norm_two_grad)
    mlp_gain_part = jnp.sum(norm_two_grad * middle * mlp_inverse, axis=0)
    branch_grad_own = middle_grad.astype(BF)
    down_part = dot(inner, down_weight).astype(BF)
    down_wgrad = dot_t(inner, cot_all).astype(BF)
    gate_up_wgrad = dot_t(norm_two, gate_up_grad).astype(BF)

    branch_grad, gate_wgrad, up_wgrad = exchange(
        (
            (spread_tokens, 0, 0, whole, rows(tokens)),
            (weight_group, 1, 1, lambda r, n: rows_at(part, 0, ff)(r, n), columns(ff)),
            (weight_group, 1, 2, lambda r, n: rows_at(part, ff, ff)(r, n), columns(ff)),
        ),
        6,
        (((group, width), BF), ((part, 8 * ff), BF), ((part, 8 * ff), BF)),
        branch_grad_own, gate_up_wgrad,
    )
    mixed_grad = lax.dot_general(branch_grad, output_weight, NT, preferred_element_type=F32).astype(BF)
    output_wgrad = dot_t(mixed, branch_grad).astype(BF)
    gate_wgrad, up_wgrad, down_wgrad, output_wgrad = lax.psum(
        (gate_wgrad, up_wgrad, down_wgrad, output_wgrad), "ctx"
    )
    query_turn, kv_part = attention_backward(
        order, own, queries, mixed_grad, attention, log_total, kv_all
    )

    kv_parts, down_parts = exchange(
        (
            (chips, 0, 0, rows(group), rows(group)),
            (return_tokens, 1, 1, rows(tokens), rows(tokens)),
        ),
        7,
        (((8 * group, 256), BF), ((group, width), BF)),
        kv_part, down_part,
    )
    layer_out = (middle + summed(down_parts, 8)).astype(BF)
    kv_sum = summed(kv_parts, 8)
    turn = jnp.concatenate([query_turn, kv_sum[:, :HEAD]], axis=1).reshape(group, 3, HEAD)
    head_grad = rotate_back(turn, cos, sin)
    pre_grad = norm_back(pre, head_inverse, head_scale, head_grad)
    head_gain_parts = jnp.sum(head_grad * pre * head_inverse, axis=0)
    qkv_grad = jnp.concatenate(
        [pre_grad.reshape(group, 384).astype(BF), kv_sum[:, HEAD:].astype(BF)], axis=1
    )
    qkv_wgrad = dot_t(norm_one, qkv_grad).astype(BF)
    norm_one_wide = lax.dot_general(qkv_grad, w_qkv, NT, preferred_element_type=F32)
    attn_gain_part = jnp.sum(norm_one_wide * x_wide * attn_inverse_all, axis=0)
    query_gain_part = (head_gain_parts[0] + head_gain_parts[1]).reshape(8, 1, 16)
    key_gain_part = head_gain_parts[2].reshape(8, 1, 16)
    gain_parts = jnp.concatenate(
        [
            attn_gain_part.reshape(8, 1, 128),
            mlp_gain_part.reshape(8, 1, 128),
            jnp.pad(query_gain_part, ((0, 0), (0, 0), (0, 112))),
            jnp.pad(key_gain_part, ((0, 0), (0, 0), (0, 112))),
            jnp.zeros((8, 4, 128), F32),
        ],
        axis=1,
    ).reshape(64, 128)

    norm_one_parts, query_wgrad, key_wgrad, value_wgrad, gain_sums = exchange(
        (
            (return_tokens, 0, 0, rows(tokens), rows(tokens)),
            (weight_group, 1, 1, rows_at(part, 0, 256), columns(256)),
            (weight_group, 1, 2, rows_at(part, 256, 128), columns(128)),
            (weight_group, 1, 3, rows_at(part, 384, 128), columns(128)),
            (weight_group, 2, 4, rows(8), rows(8)),
        ),
        8,
        (
            ((group, width), BF), ((part, 2048), BF), ((part, 1024), BF), ((part, 1024), BF),
            ((64, 128), F32),
        ),
        norm_one_wide.astype(BF), qkv_wgrad, gain_parts,
    )
    gain_sum = summed(gain_sums, 8)
    query_wgrad, key_wgrad, value_wgrad, gain_sum = lax.psum(
        (query_wgrad, key_wgrad, value_wgrad, gain_sum.astype(BF)), "ctx"
    )
    attn_inverse = inverse_rms(residual)
    input_grad = middle_grad + norm_back(residual, attn_inverse, attn_scale, summed(norm_one_parts, 8))
    gain_sum = gain_sum.astype(F32)
    return (
        layer_out[None],
        input_grad[None],
        gain_sum[0],
        query_wgrad.astype(F32),
        key_wgrad.astype(F32),
        value_wgrad.astype(F32),
        output_wgrad.astype(F32),
        gain_sum[2, :16],
        gain_sum[3, :16],
        gain_sum[1],
        gate_wgrad.astype(F32),
        up_wgrad.astype(F32),
        down_wgrad.astype(F32),
    )


def solution(mesh):
    tokens = P("dp", ("ctx", "fsdp"), None)
    places = P("dp", ("ctx", "fsdp"))
    vector = P(("dp", "fsdp"))
    matrix = P(("dp", "fsdp"), None)
    in_specs = (
        tokens, places, vector, matrix, matrix, matrix, matrix,
        vector, vector, vector, matrix, matrix, matrix, tokens,
    )
    out_specs = (
        tokens, tokens, vector, matrix, matrix, matrix, matrix,
        vector, vector, vector, matrix, matrix, matrix,
    )
    return jax.shard_map(local, mesh=mesh, in_specs=in_specs, out_specs=out_specs, check_vma=False)
```

```python
import jax
import jax.numpy as jnp
from jax import lax
from jax.experimental import pallas as pl
from jax.experimental.pallas import tpu as pltpu
from jax.sharding import PartitionSpec as P

HEAD = 128
EPS = 1e-06
THETA = 1000000.0
SCALE = HEAD ** (-0.5)
LOG2E = 1.4426950408889634
RUN = 128
CHUNK = 512
TAG = 16
X_ROWS = RUN + TAG
KV_ROWS = 8 * RUN + TAG
BF = jnp.bfloat16
F32 = jnp.float32
MESH = pl.DeviceIdType.MESH


class At:
    def __init__(self, x, y, c, d, z):
        self.x, self.y, self.c, self.d, self.z = x, y, c, d, z

    def but(self, **new):
        return At(**{**self.__dict__, **new})

    def chip(self):
        return self.x * 2 + self.y

    def head(self):
        return self.d * 4 + self.z

    def slot(self):
        return self.z * 2 + self.c

    def device(self):
        return ((self.x * 2 + self.y) * 2 + self.c, self.d, self.z)


def here():
    ctx = lax.axis_index("ctx")
    return At(ctx // 4, ctx // 2 % 2, ctx % 2, lax.axis_index("dp"), lax.axis_index("fsdp"))


class Shift:
    def __init__(self, x=0, y=0, c=0, d=0, z=0):
        self.by = (x, y, c, d, z)

    def move(self, at, sign):
        x, y, c, d, z = self.by
        return At(
            (at.x + 4 + sign * x) % 4 if x else at.x,
            1 - at.y if y else at.y,
            1 - at.c if c else at.c,
            1 - at.d if d else at.d,
            (at.z + 4 + sign * z) % 4 if z else at.z,
        )

    def to(self, at):
        return self.move(at, 1)

    def back(self, at):
        return self.move(at, -1)

    def key(self):
        return self.by


class Op:
    def __init__(self, shift, src, dst, cond=None, needs=()):
        self.shift, self.src, self.dst, self.cond, self.needs = shift, src, dst, cond, needs


def exchange(ops, collective_id, out_shapes, *arrays):
    n_in, n_out, n_ops = len(arrays), len(out_shapes), len(ops)

    def kernel(*refs):
        io = refs[: n_in + n_out]
        send_sem, recv_sem = refs[n_in + n_out :]
        me = here()

        def when(cond, act):
            if cond is None:
                act()
            else:
                pl.when(cond)(act)

        barrier = pltpu.get_barrier_semaphore()
        seen, count = set(), 0
        for op in ops:
            if op.shift is None or (op.shift.key(), op.cond) in seen:
                continue
            seen.add((op.shift.key(), op.cond))
            source = op.shift.back(me)

            def greet(source=source):
                pl.semaphore_signal(barrier, inc=1, device_id=source.device(), device_id_type=MESH)

            when(op.cond and op.cond(source), greet)
            count = count + (1 if op.cond is None else jnp.where(op.cond(me), 1, 0))
        pl.semaphore_wait(barrier, count)

        def copy(t, sender):
            op = ops[t]
            if op.shift is None:
                return pltpu.make_async_copy(op.src(io, me), op.dst(io, me), send_sem.at[t])
            return pltpu.make_async_remote_copy(
                src_ref=op.src(io, sender),
                dst_ref=op.dst(io, sender),
                send_sem=send_sem.at[t],
                recv_sem=recv_sem.at[t],
                device_id=op.shift.to(me).device(),
                device_id_type=MESH,
            )

        arrived = set()

        def arrive(t):
            if t in arrived:
                return
            arrived.add(t)
            op = ops[t]
            source = me if op.shift is None else op.shift.back(me)

            def wait():
                if op.shift is None:
                    copy(t, me).wait()
                else:
                    copy(t, source).wait_recv()

            when(op.cond and op.cond(source), wait)

        for t, op in enumerate(ops):
            for need in op.needs:
                arrive(need)
            when(op.cond and op.cond(me), lambda t=t: copy(t, me).start())
        for t, op in enumerate(ops):
            arrive(t)
            if op.shift is not None:
                when(op.cond and op.cond(me), lambda t=t: copy(t, me).wait_send())

    return pl.pallas_call(
        kernel,
        out_shape=tuple(jax.ShapeDtypeStruct(s, d) for s, d in out_shapes),
        in_specs=[pl.BlockSpec(memory_space=pl.ANY)] * n_in,
        out_specs=tuple([pl.BlockSpec(memory_space=pl.ANY)] * n_out),
        scratch_shapes=[
            pltpu.SemaphoreType.DMA((n_ops,)),
            pltpu.SemaphoreType.DMA((n_ops,)),
        ],
        compiler_params=pltpu.CompilerParams(collective_id=collective_id, has_side_effects=True),
        name="exchange_%d" % collective_id,
    )(*arrays)

def home(at):
    return at.c == at.d


def away(at):
    return at.c != at.d


def block(index, start, size):
    return lambda io, at: io[index].at[pl.ds(pl.multiple_of(start(at) * size, size), size)]


def full(index):
    return lambda io, at: io[index]


class Plan(list):
    def add(self, *args, **named):
        self.append(Op(*args, **named))
        return len(self) - 1

    def gather_tokens(self, src, dst, size):
        mine = block(dst, At.slot, size)
        self.add(None, full(src), mine, home)
        got = {}
        for name, by in (("side", {"d": 1}), ("up", {"z": 1}), ("down", {"z": -1})):
            got[name] = [
                self.add(Shift(**by), full(src), mine, home),
                self.add(Shift(c=1, **by), full(src), mine, away),
            ]
        self.add(Shift(c=1), full(src), mine, away)

        def relays():
            both = block(dst, lambda at: at.z, 2 * size)
            below = block(dst, lambda at: (at.z + 3) % 4 * 2, size)
            above = block(dst, lambda at: (at.z + 1) % 4 * 2 + 1, size)
            up = self.add(Shift(z=1), both, both, away, got["side"])
            down = self.add(Shift(z=-1), both, both, away, got["side"])
            self.add(Shift(z=1), below, below, home, got["up"])
            self.add(Shift(z=-1), above, above, home, got["down"])
            self.add(Shift(z=1), below, below, away, [up])
            self.add(Shift(z=-1), above, above, away, [down])

        return relays

    def return_tokens(self, src, dst, size):
        land = block(dst, At.head, size)
        for k in (0, 1, 3, 2):
            for c in (0, 1):
                for d, cond in ((0, home), (1, away)):
                    shift = Shift(z=k, c=c, d=d)
                    if not (k or c or d):
                        self.add(None, block(src, At.slot, size), land, cond)
                    else:
                        self.add(shift, block(src, lambda at, s=shift: s.to(at).slot(), size), land, cond)

    def group_shifts(self):
        return [Shift(d=d, z=z) for z in (1, 3, 0, 2) for d in (0, 1) if d or z]

    def chip_shifts(self):
        return [Shift(x=x, y=y) for x in (1, 3, 2, 0) for y in (0, 1) if x or y]

    def weights(self, src, dst, rows, width, start):
        half = rows // 2

        def cut(at, to):
            return lambda io: io[src].at[
                pl.ds(pl.multiple_of(at.c * half, half), half),
                pl.ds(pl.multiple_of(to.head() * width, width), width),
            ]

        def land(io, at):
            first = pl.multiple_of(at.head() * rows + at.c * half, half)
            return io[dst].at[pl.ds(first, half), pl.ds(start, width)]

        got = []
        for shift in self.group_shifts():
            got.append(
                (shift, self.add(shift, lambda io, at, s=shift: cut(at, s.to(at))(io), land))
            )
        self.add(
            None,
            lambda io, at: io[src].at[:, pl.ds(pl.multiple_of(at.head() * width, width), width)],
            lambda io, at: io[dst].at[pl.ds(pl.multiple_of(at.head() * rows, rows), rows), pl.ds(start, width)],
        )

        def relays():
            for shift, need in got:
                piece = lambda io, at, s=shift: land(io, s.back(at))
                self.add(Shift(c=1), piece, piece, needs=[need])

        return relays

    def gather_group(self, src, dst, size):
        for shift in self.group_shifts():
            self.add(shift, full(src), block(dst, At.head, size))
        self.add(None, full(src), block(dst, At.head, size))

    def gather_context(self, src, dst, size):
        land = block(dst, lambda at: at.chip() * 2 + at.c, size)
        for shift in self.chip_shifts():
            for c in (0, 1):
                self.add(Shift(shift.by[0], shift.by[1], c), full(src), land)
        self.add(Shift(c=1), full(src), land)
        self.add(None, full(src), land)

    def scatter_group(self, src, dst):
        ids = []
        for shift in self.group_shifts():
            ids.append(
                self.add(
                    shift,
                    lambda io, at, s=shift: src(io, s.to(at).head()),
                    lambda io, at: dst(io, at.head()),
                )
            )
        ids.append(
            self.add(None, lambda io, at: src(io, at.head()), lambda io, at: dst(io, at.head()))
        )
        return ids

    def scatter_chips(self, src, dst):
        for shift in self.chip_shifts():
            self.add(
                shift,
                lambda io, at, s=shift: src(io, s.to(at).chip()),
                lambda io, at: dst(io, at.chip()),
            )
        self.add(None, lambda io, at: src(io, at.chip()), lambda io, at: dst(io, at.chip()))

    def gather_chips(self, src, land, whole, needs=()):
        at_own = lambda io, at: land(io, at.chip(), at.c)
        ids = [self.add(None, src, at_own, needs=needs)]
        side = self.add(Shift(y=1), src, at_own, needs=needs)
        ids.append(side)
        for x in (1, 3, 2):
            ids.append(self.add(Shift(x=x), src, at_own, needs=needs))

        def relays():
            other = lambda io, at: land(io, at.but(y=1 - at.y).chip(), at.c)
            for x in (1, 3, 2):
                ids.append(self.add(Shift(x=x), other, other, needs=[side]))

        def share():
            mine = lambda io, at: whole(io, at.c)
            self.add(Shift(c=1), mine, mine, needs=list(ids))

        return relays, share


NT = (((1,), (1,)), ((), ()))
NN = (((1,), (0,)), ((), ()))


def mm(a, b, dims=NN):
    return lax.dot_general(a, b, dims, preferred_element_type=F32)


def stacked(ref):
    return jnp.concatenate([ref[:, :HEAD], ref[:, HEAD:]], axis=0)


def forward_kernel(order, own, q_ref, kv_ref, o_ref, l_ref, keys, vals, acc):
    step = pl.program_id(0)
    n_runs = order.shape[0]

    @pl.when(step == 0)
    def _():
        def place(r, _):
            src = pl.ds(pl.multiple_of(r // 8 * KV_ROWS + r % 8 * RUN, 16), RUN)
            dst = pl.ds(pl.multiple_of(order[r] * RUN, RUN), RUN)
            keys[dst, :] = kv_ref[src, :HEAD]
            vals[dst, :HEAD] = kv_ref[src, HEAD:]
            vals[dst, HEAD:] = jnp.ones((RUN, HEAD), BF)
            return 0

        lax.fori_loop(0, n_runs, place, 0)

    run = own[step]
    query = stacked(q_ref)
    acc[...] = jnp.zeros_like(acc)

    def visit(j, masked):
        at = pl.ds(pl.multiple_of(j * CHUNK, CHUNK), CHUNK)
        s = mm(query, keys[at, :], NT)
        p = jnp.exp2(s * (SCALE * LOG2E))
        if masked:
            row = lax.broadcasted_iota(jnp.int32, p.shape, 0) % RUN + run * RUN
            col = lax.broadcasted_iota(jnp.int32, p.shape, 1) + j * CHUNK
            p = jnp.where(col <= row, p, 0.0)
        acc[...] += mm(p.astype(BF), vals[at, :])

    last = run // (CHUNK // RUN)

    def plain(j, _):
        visit(j, False)
        return 0

    lax.fori_loop(0, last, plain, 0)
    visit(last, True)
    total = acc[:, HEAD:]
    out = acc[:, :HEAD] / total
    log = jnp.log2(total)
    o_ref[:, :HEAD] = out[:RUN]
    o_ref[:, HEAD:] = out[RUN:]
    l_ref[:, :HEAD] = log[:RUN]
    l_ref[:, HEAD:] = log[RUN:]


def attention_forward(order, own, q, kv):
    length = order.shape[0] * RUN
    tokens = q.shape[0]
    block = pl.BlockSpec((RUN, 2 * HEAD), lambda i, *_: (i, 0))
    return pl.pallas_call(
        forward_kernel,
        grid_spec=pltpu.PrefetchScalarGridSpec(
            num_scalar_prefetch=2,
            grid=(tokens // RUN,),
            in_specs=[block, pl.BlockSpec(kv.shape, lambda i, *_: (0, 0))],
            out_specs=[block, block],
            scratch_shapes=[
                pltpu.VMEM((length, HEAD), BF),
                pltpu.VMEM((length, 2 * HEAD), BF),
                pltpu.VMEM((2 * RUN, 2 * HEAD), F32),
            ],
        ),
        out_shape=(jax.ShapeDtypeStruct(q.shape, F32), jax.ShapeDtypeStruct(q.shape, F32)),
        compiler_params=pltpu.CompilerParams(
            dimension_semantics=("arbitrary",), vmem_limit_bytes=48 * 2**20
        ),
        name="attention_forward",
    )(order, own, q, kv)


def backward_kernel(
    order, own, q_ref, g_ref, o_ref, l_ref, kv_ref, dq_ref, dkv_ref,
    keys, keys_t, vals, dk, dv, dq_t, q_t, g_t,
):
    step = pl.program_id(0)
    n_runs = order.shape[0]

    @pl.when(step == 0)
    def _():
        dk[...] = jnp.zeros_like(dk)
        dv[...] = jnp.zeros_like(dv)

        def place(r, _):
            src = pl.ds(pl.multiple_of(r // 8 * KV_ROWS + r % 8 * RUN, 16), RUN)
            dst = pl.ds(pl.multiple_of(order[r] * RUN, RUN), RUN)
            k = kv_ref[src, :HEAD]
            keys[dst, :] = k
            keys_t[:, dst] = k.T
            vals[dst, :] = kv_ref[src, HEAD:]
            return 0

        lax.fori_loop(0, n_runs, place, 0)

    run = own[step]
    query = stacked(q_ref)
    grad = stacked(g_ref)
    q_t[...] = query.T
    g_t[...] = grad.T
    delta = jnp.sum((grad.astype(F32) * stacked(o_ref)).T, axis=0, keepdims=True)
    log = stacked(l_ref).T[:1]
    dq_t[...] = jnp.zeros_like(dq_t)

    def visit(j, masked):
        at = pl.ds(pl.multiple_of(j * CHUNK, CHUNK), CHUNK)
        s = mm(keys[at, :], q_t[...])
        p = jnp.exp2(s * (SCALE * LOG2E) - log)
        if masked:
            row = lax.broadcasted_iota(jnp.int32, p.shape, 1) % RUN + run * RUN
            col = lax.broadcasted_iota(jnp.int32, p.shape, 0) + j * CHUNK
            p = jnp.where(col <= row, p, 0.0)
        dp = mm(vals[at, :], g_t[...])
        ds = (p * (dp - delta)).astype(BF)
        dv[at, :] += mm(p.astype(BF), grad)
        dk[at, :] += mm(ds, query)
        dq_t[...] += mm(keys_t[:, at], ds)

    last = run // (CHUNK // RUN)

    def plain(j, _):
        visit(j, False)
        return 0

    lax.fori_loop(0, last, plain, 0)
    visit(last, True)
    out = dq_t[...].T * SCALE
    dq_ref[:, :HEAD] = out[:RUN]
    dq_ref[:, HEAD:] = out[RUN:]

    @pl.when(step == pl.num_programs(0) - 1)
    def _():
        def give(r, _):
            dst = pl.ds(pl.multiple_of(r * RUN, RUN), RUN)
            src = pl.ds(pl.multiple_of(order[r] * RUN, RUN), RUN)
            dkv_ref[dst, :HEAD] = (dk[src, :] * SCALE).astype(BF)
            dkv_ref[dst, HEAD:] = dv[src, :].astype(BF)
            return 0

        lax.fori_loop(0, n_runs, give, 0)


def attention_backward(order, own, q, g, o, log, kv):
    length = order.shape[0] * RUN
    tokens = q.shape[0]
    block = pl.BlockSpec((RUN, 2 * HEAD), lambda i, *_: (i, 0))
    all_rows = pl.BlockSpec((length, 2 * HEAD), lambda i, *_: (0, 0))
    return pl.pallas_call(
        backward_kernel,
        grid_spec=pltpu.PrefetchScalarGridSpec(
            num_scalar_prefetch=2,
            grid=(tokens // RUN,),
            in_specs=[block, block, block, block, pl.BlockSpec(kv.shape, lambda i, *_: (0, 0))],
            out_specs=[block, all_rows],
            scratch_shapes=[
                pltpu.VMEM((length, HEAD), BF),
                pltpu.VMEM((HEAD, length), BF),
                pltpu.VMEM((length, HEAD), BF),
                pltpu.VMEM((length, HEAD), F32),
                pltpu.VMEM((length, HEAD), F32),
                pltpu.VMEM((HEAD, 2 * RUN), F32),
                pltpu.VMEM((HEAD, 2 * RUN), BF),
                pltpu.VMEM((HEAD, 2 * RUN), BF),
            ],
        ),
        out_shape=(jax.ShapeDtypeStruct(q.shape, F32), jax.ShapeDtypeStruct((length, 2 * HEAD), BF)),
        compiler_params=pltpu.CompilerParams(
            dimension_semantics=("arbitrary",), vmem_limit_bytes=48 * 2**20
        ),
        name="attention_backward",
    )(order, own, q, g, o, log, kv)


def rotate(value, cos, sin):
    a, b = value[..., : HEAD // 2], value[..., HEAD // 2 :]
    return jnp.concatenate([a * cos - b * sin, b * cos + a * sin], axis=-1)


def rotate_back(grad, cos, sin):
    a, b = grad[..., : HEAD // 2], grad[..., HEAD // 2 :]
    return jnp.concatenate([a * cos + b * sin, b * cos - a * sin], axis=-1)


def inverse_rms(value):
    return lax.rsqrt(jnp.mean(value * value, axis=-1, keepdims=True) + EPS)


def norm_back(value, inverse, gain, grad):
    scaled = grad * gain
    inner = jnp.sum(scaled * value, axis=-1, keepdims=True)
    return inverse * scaled - value * inverse * inverse * inverse * inner / value.shape[-1]


def dot(a, b):
    return jnp.dot(a, b, preferred_element_type=F32)


def dot_t(a, b):
    return lax.dot_general(a, b, (((0,), (0,)), ((), ())), preferred_element_type=F32)


def summed(parts, count):
    return jnp.sum(parts.reshape((count, -1) + parts.shape[1:]).astype(F32), axis=0)


def row_of(vector):
    return jnp.pad(vector.reshape(1, -1), ((0, 0), (0, 128 - vector.shape[-1])))


def local(
    hidden_in, positions, attn_gain, query_weight, key_matrix, value_matrix, output_weight,
    query_norm_gain, key_gain, mlp_gain, gate_weight, up_weight, down_weight, cotangent,
):
    hidden = hidden_in[0]
    cot = cotangent[0]
    tokens, width = hidden.shape
    group = 8 * tokens
    ff = gate_weight.shape[1] // 8
    part = width // 8
    core = lax.axis_index("ctx") % 2
    def rows(size):
        return lambda ref: (lambda io, n: io[ref].at[pl.ds(pl.multiple_of(n * size, size), size)])

    gain_tile = jnp.concatenate(
        [row_of(g.astype(F32)) for g in (attn_gain, mlp_gain, query_norm_gain, key_gain)]
        + [jnp.zeros((4, 128), F32)],
        axis=0,
    )
    own_run = (positions[:, :1] // RUN).astype(BF)
    tagged = jnp.concatenate([hidden, jnp.broadcast_to(own_run, (TAG, width))], axis=0)
    plan = Plan()
    relays = [plan.gather_tokens(0, 5, X_ROWS)]
    plan.gather_group(1, 6, 8)
    relays += [
        plan.weights(2, 7, part, 256, 0),
        plan.weights(3, 7, part, 128, 256),
        plan.weights(4, 7, part, 128, 384),
    ]
    for relay in relays:
        relay()
    x_all, gains, w_qkv = exchange(
        plan, 1, (((8 * X_ROWS, width), BF), ((64, 128), F32), ((width, 512), BF)),
        tagged, gain_tile, query_weight, key_matrix, value_matrix,
    )
    gains = gains.reshape(8, 8, 128)
    attn_scale = gains[:, 0].reshape(1, width)
    mlp_scale = gains[:, 1].reshape(1, width)
    query_scale = gains[:, 2, :16].reshape(1, HEAD)
    key_scale = gains[:, 3, :16].reshape(1, HEAD)
    x_all = x_all.reshape(8, X_ROWS, width)
    own_bf = x_all[:, RUN, 0]
    own = own_bf.astype(jnp.int32)
    x_wide = x_all[:, :RUN].reshape(group, width).astype(F32)
    attn_inverse_all = inverse_rms(x_wide)
    norm_one = (x_wide * attn_inverse_all * attn_scale).astype(BF)
    qkv = dot(norm_one, w_qkv)
    pre = qkv[:, :384].reshape(group, 3, HEAD)
    head_scale = jnp.stack([query_scale, query_scale, key_scale], axis=1)
    head_inverse = inverse_rms(pre)
    place_rows = (own[:, None] * RUN + jnp.arange(RUN, dtype=jnp.int32)[None, :]).reshape(group)
    frequency = 1.0 / THETA ** (jnp.arange(0, HEAD, 2, dtype=F32) / HEAD)
    angle = place_rows.astype(F32)[:, None] * frequency[None, :]
    cos, sin = jnp.cos(angle)[:, None, :], jnp.sin(angle)[:, None, :]
    turned = rotate(pre * head_inverse * head_scale, cos, sin).astype(BF).reshape(group, 384)
    queries = turned[:, :256]
    kv = jnp.concatenate([turned[:, 256:], qkv[:, 384:].astype(BF)], axis=1)
    tag = jnp.pad(jnp.broadcast_to(own_bf[None, :], (TAG, 8)), ((0, 0), (0, 2 * HEAD - 8)))
    kv = jnp.concatenate([kv, tag], axis=0)

    plan = Plan()
    own_kv = block(4, At.chip, KV_ROWS)
    side_kv = block(4, lambda at: at.but(y=1 - at.y).chip(), KV_ROWS)
    half = group // 2

    def upper(io, at):
        return io[4].at[pl.ds(pl.multiple_of(at.chip() * KV_ROWS, 16), half)]

    def lower(io, at):
        return io[4].at[pl.ds(pl.multiple_of(at.chip() * KV_ROWS + half, 16), KV_ROWS - half)]

    def left(of, flip):
        return lambda io, at: of(io, at.but(x=(at.x + 3) % 4, y=1 - at.y if flip else at.y))

    def right(of, flip):
        return lambda io, at: of(io, at.but(x=(at.x + 1) % 4, y=1 - at.y if flip else at.y))

    side = plan.add(Shift(y=1), full(0), own_kv)
    right_id = plan.add(Shift(x=1), full(0), own_kv)
    left_id = plan.add(Shift(x=-1), full(0), own_kv)
    plan.add(None, full(0), own_kv)
    relays = [
        plan.gather_tokens(1, 5, tokens),
        plan.weights(2, 6, part, ff, 0),
        plan.weights(3, 6, part, ff, ff),
    ]
    side_right = plan.add(Shift(x=1), side_kv, side_kv, needs=[side])
    side_left = plan.add(Shift(x=-1), side_kv, side_kv, needs=[side])
    plan.add(Shift(x=1), left(upper, 0), left(upper, 0), needs=[right_id])
    plan.add(Shift(x=-1), right(lower, 0), right(lower, 0), needs=[left_id])
    for relay in relays:
        relay()
    plan.add(Shift(x=1), left(upper, 1), left(upper, 1), needs=[side_right])
    plan.add(Shift(x=-1), right(lower, 1), right(lower, 1), needs=[side_left])
    kv_all, cot_all, w_gu = exchange(
        plan, 2, (((8 * KV_ROWS, 256), BF), ((group, width), BF), ((width, 2 * ff), BF)),
        kv, cot, gate_weight, up_weight,
    )
    order = kv_all.reshape(8, KV_ROWS, 256)[:, 8 * RUN, :8].reshape(64).astype(jnp.int32)
    attention, log_total = attention_forward(order, own, queries, kv_all)
    mixed = attention.astype(BF)
    branch_part = dot(mixed, output_weight).astype(BF)

    plan = Plan()
    plan.return_tokens(0, 1, tokens)
    (branch,) = exchange(plan, 3, (((group, width), BF),), branch_part)
    residual = hidden.astype(F32)
    middle = residual + summed(branch, 8)
    mlp_inverse = inverse_rms(middle)
    norm_two_own = (middle * mlp_inverse * mlp_scale).astype(BF)
    plan = Plan()
    plan.gather_tokens(0, 1, tokens)()
    (norm_two,) = exchange(plan, 4, (((group, width), BF),), norm_two_own)

    gate_up = dot(norm_two, w_gu)
    gate, up = gate_up[:, :ff], gate_up[:, ff:]
    sigma = jax.nn.sigmoid(gate)
    swish = gate * sigma
    inner = (swish * up).astype(BF)
    inner_grad = lax.dot_general(cot_all, down_weight, NT, preferred_element_type=F32)
    gate_up_grad = jnp.concatenate(
        [
            (inner_grad * up * sigma * (1.0 + gate * (1.0 - sigma))).astype(BF),
            (inner_grad * swish).astype(BF),
        ],
        axis=1,
    )
    norm_two_part = lax.dot_general(gate_up_grad, w_gu, NT, preferred_element_type=F32).astype(BF)
    gate_up_wgrad = dot_t(norm_two, gate_up_grad).astype(BF).reshape(8, part, 2 * ff)
    down_wgrad = dot_t(inner, cot_all).astype(BF)

    def theirs(ref, size):
        def pick(io, at):
            cut = pl.ds(pl.multiple_of((1 - at.c) * size, size), size)
            return io[ref].at[..., cut]

        return pick

    def my_half(both, got):
        size = got.shape[-1]
        mine = lax.dynamic_slice_in_dim(both, core * size, size, axis=both.ndim - 1)
        return (mine.astype(F32) + got.astype(F32)).astype(BF)

    plan = Plan()
    plan.return_tokens(0, 3, tokens)
    plan.add(Shift(c=1), theirs(1, ff), full(4))
    plan.add(Shift(c=1), theirs(2, width // 2), full(5))
    norm_two_parts, gate_up_got, down_got = exchange(
        plan, 5, (((group, width), BF), ((8, part, ff), BF), ((ff, width // 2), BF)),
        norm_two_part, gate_up_wgrad, down_wgrad,
    )
    norm_two_grad = summed(norm_two_parts, 8)
    middle_grad = cot.astype(F32) + norm_back(middle, mlp_inverse, mlp_scale, norm_two_grad)
    mlp_gain_part = jnp.sum(norm_two_grad * middle * mlp_inverse, axis=0)
    branch_grad_own = middle_grad.astype(BF)
    gate_up_half = my_half(gate_up_wgrad, gate_up_got)
    down_half = my_half(down_wgrad, down_got)

    plan = Plan()
    relay = plan.gather_tokens(0, 3, tokens)
    plan.scatter_chips(
        lambda io, n: io[1].at[:, pl.ds(pl.multiple_of(n * 16, 16), 16)], lambda io, n: io[4].at[n]
    )
    plan.scatter_chips(rows(ff // 8)(2), lambda io, n: io[5].at[n])
    relay()
    branch_grad, gate_up_pieces, down_pieces = exchange(
        plan, 6, (((group, width), BF), ((8, 8, 16, ff), BF), ((8, ff // 8, width // 2), BF)),
        branch_grad_own, gate_up_half, down_half,
    )
    mixed_grad = lax.dot_general(branch_grad, output_weight, NT, preferred_element_type=F32).astype(BF)
    output_wgrad = dot_t(mixed, branch_grad).astype(BF)
    down_part = dot(inner, down_weight).astype(BF)
    gate_up_sum = jnp.sum(gate_up_pieces.astype(F32), axis=0).astype(BF)
    down_sum = jnp.sum(down_pieces.astype(F32), axis=0).astype(BF)
    query_turn, kv_part = attention_backward(
        order, own, queries, mixed_grad, attention, log_total, kv_all
    )

    plan = Plan()
    plan.scatter_chips(rows(group)(0), rows(group)(4))
    pair = 2 * tokens
    for k in (1, 3, 2):
        plan.add(
            Shift(z=k),
            block(1, lambda at, k=k: (at.z + k) % 4, pair),
            block(5, lambda at: at.z, pair),
        )
    plan.add(None, block(1, lambda at: at.z, pair), block(5, lambda at: at.z, pair))
    plan.add(Shift(c=1), theirs(2, width // 2), full(6))
    plan.scatter_group(
        lambda io, n: io[3].at[n],
        lambda io, n: io[7].at[:, pl.ds(pl.multiple_of(n * ff, ff), ff)],
    )
    n_rows = output_wgrad.shape[0]
    kv_parts, down_parts, output_got, gate_up_own = exchange(
        plan, 7,
        (
            ((8 * group, 256), BF), ((group, width), BF), ((n_rows, width // 2), BF),
            ((16, 8 * ff), BF),
        ),
        kv_part, down_part, output_wgrad, gate_up_sum,
    )
    down_pair = summed(down_parts, 4).astype(BF)
    output_half = my_half(output_wgrad, output_got)
    kv_sum = summed(kv_parts, 8)
    turn = jnp.concatenate([query_turn, kv_sum[:, :HEAD]], axis=1).reshape(group, 3, HEAD)
    head_grad = rotate_back(turn, cos, sin)
    pre_grad = norm_back(pre, head_inverse, head_scale, head_grad)
    head_gain_parts = jnp.sum(head_grad * pre * head_inverse, axis=0)
    qkv_grad = jnp.concatenate(
        [pre_grad.reshape(group, 384).astype(BF), kv_sum[:, HEAD:].astype(BF)], axis=1
    )
    qkv_wgrad = dot_t(norm_one, qkv_grad).astype(BF).reshape(8, part, 512)
    norm_one_wide = lax.dot_general(qkv_grad, w_qkv, NT, preferred_element_type=F32)
    attn_gain_part = jnp.sum(norm_one_wide * x_wide * attn_inverse_all, axis=0)
    query_gain_part = (head_gain_parts[0] + head_gain_parts[1]).reshape(8, 1, 16)
    key_gain_part = head_gain_parts[2].reshape(8, 1, 16)
    gain_parts = jnp.concatenate(
        [
            attn_gain_part.reshape(8, 1, 128),
            mlp_gain_part.reshape(8, 1, 128),
            jnp.pad(query_gain_part, ((0, 0), (0, 0), (0, 112))),
            jnp.pad(key_gain_part, ((0, 0), (0, 0), (0, 112))),
            jnp.zeros((8, 4, 128), F32),
        ],
        axis=1,
    ).reshape(64, 128)

    plan = Plan()
    plan.return_tokens(0, 6, tokens)

    def wgrad_piece(io, chip, c):
        return io[1].at[
            :, pl.ds(pl.multiple_of(chip * 16, 16), 16), pl.ds(pl.multiple_of(c * 256, 256), 256)
        ]

    for shift in [Shift(c=1)] + [
        Shift(s.by[0], s.by[1], c) for s in plan.chip_shifts() for c in (0, 1)
    ]:
        plan.add(
            shift,
            lambda io, at, s=shift: wgrad_piece(io, s.to(at).chip(), s.to(at).c),
            lambda io, at: io[7].at[at.chip() * 2 + at.c],
        )
    plan.add(
        None,
        lambda io, at: wgrad_piece(io, at.chip(), at.c),
        lambda io, at: io[7].at[at.chip() * 2 + at.c],
    )
    plan.scatter_chips(rows(n_rows // 8)(2), lambda io, n: io[8].at[n])
    plan.scatter_group(rows(8)(3), rows(8)(9))

    def stacked_rows(ref, size, total):
        def land(io, chip, c):
            return io[ref].at[pl.ds(pl.multiple_of(c * total + chip * size, size), size)]

        return land, lambda io, c: io[ref].at[pl.ds(pl.multiple_of(c * total, total), total)]

    def side_columns(ref, size):
        def at_core(c):
            return pl.ds(pl.multiple_of(c * (width // 2), width // 2), width // 2)

        def land(io, chip, c):
            return io[ref].at[pl.ds(pl.multiple_of(chip * size, size), size), at_core(c)]

        return land, lambda io, c: io[ref].at[:, at_core(c)]

    later = [
        plan.gather_chips(full(4), *stacked_rows(10, 16, part)),
        plan.gather_chips(full(5), *side_columns(11, ff // 8)),
    ]
    for relay, _ in later:
        relay()
    for _, share in later:
        share()
    norm_one_parts, qkv_pieces, output_pieces, gain_sums, gate_up_final, down_final = exchange(
        plan, 8,
        (
            ((group, width), BF), ((16, 8, 16, 256), BF), ((8, n_rows // 8, width // 2), BF),
            ((64, 128), F32), ((2 * part, 8 * ff), BF), ((ff, width), BF),
        ),
        norm_one_wide.astype(BF), qkv_wgrad, output_half, gain_parts, gate_up_own, down_sum,
    )
    qkv_sum = jnp.sum(qkv_pieces.astype(F32), axis=0).astype(BF)
    output_sum = jnp.sum(output_pieces.astype(F32), axis=0).astype(BF)
    gain_sum = summed(gain_sums, 8)

    plan = Plan()
    to_group = plan.scatter_group(
        lambda io, n: io[0].at[n],
        lambda io, n: io[4].at[:, pl.ds(pl.multiple_of(n * 256, 256), 256)],
    )
    relay_output, share_output = plan.gather_chips(full(1), *side_columns(6, n_rows // 8))
    plan.gather_context(2, 7, 8)
    own_block = block(3, lambda at: at.c, tokens)
    other_block = block(3, lambda at: 1 - at.c, tokens)

    def landed(n):
        return lambda io, at: io[8].at[pl.ds(n * tokens, tokens)]

    plan.add(Shift(d=1), own_block, landed(1), away)
    plan.add(Shift(d=1, c=1), other_block, landed(1), away)
    plan.add(None, own_block, landed(0), home)
    plan.add(Shift(c=1), other_block, landed(0), home)
    relay_qkv, share_qkv = plan.gather_chips(full(4), *stacked_rows(5, 16, part), needs=to_group)
    relay_output()
    relay_qkv()
    share_output()
    share_qkv()
    _, qkv_final, output_final, gain_all, down_last = exchange(
        plan, 9,
        (
            ((16, 2048), BF), ((2 * part, 2048), BF), ((n_rows, width), BF), ((128, 128), F32),
            ((2 * tokens, width), BF),
        ),
        qkv_sum, output_sum, gain_sum, down_pair,
    )
    layer_out = (middle + summed(down_last, 2)).astype(BF)
    attn_inverse = inverse_rms(residual)
    input_grad = middle_grad + norm_back(residual, attn_inverse, attn_scale, summed(norm_one_parts, 8))
    gain_total = summed(gain_all, 16)
    key_value = qkv_final[part:].astype(F32).reshape(part, 8, 2, HEAD)
    return (
        layer_out[None],
        input_grad[None],
        gain_total[0],
        qkv_final[:part].astype(F32),
        key_value[:, :, 0].reshape(part, width),
        key_value[:, :, 1].reshape(part, width),
        output_final.astype(F32),
        gain_total[2, :16],
        gain_total[3, :16],
        gain_total[1],
        gate_up_final[:part].astype(F32),
        gate_up_final[part:].astype(F32),
        down_final.astype(F32),
    )


def solution(mesh):
    tokens = P("dp", ("ctx", "fsdp"), None)
    places = P("dp", ("ctx", "fsdp"))
    vector = P(("dp", "fsdp"))
    matrix = P(("dp", "fsdp"), None)
    in_specs = (
        tokens, places, vector, matrix, matrix, matrix, matrix,
        vector, vector, vector, matrix, matrix, matrix, tokens,
    )
    out_specs = (
        tokens, tokens, vector, matrix, matrix, matrix, matrix,
        vector, vector, vector, matrix, matrix, matrix,
    )
    return jax.shard_map(local, mesh=mesh, in_specs=in_specs, out_specs=out_specs, check_vma=False)
```

```python
import jax
import jax.numpy as jnp
from jax import lax
from jax.experimental import pallas as pl
from jax.experimental.pallas import tpu as pltpu
from jax.sharding import PartitionSpec as P

HEAD = 128
EPS = 1e-06
THETA = 1000000.0
SCALE = HEAD ** (-0.5)
LOG2E = 1.4426950408889634
RUN = 128
CHUNK = 512
VMEM = 60 * 2**20
UNROLL = 4
TAG = 16
X_ROWS = RUN + TAG
KV_ROWS = 8 * RUN + TAG
BF = jnp.bfloat16
F32 = jnp.float32
MESH = pl.DeviceIdType.MESH


class At:
    def __init__(self, x, y, c, d, z):
        self.x, self.y, self.c, self.d, self.z = x, y, c, d, z

    def but(self, **new):
        return At(**{**self.__dict__, **new})

    def chip(self):
        return self.x * 2 + self.y

    def head(self):
        return self.d * 4 + self.z

    def slot(self):
        return self.z * 2 + self.c

    def device(self):
        return ((self.x * 2 + self.y) * 2 + self.c, self.d, self.z)


def here():
    ctx = lax.axis_index("ctx")
    return At(ctx // 4, ctx // 2 % 2, ctx % 2, lax.axis_index("dp"), lax.axis_index("fsdp"))


class Shift:
    def __init__(self, x=0, y=0, c=0, d=0, z=0):
        self.by = (x, y, c, d, z)

    def move(self, at, sign):
        x, y, c, d, z = self.by
        return At(
            (at.x + 4 + sign * x) % 4 if x else at.x,
            1 - at.y if y else at.y,
            1 - at.c if c else at.c,
            1 - at.d if d else at.d,
            (at.z + 4 + sign * z) % 4 if z else at.z,
        )

    def to(self, at):
        return self.move(at, 1)

    def back(self, at):
        return self.move(at, -1)

    def key(self):
        return self.by


class Op:
    def __init__(self, shift, src, dst, cond=None, needs=()):
        self.shift, self.src, self.dst, self.cond, self.needs = shift, src, dst, cond, needs


def exchange(ops, collective_id, out_shapes, *arrays):
    n_in, n_out, n_ops = len(arrays), len(out_shapes), len(ops)

    def kernel(*refs):
        io = refs[: n_in + n_out]
        send_sem, recv_sem = refs[n_in + n_out :]
        me = here()

        def when(cond, act):
            if cond is None:
                act()
            else:
                pl.when(cond)(act)

        barrier = pltpu.get_barrier_semaphore()
        seen, count = set(), 0
        for op in ops:
            if op.shift is None or (op.shift.key(), op.cond) in seen:
                continue
            seen.add((op.shift.key(), op.cond))
            source = op.shift.back(me)

            def greet(source=source):
                pl.semaphore_signal(barrier, inc=1, device_id=source.device(), device_id_type=MESH)

            when(op.cond and op.cond(source), greet)
            count = count + (1 if op.cond is None else jnp.where(op.cond(me), 1, 0))
        pl.semaphore_wait(barrier, count)

        def copy(t, sender):
            op = ops[t]
            if op.shift is None:
                return pltpu.make_async_copy(op.src(io, me), op.dst(io, me), send_sem.at[t])
            return pltpu.make_async_remote_copy(
                src_ref=op.src(io, sender),
                dst_ref=op.dst(io, sender),
                send_sem=send_sem.at[t],
                recv_sem=recv_sem.at[t],
                device_id=op.shift.to(me).device(),
                device_id_type=MESH,
            )

        arrived = set()

        def arrive(t):
            if t in arrived:
                return
            arrived.add(t)
            op = ops[t]
            source = me if op.shift is None else op.shift.back(me)

            def wait():
                if op.shift is None:
                    copy(t, me).wait()
                else:
                    copy(t, source).wait_recv()

            when(op.cond and op.cond(source), wait)

        for t, op in enumerate(ops):
            for need in op.needs:
                arrive(need)
            when(op.cond and op.cond(me), lambda t=t: copy(t, me).start())
        for t, op in enumerate(ops):
            arrive(t)
            if op.shift is not None:
                when(op.cond and op.cond(me), lambda t=t: copy(t, me).wait_send())

    return pl.pallas_call(
        kernel,
        out_shape=tuple(jax.ShapeDtypeStruct(s, d) for s, d in out_shapes),
        in_specs=[pl.BlockSpec(memory_space=pl.ANY)] * n_in,
        out_specs=tuple([pl.BlockSpec(memory_space=pl.ANY)] * n_out),
        scratch_shapes=[
            pltpu.SemaphoreType.DMA((n_ops,)),
            pltpu.SemaphoreType.DMA((n_ops,)),
        ],
        compiler_params=pltpu.CompilerParams(collective_id=collective_id, has_side_effects=True),
        name="exchange_%d" % collective_id,
    )(*arrays)

def home(at):
    return at.c == at.d


def away(at):
    return at.c != at.d


def block(index, start, size):
    return lambda io, at: io[index].at[pl.ds(pl.multiple_of(start(at) * size, size), size)]


def full(index):
    return lambda io, at: io[index]


class Plan(list):
    def add(self, *args, **named):
        self.append(Op(*args, **named))
        return len(self) - 1

    def gather_tokens(self, src, dst, size):
        mine = block(dst, At.slot, size)
        self.add(None, full(src), mine, home)
        got = {}
        for name, by in (("side", {"d": 1}), ("up", {"z": 1}), ("down", {"z": -1})):
            got[name] = [
                self.add(Shift(**by), full(src), mine, home),
                self.add(Shift(c=1, **by), full(src), mine, away),
            ]
        self.add(Shift(c=1), full(src), mine, away)

        def relays():
            both = block(dst, lambda at: at.z, 2 * size)
            below = block(dst, lambda at: (at.z + 3) % 4 * 2, size)
            above = block(dst, lambda at: (at.z + 1) % 4 * 2 + 1, size)
            up = self.add(Shift(z=1), both, both, away, got["side"])
            down = self.add(Shift(z=-1), both, both, away, got["side"])
            self.add(Shift(z=1), below, below, home, got["up"])
            self.add(Shift(z=-1), above, above, home, got["down"])
            self.add(Shift(z=1), below, below, away, [up])
            self.add(Shift(z=-1), above, above, away, [down])

        return relays

    def return_tokens(self, src, dst, size):
        land = block(dst, At.head, size)
        for k in (0, 1, 3, 2):
            for c in (0, 1):
                for d, cond in ((0, home), (1, away)):
                    shift = Shift(z=k, c=c, d=d)
                    if not (k or c or d):
                        self.add(None, block(src, At.slot, size), land, cond)
                    else:
                        self.add(shift, block(src, lambda at, s=shift: s.to(at).slot(), size), land, cond)

    def group_shifts(self):
        return [Shift(d=d, z=z) for z in (1, 3, 0, 2) for d in (0, 1) if d or z]

    def chip_shifts(self):
        return [Shift(x=x, y=y) for x in (1, 3, 2, 0) for y in (0, 1) if x or y]

    def weights(self, src, dst, rows, width, start):
        half = rows // 2

        def cut(at, to):
            return lambda io: io[src].at[
                pl.ds(pl.multiple_of(at.c * half, half), half),
                pl.ds(pl.multiple_of(to.head() * width, width), width),
            ]

        def land(io, at):
            first = pl.multiple_of(at.head() * rows + at.c * half, half)
            return io[dst].at[pl.ds(first, half), pl.ds(start, width)]

        got = []
        for shift in self.group_shifts():
            got.append(
                (shift, self.add(shift, lambda io, at, s=shift: cut(at, s.to(at))(io), land))
            )
        self.add(
            None,
            lambda io, at: io[src].at[:, pl.ds(pl.multiple_of(at.head() * width, width), width)],
            lambda io, at: io[dst].at[pl.ds(pl.multiple_of(at.head() * rows, rows), rows), pl.ds(start, width)],
        )

        def relays():
            for shift, need in got:
                piece = lambda io, at, s=shift: land(io, s.back(at))
                self.add(Shift(c=1), piece, piece, needs=[need])

        return relays

    def gather_group(self, src, dst, size):
        for shift in self.group_shifts():
            self.add(shift, full(src), block(dst, At.head, size))
        self.add(None, full(src), block(dst, At.head, size))

    def gather_context(self, src, dst, size):
        land = block(dst, lambda at: at.chip() * 2 + at.c, size)
        for shift in self.chip_shifts():
            for c in (0, 1):
                self.add(Shift(shift.by[0], shift.by[1], c), full(src), land)
        self.add(Shift(c=1), full(src), land)
        self.add(None, full(src), land)

    def scatter_group(self, src, dst):
        ids = []
        for shift in self.group_shifts():
            ids.append(
                self.add(
                    shift,
                    lambda io, at, s=shift: src(io, s.to(at).head()),
                    lambda io, at: dst(io, at.head()),
                )
            )
        ids.append(
            self.add(None, lambda io, at: src(io, at.head()), lambda io, at: dst(io, at.head()))
        )
        return ids

    def scatter_chips(self, src, dst):
        for shift in self.chip_shifts():
            self.add(
                shift,
                lambda io, at, s=shift: src(io, s.to(at).chip()),
                lambda io, at: dst(io, at.chip()),
            )
        self.add(None, lambda io, at: src(io, at.chip()), lambda io, at: dst(io, at.chip()))

    def gather_chips(self, src, land, whole, needs=()):
        at_own = lambda io, at: land(io, at.chip(), at.c)
        ids = [self.add(None, src, at_own, needs=needs)]
        side = self.add(Shift(y=1), src, at_own, needs=needs)
        ids.append(side)
        for x in (1, 3, 2):
            ids.append(self.add(Shift(x=x), src, at_own, needs=needs))

        def relays():
            other = lambda io, at: land(io, at.but(y=1 - at.y).chip(), at.c)
            for x in (1, 3, 2):
                ids.append(self.add(Shift(x=x), other, other, needs=[side]))

        def share():
            mine = lambda io, at: whole(io, at.c)
            self.add(Shift(c=1), mine, mine, needs=list(ids))

        return relays, share


NT = (((1,), (1,)), ((), ()))
NN = (((1,), (0,)), ((), ()))


def mm(a, b, dims=NN):
    return lax.dot_general(a, b, dims, preferred_element_type=F32)


def stacked(ref):
    return jnp.concatenate([ref[:, :HEAD], ref[:, HEAD:]], axis=0)


def forward_kernel(order, own, q_ref, kv_ref, o_ref, l_ref, keys, vals, acc):
    step = pl.program_id(0)
    n_runs = order.shape[0]

    @pl.when(step == 0)
    def _():
        def place(r, _):
            src = pl.ds(pl.multiple_of(r // 8 * KV_ROWS + r % 8 * RUN, 16), RUN)
            dst = pl.ds(pl.multiple_of(order[r] * RUN, RUN), RUN)
            keys[dst, :] = kv_ref[src, :HEAD]
            vals[dst, :HEAD] = kv_ref[src, HEAD:]
            vals[dst, HEAD:] = jnp.ones((RUN, HEAD), BF)
            return 0

        lax.fori_loop(0, n_runs, place, 0, unroll=8)

    run = own[step]
    query = stacked(q_ref)
    acc[...] = jnp.zeros_like(acc)

    def visit(j, masked):
        at = pl.ds(pl.multiple_of(j * CHUNK, CHUNK), CHUNK)
        s = mm(query, keys[at, :], NT)
        p = jnp.exp2(s * (SCALE * LOG2E))
        if masked:
            row = lax.broadcasted_iota(jnp.int32, p.shape, 0) % RUN + run * RUN
            col = lax.broadcasted_iota(jnp.int32, p.shape, 1) + j * CHUNK
            p = jnp.where(col <= row, p, 0.0)
        acc[...] += mm(p.astype(BF), vals[at, :])

    last = run // (CHUNK // RUN)

    def plain(j, _):
        for u in range(UNROLL):
            visit(j * UNROLL + u, False)
        return 0

    def single(j, _):
        visit(j, False)
        return 0

    lax.fori_loop(0, last // UNROLL, plain, 0)
    lax.fori_loop(last // UNROLL * UNROLL, last, single, 0)
    visit(last, True)
    total = acc[:, HEAD:]
    out = acc[:, :HEAD] / total
    log = jnp.log2(total)
    o_ref[:, :HEAD] = out[:RUN]
    o_ref[:, HEAD:] = out[RUN:]
    l_ref[:, :HEAD] = log[:RUN]
    l_ref[:, HEAD:] = log[RUN:]


def attention_forward(order, own, q, kv):
    length = order.shape[0] * RUN
    tokens = q.shape[0]
    block = pl.BlockSpec((RUN, 2 * HEAD), lambda i, *_: (i, 0))
    return pl.pallas_call(
        forward_kernel,
        grid_spec=pltpu.PrefetchScalarGridSpec(
            num_scalar_prefetch=2,
            grid=(tokens // RUN,),
            in_specs=[block, pl.BlockSpec(kv.shape, lambda i, *_: (0, 0))],
            out_specs=[block, block],
            scratch_shapes=[
                pltpu.VMEM((length, HEAD), BF),
                pltpu.VMEM((length, 2 * HEAD), BF),
                pltpu.VMEM((2 * RUN, 2 * HEAD), F32),
            ],
        ),
        out_shape=(jax.ShapeDtypeStruct(q.shape, F32), jax.ShapeDtypeStruct(q.shape, F32)),
        compiler_params=pltpu.CompilerParams(
            dimension_semantics=("arbitrary",), vmem_limit_bytes=VMEM
        ),
        name="attention_forward",
    )(order, own, q, kv)


def backward_kernel(
    order, own, q_ref, g_ref, o_ref, l_ref, kv_ref, dq_ref, dkv_ref,
    keys, keys_t, vals, dk, dv, dq_t, q_t, g_t,
):
    step = pl.program_id(0)
    n_runs = order.shape[0]

    @pl.when(step == 0)
    def _():
        dk[...] = jnp.zeros_like(dk)
        dv[...] = jnp.zeros_like(dv)

        def place(r, _):
            src = pl.ds(pl.multiple_of(r // 8 * KV_ROWS + r % 8 * RUN, 16), RUN)
            dst = pl.ds(pl.multiple_of(order[r] * RUN, RUN), RUN)
            k = kv_ref[src, :HEAD]
            keys[dst, :] = k
            keys_t[:, dst] = k.T
            vals[dst, :] = kv_ref[src, HEAD:]
            return 0

        lax.fori_loop(0, n_runs, place, 0, unroll=8)

    run = own[step]
    query = stacked(q_ref)
    grad = stacked(g_ref)
    q_t[...] = query.T
    g_t[...] = grad.T
    delta = jnp.sum((grad.astype(F32) * stacked(o_ref)).T, axis=0, keepdims=True)
    log = stacked(l_ref).T[:1]
    dq_t[...] = jnp.zeros_like(dq_t)

    def visit(j, masked):
        at = pl.ds(pl.multiple_of(j * CHUNK, CHUNK), CHUNK)
        s = mm(keys[at, :], q_t[...])
        p = jnp.exp2(s * (SCALE * LOG2E) - log)
        if masked:
            row = lax.broadcasted_iota(jnp.int32, p.shape, 1) % RUN + run * RUN
            col = lax.broadcasted_iota(jnp.int32, p.shape, 0) + j * CHUNK
            p = jnp.where(col <= row, p, 0.0)
        dp = mm(vals[at, :], g_t[...])
        ds = (p * (dp - delta)).astype(BF)
        dv[at, :] += mm(p.astype(BF), grad)
        dk[at, :] += mm(ds, query)
        dq_t[...] += mm(keys_t[:, at], ds)

    last = run // (CHUNK // RUN)

    def plain(j, _):
        for u in range(UNROLL):
            visit(j * UNROLL + u, False)
        return 0

    def single(j, _):
        visit(j, False)
        return 0

    lax.fori_loop(0, last // UNROLL, plain, 0)
    lax.fori_loop(last // UNROLL * UNROLL, last, single, 0)
    visit(last, True)
    out = dq_t[...].T * SCALE
    dq_ref[:, :HEAD] = out[:RUN]
    dq_ref[:, HEAD:] = out[RUN:]

    @pl.when(step == pl.num_programs(0) - 1)
    def _():
        def give(r, _):
            dst = pl.ds(pl.multiple_of(r * RUN, RUN), RUN)
            src = pl.ds(pl.multiple_of(order[r] * RUN, RUN), RUN)
            dkv_ref[dst, :HEAD] = (dk[src, :] * SCALE).astype(BF)
            dkv_ref[dst, HEAD:] = dv[src, :].astype(BF)
            return 0

        lax.fori_loop(0, n_runs, give, 0, unroll=8)


def attention_backward(order, own, q, g, o, log, kv):
    length = order.shape[0] * RUN
    tokens = q.shape[0]
    block = pl.BlockSpec((RUN, 2 * HEAD), lambda i, *_: (i, 0))
    all_rows = pl.BlockSpec((length, 2 * HEAD), lambda i, *_: (0, 0))
    return pl.pallas_call(
        backward_kernel,
        grid_spec=pltpu.PrefetchScalarGridSpec(
            num_scalar_prefetch=2,
            grid=(tokens // RUN,),
            in_specs=[block, block, block, block, pl.BlockSpec(kv.shape, lambda i, *_: (0, 0))],
            out_specs=[block, all_rows],
            scratch_shapes=[
                pltpu.VMEM((length, HEAD), BF),
                pltpu.VMEM((HEAD, length), BF),
                pltpu.VMEM((length, HEAD), BF),
                pltpu.VMEM((length, HEAD), F32),
                pltpu.VMEM((length, HEAD), F32),
                pltpu.VMEM((HEAD, 2 * RUN), F32),
                pltpu.VMEM((HEAD, 2 * RUN), BF),
                pltpu.VMEM((HEAD, 2 * RUN), BF),
            ],
        ),
        out_shape=(jax.ShapeDtypeStruct(q.shape, F32), jax.ShapeDtypeStruct((length, 2 * HEAD), BF)),
        compiler_params=pltpu.CompilerParams(
            dimension_semantics=("arbitrary",), vmem_limit_bytes=VMEM
        ),
        name="attention_backward",
    )(order, own, q, g, o, log, kv)


def inverse_rms(value):
    return lax.rsqrt(jnp.mean(value * value, axis=-1, keepdims=True) + EPS)


def norm_back(value, inverse, gain, grad):
    scaled = grad * gain
    inner = jnp.sum(scaled * value, axis=-1, keepdims=True)
    return inverse * scaled - value * inverse * inverse * inverse * inner / value.shape[-1]


def finish_kernel(
    gate_ref, up_ref, down_ref, out_ref, query_ref, pair_ref, parts_ref, grad_ref, x_ref, scale_ref,
    middle_ref, last_ref,
    layer_o, input_o, query_o, key_o, value_o, out_o, gate_o, up_o, down_o,
):
    for source, target in (
        (gate_ref, gate_o), (up_ref, up_o), (down_ref, down_o), (out_ref, out_o), (query_ref, query_o)
    ):
        target[...] = source[...].astype(F32)
    for i in range(8):
        to = slice(i * HEAD, (i + 1) * HEAD)
        key_o[:, to] = pair_ref[:, 2 * i * HEAD : (2 * i + 1) * HEAD].astype(F32)
        value_o[:, to] = pair_ref[:, (2 * i + 1) * HEAD : (2 * i + 2) * HEAD].astype(F32)
    x = x_ref[...].astype(F32)
    grad = jnp.sum(parts_ref[...].astype(F32), axis=0)
    input_o[...] = grad_ref[...] + norm_back(x, inverse_rms(x), scale_ref[...], grad)
    last = jnp.sum(last_ref[...].astype(F32), axis=0)
    layer_o[...] = (middle_ref[...] + last).astype(BF)


def finish(gate_up, down, out, qkv, parts, grad, x, scale, middle, last):
    steps = 4
    tokens, width = x.shape

    def rows_of(a, n, offset=0):
        return pl.BlockSpec((n // steps, a.shape[-1]), lambda i: (i + offset, 0))

    def deep(a):
        return pl.BlockSpec((a.shape[0], tokens // steps, width), lambda i: (0, i, 0))

    part = qkv.shape[0] // 2
    specs = [
        rows_of(gate_up, part), rows_of(gate_up, part, steps), rows_of(down, down.shape[0]),
        rows_of(out, out.shape[0]), rows_of(qkv, part), rows_of(qkv, part, steps), deep(parts),
        rows_of(grad, tokens), rows_of(x, tokens), pl.BlockSpec(scale.shape, lambda i: (0, 0)),
        rows_of(middle, tokens), deep(last),
    ]
    shapes = [
        ((tokens, width), BF), ((tokens, width), F32), ((part, 2 * width), F32), ((part, width), F32),
        ((part, width), F32), (out.shape, F32), ((part, gate_up.shape[1]), F32),
        ((part, gate_up.shape[1]), F32), (down.shape, F32),
    ]
    return pl.pallas_call(
        finish_kernel,
        grid=(steps,),
        in_specs=specs,
        out_specs=[pl.BlockSpec((s[0] // steps, s[1]), lambda i: (i, 0)) for s, _ in shapes],
        out_shape=tuple(jax.ShapeDtypeStruct(s, d) for s, d in shapes),
        compiler_params=pltpu.CompilerParams(
            dimension_semantics=("arbitrary",), vmem_limit_bytes=VMEM
        ),
        name="finish",
    )(gate_up, gate_up, down, out, qkv, qkv, parts, grad, x, scale, middle, last)


def dot(a, b):
    return jnp.dot(a, b, preferred_element_type=F32)


def dot_t(a, b):
    return lax.dot_general(a, b, (((0,), (0,)), ((), ())), preferred_element_type=F32)


def summed(parts, count):
    return jnp.sum(parts.reshape((count, -1) + parts.shape[1:]).astype(F32), axis=0)


def row_of(vector):
    return jnp.pad(vector.reshape(1, -1), ((0, 0), (0, 128 - vector.shape[-1])))


def project_kernel(x_ref, w_ref, scale_ref, head_ref, cos_ref, sin_ref, tag_ref, n_ref, p_ref, q_ref, kv_ref):
    step = pl.program_id(0)
    x = x_ref[0, :RUN, :].astype(F32)
    low = (x * inverse_rms(x) * scale_ref[...]).astype(BF)
    n_ref[...] = low
    out = mm(low, w_ref[...])
    p_ref[...] = out[:, : 3 * HEAD]
    turned = []
    for h in range(3):
        v = out[:, h * HEAD : (h + 1) * HEAD]
        v = v * inverse_rms(v) * head_ref[h : h + 1, :]
        turned.append((v * cos_ref[...] + pltpu.roll(v, HEAD // 2, 1) * sin_ref[...]).astype(BF))
    q_ref[:, :HEAD] = turned[0]
    q_ref[:, HEAD:] = turned[1]
    at = pl.ds(pl.multiple_of(step * RUN, RUN), RUN)
    kv_ref[at, :HEAD] = turned[2]
    kv_ref[at, HEAD:] = out[:, 3 * HEAD :].astype(BF)

    @pl.when(step == 0)
    def _():
        kv_ref[pl.ds(8 * RUN, TAG), :] = tag_ref[...]


def project(x, w, scale, head_scale, cos, sin, tag):
    width = x.shape[-1]
    group = 8 * RUN

    def fixed(a):
        return pl.BlockSpec(a.shape, lambda i: (0,) * a.ndim)

    def moving(n):
        return pl.BlockSpec((RUN, n), lambda i: (i, 0))

    return pl.pallas_call(
        project_kernel,
        grid=(8,),
        in_specs=[
            pl.BlockSpec((1, X_ROWS, width), lambda i: (i, 0, 0)),
            fixed(w), fixed(scale), fixed(head_scale), moving(HEAD), moving(HEAD), fixed(tag),
        ],
        out_specs=[
            moving(width), moving(3 * HEAD), moving(2 * HEAD),
            pl.BlockSpec((KV_ROWS, 2 * HEAD), lambda i: (0, 0)),
        ],
        out_shape=(
            jax.ShapeDtypeStruct((group, width), BF),
            jax.ShapeDtypeStruct((group, 3 * HEAD), F32),
            jax.ShapeDtypeStruct((group, 2 * HEAD), BF),
            jax.ShapeDtypeStruct((KV_ROWS, 2 * HEAD), BF),
        ),
        compiler_params=pltpu.CompilerParams(
            dimension_semantics=("arbitrary",), vmem_limit_bytes=VMEM
        ),
        name="project",
    )(x, w, scale, head_scale, cos, sin, tag)


def unproject_kernel(
    kv_ref, t_ref, p_ref, x_ref, w_ref, head_ref, cos_ref, sin_ref, mlp_ref,
    g_ref, n_ref, tile_ref, attn_acc, head_acc,
):
    step = pl.program_id(0)

    @pl.when(step == 0)
    def _():
        attn_acc[...] = jnp.zeros_like(attn_acc)
        head_acc[...] = jnp.zeros_like(head_acc)

    kv = kv_ref[0].astype(F32)
    for chip in range(1, 8):
        kv = kv + kv_ref[chip].astype(F32)
    for h in range(3):
        turn = kv[:, :HEAD] if h == 2 else t_ref[:, h * HEAD : (h + 1) * HEAD]
        grad = turn * cos_ref[...] - pltpu.roll(turn, HEAD // 2, 1) * sin_ref[...]
        v = p_ref[:, h * HEAD : (h + 1) * HEAD]
        inverse = inverse_rms(v)
        back = norm_back(v, inverse, head_ref[h : h + 1, :], grad)
        g_ref[:, h * HEAD : (h + 1) * HEAD] = back.astype(BF)
        head_acc[h // 2 : h // 2 + 1, :] += jnp.sum(grad * v * inverse, axis=0, keepdims=True)
    g_ref[:, 3 * HEAD :] = kv[:, HEAD:].astype(BF)
    wide = mm(g_ref[...], w_ref[...], NT)
    n_ref[...] = wide.astype(BF)
    x = x_ref[0, :RUN, :].astype(F32)
    attn_acc[...] += jnp.sum(wide * x * inverse_rms(x), axis=0, keepdims=True)

    @pl.when(step == pl.num_programs(0) - 1)
    def _():
        tile_ref[...] = jnp.zeros_like(tile_ref)
        for j in range(8):
            tile_ref[j * 8 : j * 8 + 1, :] = attn_acc[:, j * 128 : (j + 1) * 128]
            tile_ref[j * 8 + 1 : j * 8 + 2, :] = mlp_ref[:, j * 128 : (j + 1) * 128]
            tile_ref[j * 8 + 2 : j * 8 + 4, :] = head_acc[...]


def unproject(kv_parts, turn, pre, x, w, head_scale, cos, sin, mlp_part):
    width = x.shape[-1]
    group = 8 * RUN

    def fixed(a):
        return pl.BlockSpec(a.shape, lambda i: (0,) * a.ndim)

    def moving(n):
        return pl.BlockSpec((RUN, n), lambda i: (i, 0))

    return pl.pallas_call(
        unproject_kernel,
        grid=(8,),
        in_specs=[
            pl.BlockSpec((8, RUN, 2 * HEAD), lambda i: (0, i, 0)),
            moving(2 * HEAD), moving(3 * HEAD),
            pl.BlockSpec((1, X_ROWS, width), lambda i: (i, 0, 0)),
            fixed(w), fixed(head_scale), moving(HEAD), moving(HEAD), fixed(mlp_part),
        ],
        out_specs=[moving(4 * HEAD), moving(width), pl.BlockSpec((64, 128), lambda i: (0, 0))],
        out_shape=(
            jax.ShapeDtypeStruct((group, 4 * HEAD), BF),
            jax.ShapeDtypeStruct((group, width), BF),
            jax.ShapeDtypeStruct((64, 128), F32),
        ),
        scratch_shapes=[pltpu.VMEM((1, width), F32), pltpu.VMEM((2, HEAD), F32)],
        compiler_params=pltpu.CompilerParams(
            dimension_semantics=("arbitrary",), vmem_limit_bytes=VMEM
        ),
        name="unproject",
    )(kv_parts, turn, pre, x, w, head_scale, cos, sin, mlp_part)


def local(
    hidden_in, positions, attn_gain, query_weight, key_matrix, value_matrix, output_weight,
    query_norm_gain, key_gain, mlp_gain, gate_weight, up_weight, down_weight, cotangent,
):
    hidden = hidden_in[0]
    cot = cotangent[0]
    tokens, width = hidden.shape
    group = 8 * tokens
    ff = gate_weight.shape[1] // 8
    part = width // 8
    core = lax.axis_index("ctx") % 2
    def rows(size):
        return lambda ref: (lambda io, n: io[ref].at[pl.ds(pl.multiple_of(n * size, size), size)])

    gain_tile = jnp.concatenate(
        [row_of(g.astype(F32)) for g in (attn_gain, mlp_gain, query_norm_gain, key_gain)]
        + [jnp.zeros((4, 128), F32)],
        axis=0,
    )
    own_run = (positions[:, :1] // RUN).astype(BF)
    tagged = jnp.concatenate([hidden, jnp.broadcast_to(own_run, (TAG, width))], axis=0)
    plan = Plan()
    relays = [plan.gather_tokens(0, 5, X_ROWS)]
    plan.gather_group(1, 6, 8)
    relays += [
        plan.weights(2, 7, part, 256, 0),
        plan.weights(3, 7, part, 128, 256),
        plan.weights(4, 7, part, 128, 384),
    ]
    for relay in relays:
        relay()
    x_all, gains, w_qkv = exchange(
        plan, 1, (((8 * X_ROWS, width), BF), ((64, 128), F32), ((width, 512), BF)),
        tagged, gain_tile, query_weight, key_matrix, value_matrix,
    )
    gains = gains.reshape(8, 8, 128)
    attn_scale = gains[:, 0].reshape(1, width)
    mlp_scale = gains[:, 1].reshape(1, width)
    query_scale = gains[:, 2, :16].reshape(1, HEAD)
    key_scale = gains[:, 3, :16].reshape(1, HEAD)
    x_all = x_all.reshape(8, X_ROWS, width)
    own_bf = x_all[:, RUN, 0]
    own = own_bf.astype(jnp.int32)
    head_scale = jnp.concatenate([query_scale, query_scale, key_scale], axis=0)
    place_rows = (own[:, None] * RUN + jnp.arange(RUN, dtype=jnp.int32)[None, :]).reshape(group)
    frequency = 1.0 / THETA ** (jnp.arange(0, HEAD, 2, dtype=F32) / HEAD)
    angle = place_rows.astype(F32)[:, None] * jnp.tile(frequency, 2)[None, :]
    sign = jnp.where(jnp.arange(HEAD) < HEAD // 2, -1.0, 1.0).astype(F32)
    cos, sin = jnp.cos(angle), jnp.sin(angle) * sign[None, :]
    tag = jnp.pad(jnp.broadcast_to(own_bf[None, :], (TAG, 8)), ((0, 0), (0, 2 * HEAD - 8)))
    norm_one, pre, queries, kv = project(x_all, w_qkv, attn_scale, head_scale, cos, sin, tag)

    plan = Plan()
    own_kv = block(4, At.chip, KV_ROWS)
    side_kv = block(4, lambda at: at.but(y=1 - at.y).chip(), KV_ROWS)
    half = group // 2

    def upper(io, at):
        return io[4].at[pl.ds(pl.multiple_of(at.chip() * KV_ROWS, 16), half)]

    def lower(io, at):
        return io[4].at[pl.ds(pl.multiple_of(at.chip() * KV_ROWS + half, 16), KV_ROWS - half)]

    def left(of, flip):
        return lambda io, at: of(io, at.but(x=(at.x + 3) % 4, y=1 - at.y if flip else at.y))

    def right(of, flip):
        return lambda io, at: of(io, at.but(x=(at.x + 1) % 4, y=1 - at.y if flip else at.y))

    side = plan.add(Shift(y=1), full(0), own_kv)
    right_id = plan.add(Shift(x=1), full(0), own_kv)
    left_id = plan.add(Shift(x=-1), full(0), own_kv)
    plan.add(None, full(0), own_kv)
    relay_tokens = plan.gather_tokens(1, 5, tokens)
    relays = [plan.weights(2, 6, part, ff, 0), plan.weights(3, 6, part, ff, ff)]
    side_right = plan.add(Shift(x=1), side_kv, side_kv, needs=[side])
    side_left = plan.add(Shift(x=-1), side_kv, side_kv, needs=[side])
    plan.add(Shift(x=1), left(upper, 0), left(upper, 0), needs=[right_id])
    plan.add(Shift(x=-1), right(lower, 0), right(lower, 0), needs=[left_id])
    relay_tokens()
    plan.add(Shift(x=1), left(upper, 1), left(upper, 1), needs=[side_right])
    plan.add(Shift(x=-1), right(lower, 1), right(lower, 1), needs=[side_left])
    for relay in relays:
        relay()
    kv_all, cot_all, w_gu = exchange(
        plan, 2, (((8 * KV_ROWS, 256), BF), ((group, width), BF), ((width, 2 * ff), BF)),
        kv, cot, gate_weight, up_weight,
    )
    order = kv_all.reshape(8, KV_ROWS, 256)[:, 8 * RUN, :8].reshape(64).astype(jnp.int32)
    attention, log_total = attention_forward(order, own, queries, kv_all)
    mixed = attention.astype(BF)
    branch_part = dot(mixed, output_weight).astype(BF)

    plan = Plan()
    plan.return_tokens(0, 1, tokens)
    (branch,) = exchange(plan, 3, (((group, width), BF),), branch_part)
    residual = hidden.astype(F32)
    middle = residual + summed(branch, 8)
    mlp_inverse = inverse_rms(middle)
    norm_two_own = (middle * mlp_inverse * mlp_scale).astype(BF)
    plan = Plan()
    plan.gather_tokens(0, 1, tokens)()
    (norm_two,) = exchange(plan, 4, (((group, width), BF),), norm_two_own)

    gate_up = dot(norm_two, w_gu)
    gate, up = gate_up[:, :ff], gate_up[:, ff:]
    sigma = jax.nn.sigmoid(gate)
    swish = gate * sigma
    inner = (swish * up).astype(BF)
    inner_grad = lax.dot_general(cot_all, down_weight, NT, preferred_element_type=F32)
    gate_up_grad = jnp.concatenate(
        [
            (inner_grad * up * sigma * (1.0 + gate * (1.0 - sigma))).astype(BF),
            (inner_grad * swish).astype(BF),
        ],
        axis=1,
    )
    norm_two_part = lax.dot_general(gate_up_grad, w_gu, NT, preferred_element_type=F32).astype(BF)
    gate_up_wgrad = dot_t(norm_two, gate_up_grad).astype(BF).reshape(8, part, 2 * ff)
    down_wgrad = dot_t(inner, cot_all).astype(BF)

    def theirs(ref, size):
        def pick(io, at):
            cut = pl.ds(pl.multiple_of((1 - at.c) * size, size), size)
            return io[ref].at[..., cut]

        return pick

    def my_half(both, got):
        size = got.shape[-1]
        mine = lax.dynamic_slice_in_dim(both, core * size, size, axis=both.ndim - 1)
        return (mine.astype(F32) + got.astype(F32)).astype(BF)

    plan = Plan()
    plan.return_tokens(0, 3, tokens)
    plan.add(Shift(c=1), theirs(1, ff), full(4))
    plan.add(Shift(c=1), theirs(2, width // 2), full(5))
    norm_two_parts, gate_up_got, down_got = exchange(
        plan, 5, (((group, width), BF), ((8, part, ff), BF), ((ff, width // 2), BF)),
        norm_two_part, gate_up_wgrad, down_wgrad,
    )
    norm_two_grad = summed(norm_two_parts, 8)
    middle_grad = cot.astype(F32) + norm_back(middle, mlp_inverse, mlp_scale, norm_two_grad)
    mlp_gain_part = jnp.sum(norm_two_grad * middle * mlp_inverse, axis=0)
    branch_grad_own = middle_grad.astype(BF)
    gate_up_half = my_half(gate_up_wgrad, gate_up_got)
    down_half = my_half(down_wgrad, down_got)

    plan = Plan()
    plan.gather_tokens(0, 3, tokens)()
    plan.scatter_chips(
        lambda io, n: io[1].at[:, pl.ds(pl.multiple_of(n * 16, 16), 16)], lambda io, n: io[4].at[n]
    )
    plan.scatter_chips(rows(ff // 8)(2), lambda io, n: io[5].at[n])
    branch_grad, gate_up_pieces, down_pieces = exchange(
        plan, 6, (((group, width), BF), ((8, 8, 16, ff), BF), ((8, ff // 8, width // 2), BF)),
        branch_grad_own, gate_up_half, down_half,
    )
    mixed_grad = lax.dot_general(branch_grad, output_weight, NT, preferred_element_type=F32).astype(BF)
    output_wgrad = dot_t(mixed, branch_grad).astype(BF)
    down_part = dot(inner, down_weight).astype(BF)
    gate_up_sum = jnp.sum(gate_up_pieces.astype(F32), axis=0).astype(BF)
    down_sum = jnp.sum(down_pieces.astype(F32), axis=0).astype(BF)
    query_turn, kv_part = attention_backward(
        order, own, queries, mixed_grad, attention, log_total, kv_all
    )

    plan = Plan()
    plan.scatter_chips(rows(group)(0), rows(group)(4))
    pair = 2 * tokens
    for k in (1, 3, 2):
        plan.add(
            Shift(z=k),
            block(1, lambda at, k=k: (at.z + k) % 4, pair),
            block(5, lambda at: at.z, pair),
        )
    plan.add(None, block(1, lambda at: at.z, pair), block(5, lambda at: at.z, pair))
    plan.add(Shift(c=1), theirs(2, width // 2), full(6))
    plan.scatter_group(
        lambda io, n: io[3].at[n],
        lambda io, n: io[7].at[:, pl.ds(pl.multiple_of(n * ff, ff), ff)],
    )
    n_rows = output_wgrad.shape[0]
    kv_parts, down_parts, output_got, gate_up_own = exchange(
        plan, 7,
        (
            ((8 * group, 256), BF), ((group, width), BF), ((n_rows, width // 2), BF),
            ((16, 8 * ff), BF),
        ),
        kv_part, down_part, output_wgrad, gate_up_sum,
    )
    down_pair = summed(down_parts, 4).astype(BF)
    output_half = my_half(output_wgrad, output_got)
    qkv_grad, norm_one_part, gain_parts = unproject(
        kv_parts.reshape(8, group, 2 * HEAD), query_turn, pre, x_all, w_qkv, head_scale, cos, sin,
        mlp_gain_part.reshape(1, width),
    )
    qkv_wgrad = dot_t(norm_one, qkv_grad).astype(BF).reshape(8, part, 512)

    plan = Plan()
    plan.return_tokens(0, 4, tokens)

    def wgrad_piece(io, chip, c):
        return io[1].at[
            :, pl.ds(pl.multiple_of(chip * 16, 16), 16), pl.ds(pl.multiple_of(c * 256, 256), 256)
        ]

    for shift in [Shift(c=1)] + [
        Shift(s.by[0], s.by[1], c) for s in plan.chip_shifts() for c in (0, 1)
    ]:
        plan.add(
            shift,
            lambda io, at, s=shift: wgrad_piece(io, s.to(at).chip(), s.to(at).c),
            lambda io, at: io[5].at[at.chip() * 2 + at.c],
        )
    plan.add(
        None,
        lambda io, at: wgrad_piece(io, at.chip(), at.c),
        lambda io, at: io[5].at[at.chip() * 2 + at.c],
    )
    plan.scatter_chips(rows(n_rows // 8)(2), lambda io, n: io[6].at[n])
    plan.scatter_group(rows(8)(3), rows(8)(7))

    def stacked_rows(ref, size, total):
        def land(io, chip, c):
            return io[ref].at[pl.ds(pl.multiple_of(c * total + chip * size, size), size)]

        return land, lambda io, c: io[ref].at[pl.ds(pl.multiple_of(c * total, total), total)]

    def side_columns(ref, size):
        def at_core(c):
            return pl.ds(pl.multiple_of(c * (width // 2), width // 2), width // 2)

        def land(io, chip, c):
            return io[ref].at[pl.ds(pl.multiple_of(chip * size, size), size), at_core(c)]

        return land, lambda io, c: io[ref].at[:, at_core(c)]

    norm_one_parts, qkv_pieces, output_pieces, gain_sums = exchange(
        plan, 8,
        (
            ((group, width), BF), ((16, 8, 16, 256), BF), ((8, n_rows // 8, width // 2), BF),
            ((64, 128), F32),
        ),
        norm_one_part, qkv_wgrad, output_half, gain_parts,
    )
    qkv_sum = jnp.sum(qkv_pieces.astype(F32), axis=0).astype(BF)
    output_sum = jnp.sum(output_pieces.astype(F32), axis=0).astype(BF)
    gain_sum = summed(gain_sums, 8)

    plan = Plan()
    to_group = plan.scatter_group(
        lambda io, n: io[0].at[n],
        lambda io, n: io[6].at[:, pl.ds(pl.multiple_of(n * 256, 256), 256)],
    )
    later = [
        plan.gather_chips(full(4), *stacked_rows(11, 16, part)),
        plan.gather_chips(full(5), *side_columns(12, ff // 8)),
        plan.gather_chips(full(1), *side_columns(8, n_rows // 8)),
    ]
    plan.gather_context(2, 9, 8)
    own_block = block(3, lambda at: at.c, tokens)
    other_block = block(3, lambda at: 1 - at.c, tokens)

    def landed(n):
        return lambda io, at: io[10].at[pl.ds(n * tokens, tokens)]

    plan.add(Shift(d=1), own_block, landed(1), away)
    plan.add(Shift(d=1, c=1), other_block, landed(1), away)
    plan.add(None, own_block, landed(0), home)
    plan.add(Shift(c=1), other_block, landed(0), home)
    later.append(plan.gather_chips(full(6), *stacked_rows(7, 16, part), needs=to_group))
    for relay, _ in later:
        relay()
    for _, share in later:
        share()
    _, qkv_final, output_final, gain_all, down_last, gate_up_final, down_final = exchange(
        plan, 9,
        (
            ((16, 2048), BF), ((2 * part, 2048), BF), ((n_rows, width), BF), ((128, 128), F32),
            ((2 * tokens, width), BF), ((2 * part, 8 * ff), BF), ((ff, width), BF),
        ),
        qkv_sum, output_sum, gain_sum, down_pair, gate_up_own, down_sum,
    )
    layer_out, input_grad, query_wgrad, key_wgrad, value_wgrad, output_wgrad, gate_wgrad, up_wgrad, down_wgrad = finish(
        gate_up_final, down_final, output_final, qkv_final, norm_one_parts.reshape(8, tokens, width),
        middle_grad, hidden, attn_scale, middle, down_last.reshape(2, tokens, width),
    )
    gain_total = summed(gain_all, 16)
    head = lax.axis_index("dp") * 4 + lax.axis_index("fsdp")
    return (
        layer_out[None],
        input_grad[None],
        gain_total[0],
        query_wgrad,
        key_wgrad,
        value_wgrad,
        output_wgrad,
        lax.dynamic_slice_in_dim(gain_total[2], head * 16, 16),
        lax.dynamic_slice_in_dim(gain_total[3], head * 16, 16),
        gain_total[1],
        gate_wgrad,
        up_wgrad,
        down_wgrad,
    )


def solution(mesh):
    tokens = P("dp", ("ctx", "fsdp"), None)
    places = P("dp", ("ctx", "fsdp"))
    vector = P(("dp", "fsdp"))
    matrix = P(("dp", "fsdp"), None)
    in_specs = (
        tokens, places, vector, matrix, matrix, matrix, matrix,
        vector, vector, vector, matrix, matrix, matrix, tokens,
    )
    out_specs = (
        tokens, tokens, vector, matrix, matrix, matrix, matrix,
        vector, vector, vector, matrix, matrix, matrix,
    )
    return jax.shard_map(local, mesh=mesh, in_specs=in_specs, out_specs=out_specs, check_vma=False)
```

```python
import jax
import jax.numpy as jnp
from jax import lax
from jax.experimental import pallas as pl
from jax.experimental.pallas import tpu as pltpu
from jax.sharding import PartitionSpec as P

HEAD = 128
EPS = 1e-06
THETA = 1000000.0
SCALE = HEAD ** (-0.5)
LOG2E = 1.4426950408889634
RUN = 128
CHUNK = 512
VMEM = 60 * 2**20
UNROLL = 4
TAG = 16
X_ROWS = RUN + TAG
KV_ROWS = 8 * RUN + TAG
BF = jnp.bfloat16
F32 = jnp.float32
MESH = pl.DeviceIdType.MESH


class At:
    def __init__(self, x, y, c, d, z):
        self.x, self.y, self.c, self.d, self.z = x, y, c, d, z

    def but(self, **new):
        return At(**{**self.__dict__, **new})

    def chip(self):
        return self.x * 2 + self.y

    def head(self):
        return self.d * 4 + self.z

    def slot(self):
        return self.z * 2 + self.c

    def device(self):
        return ((self.x * 2 + self.y) * 2 + self.c, self.d, self.z)


def here():
    ctx = lax.axis_index("ctx")
    return At(ctx // 4, ctx // 2 % 2, ctx % 2, lax.axis_index("dp"), lax.axis_index("fsdp"))


class Shift:
    def __init__(self, x=0, y=0, c=0, d=0, z=0):
        self.by = (x, y, c, d, z)

    def move(self, at, sign):
        x, y, c, d, z = self.by
        return At(
            (at.x + 4 + sign * x) % 4 if x else at.x,
            1 - at.y if y else at.y,
            1 - at.c if c else at.c,
            1 - at.d if d else at.d,
            (at.z + 4 + sign * z) % 4 if z else at.z,
        )

    def to(self, at):
        return self.move(at, 1)

    def back(self, at):
        return self.move(at, -1)

    def key(self):
        return self.by


class Op:
    def __init__(self, shift, src, dst, cond=None, needs=()):
        self.shift, self.src, self.dst, self.cond, self.needs = shift, src, dst, cond, needs


class Work:
    def __init__(self, inputs, outs, scratch, greets, body):
        self.inputs, self.outs, self.scratch, self.greets, self.body = inputs, outs, scratch, greets, body


def exchange(ops, collective_id, out_shapes, *arrays, work=None):
    n_in, n_out, n_ops = len(arrays), len(out_shapes), len(ops)
    work = work or Work([], [], [], [], None)
    n_more, n_made = len(work.inputs), len(work.outs)

    def kernel(*refs):
        refs = list(refs)
        ins, more = refs[:n_in], refs[n_in : n_in + n_more]
        refs = refs[n_in + n_more :]
        outs, made = refs[:n_out], refs[n_out : n_out + n_made]
        send_sem, recv_sem = refs[n_out + n_made : n_out + n_made + 2]
        scratch = refs[n_out + n_made + 2 :]
        io = ins + outs
        me = here()

        def when(cond, act):
            if cond is None:
                act()
            else:
                pl.when(cond)(act)

        barrier = pltpu.get_barrier_semaphore()
        seen, count = set(), 0
        for op in ops:
            if op.shift is None or (op.shift.key(), op.cond) in seen:
                continue
            seen.add((op.shift.key(), op.cond))
            source = op.shift.back(me)

            def greet(source=source):
                pl.semaphore_signal(barrier, inc=1, device_id=source.device(), device_id_type=MESH)

            when(op.cond and op.cond(source), greet)
            count = count + (1 if op.cond is None else jnp.where(op.cond(me), 1, 0))
        for shift in work.greets:
            source = shift.back(me)
            pl.semaphore_signal(barrier, inc=1, device_id=source.device(), device_id_type=MESH)
            count = count + 1
        pl.semaphore_wait(barrier, count)

        def copy(t, sender):
            op = ops[t]
            if op.shift is None:
                return pltpu.make_async_copy(op.src(io, me), op.dst(io, me), send_sem.at[t])
            return pltpu.make_async_remote_copy(
                src_ref=op.src(io, sender),
                dst_ref=op.dst(io, sender),
                send_sem=send_sem.at[t],
                recv_sem=recv_sem.at[t],
                device_id=op.shift.to(me).device(),
                device_id_type=MESH,
            )

        arrived = set()

        def arrive(t):
            if t in arrived:
                return
            arrived.add(t)
            op = ops[t]
            source = me if op.shift is None else op.shift.back(me)

            def wait():
                if op.shift is None:
                    copy(t, me).wait()
                else:
                    copy(t, source).wait_recv()

            when(op.cond and op.cond(source), wait)

        for t, op in enumerate(ops):
            for need in op.needs:
                arrive(need)
            when(op.cond and op.cond(me), lambda t=t: copy(t, me).start())
        if work.body is not None:
            work.body(me, more, outs, made, scratch)
        for t, op in enumerate(ops):
            arrive(t)
            if op.shift is not None:
                when(op.cond and op.cond(me), lambda t=t: copy(t, me).wait_send())

    anywhere = pl.BlockSpec(memory_space=pl.ANY)
    return pl.pallas_call(
        kernel,
        out_shape=tuple(jax.ShapeDtypeStruct(s, d) for s, d in out_shapes)
        + tuple(jax.ShapeDtypeStruct(s, d) for s, d in work.outs),
        in_specs=[anywhere] * n_in + [pl.BlockSpec(memory_space=m) for _, m in work.inputs],
        out_specs=tuple([anywhere] * n_out + [pl.BlockSpec(memory_space=pltpu.VMEM)] * n_made),
        scratch_shapes=[
            pltpu.SemaphoreType.DMA((n_ops,)),
            pltpu.SemaphoreType.DMA((n_ops,)),
        ]
        + work.scratch,
        compiler_params=pltpu.CompilerParams(
            collective_id=collective_id,
            has_side_effects=True,
            vmem_limit_bytes=VMEM if work.body else None,
        ),
        name="exchange_%d" % collective_id,
    )(*arrays, *(a for a, _ in work.inputs))


def home(at):
    return at.c == at.d


def away(at):
    return at.c != at.d


def block(index, start, size):
    return lambda io, at: io[index].at[pl.ds(pl.multiple_of(start(at) * size, size), size)]


def full(index):
    return lambda io, at: io[index]


class Plan(list):
    def add(self, *args, **named):
        self.append(Op(*args, **named))
        return len(self) - 1

    def gather_tokens(self, src, dst, size):
        mine = block(dst, At.slot, size)
        self.add(None, full(src), mine, home)
        got = {}
        for name, by in (("side", {"d": 1}), ("up", {"z": 1}), ("down", {"z": -1})):
            got[name] = [
                self.add(Shift(**by), full(src), mine, home),
                self.add(Shift(c=1, **by), full(src), mine, away),
            ]
        self.add(Shift(c=1), full(src), mine, away)

        def relays():
            both = block(dst, lambda at: at.z, 2 * size)
            below = block(dst, lambda at: (at.z + 3) % 4 * 2, size)
            above = block(dst, lambda at: (at.z + 1) % 4 * 2 + 1, size)
            up = self.add(Shift(z=1), both, both, away, got["side"])
            down = self.add(Shift(z=-1), both, both, away, got["side"])
            self.add(Shift(z=1), below, below, home, got["up"])
            self.add(Shift(z=-1), above, above, home, got["down"])
            self.add(Shift(z=1), below, below, away, [up])
            self.add(Shift(z=-1), above, above, away, [down])

        return relays

    def return_tokens(self, src, dst, size):
        land = block(dst, At.head, size)
        for k in (0, 1, 3, 2):
            for c in (0, 1):
                for d, cond in ((0, home), (1, away)):
                    shift = Shift(z=k, c=c, d=d)
                    if not (k or c or d):
                        self.add(None, block(src, At.slot, size), land, cond)
                    else:
                        self.add(shift, block(src, lambda at, s=shift: s.to(at).slot(), size), land, cond)

    def group_shifts(self):
        return [Shift(d=d, z=z) for z in (1, 3, 0, 2) for d in (0, 1) if d or z]

    def chip_shifts(self):
        return [Shift(x=x, y=y) for x in (1, 3, 2, 0) for y in (0, 1) if x or y]

    def weights(self, src, dst, rows, width, start):
        half = rows // 2

        def cut(at, to):
            return lambda io: io[src].at[
                pl.ds(pl.multiple_of(at.c * half, half), half),
                pl.ds(pl.multiple_of(to.head() * width, width), width),
            ]

        def land(io, at):
            first = pl.multiple_of(at.head() * rows + at.c * half, half)
            return io[dst].at[pl.ds(first, half), pl.ds(start, width)]

        got = []
        for shift in self.group_shifts():
            got.append(
                (shift, self.add(shift, lambda io, at, s=shift: cut(at, s.to(at))(io), land))
            )
        self.add(
            None,
            lambda io, at: io[src].at[:, pl.ds(pl.multiple_of(at.head() * width, width), width)],
            lambda io, at: io[dst].at[pl.ds(pl.multiple_of(at.head() * rows, rows), rows), pl.ds(start, width)],
        )

        def relays():
            for shift, need in got:
                piece = lambda io, at, s=shift: land(io, s.back(at))
                self.add(Shift(c=1), piece, piece, needs=[need])

        return relays

    def gather_group(self, src, dst, size):
        for shift in self.group_shifts():
            self.add(shift, full(src), block(dst, At.head, size))
        self.add(None, full(src), block(dst, At.head, size))

    def gather_context(self, src, dst, size):
        land = block(dst, lambda at: at.chip() * 2 + at.c, size)
        for shift in self.chip_shifts():
            for c in (0, 1):
                self.add(Shift(shift.by[0], shift.by[1], c), full(src), land)
        self.add(Shift(c=1), full(src), land)
        self.add(None, full(src), land)

    def scatter_group(self, src, dst):
        ids = []
        for shift in self.group_shifts():
            ids.append(
                self.add(
                    shift,
                    lambda io, at, s=shift: src(io, s.to(at).head()),
                    lambda io, at: dst(io, at.head()),
                )
            )
        ids.append(
            self.add(None, lambda io, at: src(io, at.head()), lambda io, at: dst(io, at.head()))
        )
        return ids

    def scatter_chips(self, src, dst):
        for shift in self.chip_shifts():
            self.add(
                shift,
                lambda io, at, s=shift: src(io, s.to(at).chip()),
                lambda io, at: dst(io, at.chip()),
            )
        self.add(None, lambda io, at: src(io, at.chip()), lambda io, at: dst(io, at.chip()))

    def gather_chips(self, src, land, whole, needs=()):
        at_own = lambda io, at: land(io, at.chip(), at.c)
        ids = [self.add(None, src, at_own, needs=needs)]
        side = self.add(Shift(y=1), src, at_own, needs=needs)
        ids.append(side)
        for x in (1, 3, 2):
            ids.append(self.add(Shift(x=x), src, at_own, needs=needs))

        def relays():
            other = lambda io, at: land(io, at.but(y=1 - at.y).chip(), at.c)
            for x in (1, 3, 2):
                ids.append(self.add(Shift(x=x), other, other, needs=[side]))

        def share():
            mine = lambda io, at: whole(io, at.c)
            self.add(Shift(c=1), mine, mine, needs=list(ids))

        return relays, share


NT = (((1,), (1,)), ((), ()))
NN = (((1,), (0,)), ((), ()))


def mm(a, b, dims=NN):
    return lax.dot_general(a, b, dims, preferred_element_type=F32)


def stacked(ref):
    return jnp.concatenate([ref[:, :HEAD], ref[:, HEAD:]], axis=0)


def forward_kernel(order, own, q_ref, kv_ref, o_ref, l_ref, keys, vals, acc):
    step = pl.program_id(0)
    n_runs = order.shape[0]

    @pl.when(step == 0)
    def _():
        def place(r, _):
            src = pl.ds(pl.multiple_of(r // 8 * KV_ROWS + r % 8 * RUN, 16), RUN)
            dst = pl.ds(pl.multiple_of(order[r] * RUN, RUN), RUN)
            keys[dst, :] = kv_ref[src, :HEAD]
            vals[dst, :HEAD] = kv_ref[src, HEAD:]
            vals[dst, HEAD:] = jnp.ones((RUN, HEAD), BF)
            return 0

        lax.fori_loop(0, n_runs, place, 0, unroll=8)

    run = own[step]
    query = stacked(q_ref)
    acc[...] = jnp.zeros_like(acc)

    def visit(j, masked):
        at = pl.ds(pl.multiple_of(j * CHUNK, CHUNK), CHUNK)
        s = mm(query, keys[at, :], NT)
        p = jnp.exp2(s * (SCALE * LOG2E))
        if masked:
            row = lax.broadcasted_iota(jnp.int32, p.shape, 0) % RUN + run * RUN
            col = lax.broadcasted_iota(jnp.int32, p.shape, 1) + j * CHUNK
            p = jnp.where(col <= row, p, 0.0)
        acc[...] += mm(p.astype(BF), vals[at, :])

    last = run // (CHUNK // RUN)

    def plain(j, _):
        for u in range(UNROLL):
            visit(j * UNROLL + u, False)
        return 0

    def single(j, _):
        visit(j, False)
        return 0

    lax.fori_loop(0, last // UNROLL, plain, 0)
    lax.fori_loop(last // UNROLL * UNROLL, last, single, 0)
    visit(last, True)
    total = acc[:, HEAD:]
    out = acc[:, :HEAD] / total
    log = jnp.log2(total)
    o_ref[:, :HEAD] = out[:RUN]
    o_ref[:, HEAD:] = out[RUN:]
    l_ref[:, :HEAD] = log[:RUN]
    l_ref[:, HEAD:] = log[RUN:]


def attention_forward(order, own, q, kv):
    length = order.shape[0] * RUN
    tokens = q.shape[0]
    block = pl.BlockSpec((RUN, 2 * HEAD), lambda i, *_: (i, 0))
    return pl.pallas_call(
        forward_kernel,
        grid_spec=pltpu.PrefetchScalarGridSpec(
            num_scalar_prefetch=2,
            grid=(tokens // RUN,),
            in_specs=[block, pl.BlockSpec(kv.shape, lambda i, *_: (0, 0))],
            out_specs=[block, block],
            scratch_shapes=[
                pltpu.VMEM((length, HEAD), BF),
                pltpu.VMEM((length, 2 * HEAD), BF),
                pltpu.VMEM((2 * RUN, 2 * HEAD), F32),
            ],
        ),
        out_shape=(jax.ShapeDtypeStruct(q.shape, F32), jax.ShapeDtypeStruct(q.shape, F32)),
        compiler_params=pltpu.CompilerParams(
            dimension_semantics=("arbitrary",), vmem_limit_bytes=VMEM
        ),
        name="attention_forward",
    )(order, own, q, kv)


def attention_backward(order, own, q, g, o, log, kv):
    tokens = q.shape[0]
    runs = tokens // RUN
    half = tokens // 2
    chips = order.shape[0] // runs

    def body(me, more, outs, made, scratch):
        order_ref, own_ref, q_ref, g_ref, o_ref, l_ref, kv_ref = more
        (landed,) = outs[:1]
        (dq_ref,) = made
        q2, g2, q_t, g_t, rows, dq_t, dk, dv, keys_t, send, send_sem, recv_sem, own_sem = scratch
        mine = me.chip()

        def prepare(i, _):
            at = pl.ds(pl.multiple_of(i * RUN, RUN), RUN)
            cut = pl.ds(pl.multiple_of(i % 2 * 2 * RUN, 2 * RUN), 2 * RUN)
            query, grad = stacked(q_ref.at[at]), stacked(g_ref.at[at])
            j = i // 2
            q2[j, cut, :] = query
            g2[j, cut, :] = grad
            q_t[j, :, cut] = query.T
            g_t[j, :, cut] = grad.T
            rows[j, 0:1, cut] = jnp.sum((grad.astype(F32) * stacked(o_ref.at[at])).T, axis=0, keepdims=True)
            rows[j, 1:2, cut] = stacked(l_ref.at[at]).T[:1]
            return 0

        lax.fori_loop(0, runs, prepare, 0)
        dq_t[...] = jnp.zeros_like(dq_t)

        def per_run(j, value):
            return jnp.concatenate(
                [jnp.broadcast_to(value(own_ref[j * 2 + u]), (1, 2 * RUN)) for u in (0, 1)], axis=1
            )

        def remote(step, chip, slot):
            return pltpu.make_async_remote_copy(
                src_ref=send.at[step],
                dst_ref=landed.at[slot],
                send_sem=send_sem.at[step],
                recv_sem=recv_sem.at[slot],
                device_id=(chip * 2 + me.c, me.d, me.z),
                device_id_type=MESH,
            )

        def one_chip(step, chip, diagonal):
            base = chip * KV_ROWS
            for r in range(runs):
                cut = slice(r * RUN, (r + 1) * RUN)
                keys_t[:, cut] = kv_ref[pl.ds(pl.multiple_of(base + r * RUN, 16), RUN), :HEAD].T
            dk[...] = jnp.zeros_like(dk)
            dv[...] = jnp.zeros_like(dv)

            def visit(j, part):
                at = pl.ds(pl.multiple_of(base + part * half, 16), half)
                cut = slice(part * half, (part + 1) * half)
                s = mm(kv_ref[at, :HEAD], q_t[j]) * (SCALE * LOG2E)
                log = rows[j, 1:2, :]
                pieces = []
                for r in range(runs // 2):
                    run = order_ref[chip * runs + part * (runs // 2) + r]
                    piece = s[r * RUN : (r + 1) * RUN]
                    if diagonal:
                        ahead = lax.broadcasted_iota(jnp.int32, piece.shape, 0) - (
                            lax.broadcasted_iota(jnp.int32, piece.shape, 1) % RUN
                        )
                        seen = ahead <= per_run(j, lambda mine: (mine - run) * RUN)
                        pieces.append(jnp.where(seen, jnp.exp2(piece - log), 0.0))
                    else:
                        hide = per_run(j, lambda mine: jnp.where(run <= mine, 0.0, 1e30))
                        pieces.append(jnp.exp2(piece - (log + hide)))
                p = jnp.concatenate(pieces, axis=0)
                dp = mm(kv_ref[at, HEAD:], g_t[j])
                ds = (p * (dp - rows[j, 0:1, :])).astype(BF)
                dv[cut, :] += mm(p.astype(BF), g2[j])
                dk[cut, :] += mm(ds, q2[j])
                dq_t[j] += mm(keys_t[:, cut], ds)

            def two_runs(j, _):
                visit(j, 0)
                visit(j, 1)
                return 0

            lax.fori_loop(0, runs // 2, two_runs, 0)
            send[step, :, :HEAD] = (dk[...] * SCALE).astype(BF)
            send[step, :, HEAD:] = dv[...].astype(BF)

        def other_chip(step, _):
            chip = (mine + 1 + step) % chips
            one_chip(step, chip, False)
            remote(step, chip, mine).start()
            return 0

        lax.fori_loop(0, chips - 1, other_chip, 0)
        one_chip(chips - 1, mine, True)
        keep = pltpu.make_async_copy(send.at[chips - 1], landed.at[mine], own_sem)
        keep.start()

        def give(i, _):
            at = pl.ds(pl.multiple_of(i * RUN, RUN), RUN)
            cut = pl.ds(pl.multiple_of(i % 2 * 2 * RUN, 2 * RUN), 2 * RUN)
            out = dq_t[i // 2, :, cut].T * SCALE
            dq_ref[at, :HEAD] = out[:RUN]
            dq_ref[at, HEAD:] = out[RUN:]
            return 0

        lax.fori_loop(0, runs, give, 0)
        keep.wait()
        for step in range(chips - 1):
            remote(step, (mine + 1 + step) % chips, mine).wait_send()
            remote(step, (mine + 1 + step) % chips, (mine + 1 + step) % chips).wait_recv()

    smem, vmem = pltpu.SMEM, pltpu.VMEM
    return Work(
        inputs=[(order, smem), (own, smem), (q, vmem), (g, vmem), (o, vmem), (log, vmem), (kv, vmem)],
        outs=[(q.shape, F32)],
        scratch=[
            pltpu.VMEM((runs // 2, 4 * RUN, HEAD), BF),
            pltpu.VMEM((runs // 2, 4 * RUN, HEAD), BF),
            pltpu.VMEM((runs // 2, HEAD, 4 * RUN), BF),
            pltpu.VMEM((runs // 2, HEAD, 4 * RUN), BF),
            pltpu.VMEM((runs // 2, 8, 4 * RUN), F32),
            pltpu.VMEM((runs // 2, HEAD, 4 * RUN), F32),
            pltpu.VMEM((tokens, HEAD), F32),
            pltpu.VMEM((tokens, HEAD), F32),
            pltpu.VMEM((HEAD, tokens), BF),
            pltpu.VMEM((chips, tokens, 2 * HEAD), BF),
            pltpu.SemaphoreType.DMA((chips,)),
            pltpu.SemaphoreType.DMA((chips,)),
            pltpu.SemaphoreType.DMA(()),
        ],
        greets=Plan().chip_shifts(),
        body=body,
    )


def inverse_rms(value):
    return lax.rsqrt(jnp.mean(value * value, axis=-1, keepdims=True) + EPS)


def norm_back(value, inverse, gain, grad):
    scaled = grad * gain
    inner = jnp.sum(scaled * value, axis=-1, keepdims=True)
    return inverse * scaled - value * inverse * inverse * inverse * inner / value.shape[-1]


def finish_kernel(
    gate_ref, up_ref, down_ref, out_ref, query_ref, pair_ref, parts_ref, grad_ref, x_ref, scale_ref,
    middle_ref, last_ref,
    layer_o, input_o, query_o, key_o, value_o, out_o, gate_o, up_o, down_o,
):
    for source, target in (
        (gate_ref, gate_o), (up_ref, up_o), (down_ref, down_o), (out_ref, out_o), (query_ref, query_o)
    ):
        target[...] = source[...].astype(F32)
    for i in range(8):
        to = slice(i * HEAD, (i + 1) * HEAD)
        key_o[:, to] = pair_ref[:, 2 * i * HEAD : (2 * i + 1) * HEAD].astype(F32)
        value_o[:, to] = pair_ref[:, (2 * i + 1) * HEAD : (2 * i + 2) * HEAD].astype(F32)
    x = x_ref[...].astype(F32)
    grad = jnp.sum(parts_ref[...].astype(F32), axis=0)
    input_o[...] = grad_ref[...] + norm_back(x, inverse_rms(x), scale_ref[...], grad)
    last = jnp.sum(last_ref[...].astype(F32), axis=0)
    layer_o[...] = (middle_ref[...] + last).astype(BF)


def finish(gate_up, down, out, qkv, parts, grad, x, scale, middle, last):
    steps = 4
    tokens, width = x.shape

    def rows_of(a, n, offset=0):
        return pl.BlockSpec((n // steps, a.shape[-1]), lambda i: (i + offset, 0))

    def deep(a):
        return pl.BlockSpec((a.shape[0], tokens // steps, width), lambda i: (0, i, 0))

    part = qkv.shape[0] // 2
    specs = [
        rows_of(gate_up, part), rows_of(gate_up, part, steps), rows_of(down, down.shape[0]),
        rows_of(out, out.shape[0]), rows_of(qkv, part), rows_of(qkv, part, steps), deep(parts),
        rows_of(grad, tokens), rows_of(x, tokens), pl.BlockSpec(scale.shape, lambda i: (0, 0)),
        rows_of(middle, tokens), deep(last),
    ]
    shapes = [
        ((tokens, width), BF), ((tokens, width), F32), ((part, 2 * width), F32), ((part, width), F32),
        ((part, width), F32), (out.shape, F32), ((part, gate_up.shape[1]), F32),
        ((part, gate_up.shape[1]), F32), (down.shape, F32),
    ]
    return pl.pallas_call(
        finish_kernel,
        grid=(steps,),
        in_specs=specs,
        out_specs=[pl.BlockSpec((s[0] // steps, s[1]), lambda i: (i, 0)) for s, _ in shapes],
        out_shape=tuple(jax.ShapeDtypeStruct(s, d) for s, d in shapes),
        compiler_params=pltpu.CompilerParams(
            dimension_semantics=("arbitrary",), vmem_limit_bytes=VMEM
        ),
        name="finish",
    )(gate_up, gate_up, down, out, qkv, qkv, parts, grad, x, scale, middle, last)


def dot(a, b):
    return jnp.dot(a, b, preferred_element_type=F32)


def dot_t(a, b):
    return lax.dot_general(a, b, (((0,), (0,)), ((), ())), preferred_element_type=F32)


def summed(parts, count):
    return jnp.sum(parts.reshape((count, -1) + parts.shape[1:]).astype(F32), axis=0)


def row_of(vector):
    return jnp.pad(vector.reshape(1, -1), ((0, 0), (0, 128 - vector.shape[-1])))


def project_kernel(x_ref, w_ref, scale_ref, head_ref, cos_ref, sin_ref, tag_ref, n_ref, p_ref, q_ref, kv_ref):
    step = pl.program_id(0)
    x = x_ref[0, :RUN, :].astype(F32)
    low = (x * inverse_rms(x) * scale_ref[...]).astype(BF)
    n_ref[...] = low
    out = mm(low, w_ref[...])
    p_ref[...] = out[:, : 3 * HEAD]
    turned = []
    for h in range(3):
        v = out[:, h * HEAD : (h + 1) * HEAD]
        v = v * inverse_rms(v) * head_ref[h : h + 1, :]
        turned.append((v * cos_ref[...] + pltpu.roll(v, HEAD // 2, 1) * sin_ref[...]).astype(BF))
    q_ref[:, :HEAD] = turned[0]
    q_ref[:, HEAD:] = turned[1]
    at = pl.ds(pl.multiple_of(step * RUN, RUN), RUN)
    kv_ref[at, :HEAD] = turned[2]
    kv_ref[at, HEAD:] = out[:, 3 * HEAD :].astype(BF)

    @pl.when(step == 0)
    def _():
        kv_ref[pl.ds(8 * RUN, TAG), :] = tag_ref[...]


def project(x, w, scale, head_scale, cos, sin, tag):
    width = x.shape[-1]
    group = 8 * RUN

    def fixed(a):
        return pl.BlockSpec(a.shape, lambda i: (0,) * a.ndim)

    def moving(n):
        return pl.BlockSpec((RUN, n), lambda i: (i, 0))

    return pl.pallas_call(
        project_kernel,
        grid=(8,),
        in_specs=[
            pl.BlockSpec((1, X_ROWS, width), lambda i: (i, 0, 0)),
            fixed(w), fixed(scale), fixed(head_scale), moving(HEAD), moving(HEAD), fixed(tag),
        ],
        out_specs=[
            moving(width), moving(3 * HEAD), moving(2 * HEAD),
            pl.BlockSpec((KV_ROWS, 2 * HEAD), lambda i: (0, 0)),
        ],
        out_shape=(
            jax.ShapeDtypeStruct((group, width), BF),
            jax.ShapeDtypeStruct((group, 3 * HEAD), F32),
            jax.ShapeDtypeStruct((group, 2 * HEAD), BF),
            jax.ShapeDtypeStruct((KV_ROWS, 2 * HEAD), BF),
        ),
        compiler_params=pltpu.CompilerParams(
            dimension_semantics=("arbitrary",), vmem_limit_bytes=VMEM
        ),
        name="project",
    )(x, w, scale, head_scale, cos, sin, tag)


def unproject_kernel(
    kv_ref, t_ref, p_ref, x_ref, w_ref, head_ref, cos_ref, sin_ref, mlp_ref,
    g_ref, n_ref, tile_ref, attn_acc, head_acc,
):
    step = pl.program_id(0)

    @pl.when(step == 0)
    def _():
        attn_acc[...] = jnp.zeros_like(attn_acc)
        head_acc[...] = jnp.zeros_like(head_acc)

    kv = kv_ref[0].astype(F32)
    for chip in range(1, 8):
        kv = kv + kv_ref[chip].astype(F32)
    for h in range(3):
        turn = kv[:, :HEAD] if h == 2 else t_ref[:, h * HEAD : (h + 1) * HEAD]
        grad = turn * cos_ref[...] - pltpu.roll(turn, HEAD // 2, 1) * sin_ref[...]
        v = p_ref[:, h * HEAD : (h + 1) * HEAD]
        inverse = inverse_rms(v)
        back = norm_back(v, inverse, head_ref[h : h + 1, :], grad)
        g_ref[:, h * HEAD : (h + 1) * HEAD] = back.astype(BF)
        head_acc[h // 2 : h // 2 + 1, :] += jnp.sum(grad * v * inverse, axis=0, keepdims=True)
    g_ref[:, 3 * HEAD :] = kv[:, HEAD:].astype(BF)
    wide = mm(g_ref[...], w_ref[...], NT)
    n_ref[...] = wide.astype(BF)
    x = x_ref[0, :RUN, :].astype(F32)
    attn_acc[...] += jnp.sum(wide * x * inverse_rms(x), axis=0, keepdims=True)

    @pl.when(step == pl.num_programs(0) - 1)
    def _():
        tile_ref[...] = jnp.zeros_like(tile_ref)
        for j in range(8):
            tile_ref[j * 8 : j * 8 + 1, :] = attn_acc[:, j * 128 : (j + 1) * 128]
            tile_ref[j * 8 + 1 : j * 8 + 2, :] = mlp_ref[:, j * 128 : (j + 1) * 128]
            tile_ref[j * 8 + 2 : j * 8 + 4, :] = head_acc[...]


def unproject(kv_parts, turn, pre, x, w, head_scale, cos, sin, mlp_part):
    width = x.shape[-1]
    group = 8 * RUN

    def fixed(a):
        return pl.BlockSpec(a.shape, lambda i: (0,) * a.ndim)

    def moving(n):
        return pl.BlockSpec((RUN, n), lambda i: (i, 0))

    return pl.pallas_call(
        unproject_kernel,
        grid=(8,),
        in_specs=[
            pl.BlockSpec((8, RUN, 2 * HEAD), lambda i: (0, i, 0)),
            moving(2 * HEAD), moving(3 * HEAD),
            pl.BlockSpec((1, X_ROWS, width), lambda i: (i, 0, 0)),
            fixed(w), fixed(head_scale), moving(HEAD), moving(HEAD), fixed(mlp_part),
        ],
        out_specs=[moving(4 * HEAD), moving(width), pl.BlockSpec((64, 128), lambda i: (0, 0))],
        out_shape=(
            jax.ShapeDtypeStruct((group, 4 * HEAD), BF),
            jax.ShapeDtypeStruct((group, width), BF),
            jax.ShapeDtypeStruct((64, 128), F32),
        ),
        scratch_shapes=[pltpu.VMEM((1, width), F32), pltpu.VMEM((2, HEAD), F32)],
        compiler_params=pltpu.CompilerParams(
            dimension_semantics=("arbitrary",), vmem_limit_bytes=VMEM
        ),
        name="unproject",
    )(kv_parts, turn, pre, x, w, head_scale, cos, sin, mlp_part)


def local(
    hidden_in, positions, attn_gain, query_weight, key_matrix, value_matrix, output_weight,
    query_norm_gain, key_gain, mlp_gain, gate_weight, up_weight, down_weight, cotangent,
):
    hidden = hidden_in[0]
    cot = cotangent[0]
    tokens, width = hidden.shape
    group = 8 * tokens
    ff = gate_weight.shape[1] // 8
    part = width // 8
    core = lax.axis_index("ctx") % 2
    def rows(size):
        return lambda ref: (lambda io, n: io[ref].at[pl.ds(pl.multiple_of(n * size, size), size)])

    gain_tile = jnp.concatenate(
        [row_of(g.astype(F32)) for g in (attn_gain, mlp_gain, query_norm_gain, key_gain)]
        + [jnp.zeros((4, 128), F32)],
        axis=0,
    )
    own_run = (positions[:, :1] // RUN).astype(BF)
    tagged = jnp.concatenate([hidden, jnp.broadcast_to(own_run, (TAG, width))], axis=0)
    plan = Plan()
    relays = [plan.gather_tokens(0, 5, X_ROWS)]
    plan.gather_group(1, 6, 8)
    relays += [
        plan.weights(2, 7, part, 256, 0),
        plan.weights(3, 7, part, 128, 256),
        plan.weights(4, 7, part, 128, 384),
    ]
    for relay in relays:
        relay()
    x_all, gains, w_qkv = exchange(
        plan, 1, (((8 * X_ROWS, width), BF), ((64, 128), F32), ((width, 512), BF)),
        tagged, gain_tile, query_weight, key_matrix, value_matrix,
    )
    gains = gains.reshape(8, 8, 128)
    attn_scale = gains[:, 0].reshape(1, width)
    mlp_scale = gains[:, 1].reshape(1, width)
    query_scale = gains[:, 2, :16].reshape(1, HEAD)
    key_scale = gains[:, 3, :16].reshape(1, HEAD)
    x_all = x_all.reshape(8, X_ROWS, width)
    own_bf = x_all[:, RUN, 0]
    own = own_bf.astype(jnp.int32)
    head_scale = jnp.concatenate([query_scale, query_scale, key_scale], axis=0)
    place_rows = (own[:, None] * RUN + jnp.arange(RUN, dtype=jnp.int32)[None, :]).reshape(group)
    frequency = 1.0 / THETA ** (jnp.arange(0, HEAD, 2, dtype=F32) / HEAD)
    angle = place_rows.astype(F32)[:, None] * jnp.tile(frequency, 2)[None, :]
    sign = jnp.where(jnp.arange(HEAD) < HEAD // 2, -1.0, 1.0).astype(F32)
    cos, sin = jnp.cos(angle), jnp.sin(angle) * sign[None, :]
    tag = jnp.pad(jnp.broadcast_to(own_bf[None, :], (TAG, 8)), ((0, 0), (0, 2 * HEAD - 8)))
    norm_one, pre, queries, kv = project(x_all, w_qkv, attn_scale, head_scale, cos, sin, tag)

    plan = Plan()
    own_kv = block(4, At.chip, KV_ROWS)
    side_kv = block(4, lambda at: at.but(y=1 - at.y).chip(), KV_ROWS)
    half = group // 2

    def upper(io, at):
        return io[4].at[pl.ds(pl.multiple_of(at.chip() * KV_ROWS, 16), half)]

    def lower(io, at):
        return io[4].at[pl.ds(pl.multiple_of(at.chip() * KV_ROWS + half, 16), KV_ROWS - half)]

    def left(of, flip):
        return lambda io, at: of(io, at.but(x=(at.x + 3) % 4, y=1 - at.y if flip else at.y))

    def right(of, flip):
        return lambda io, at: of(io, at.but(x=(at.x + 1) % 4, y=1 - at.y if flip else at.y))

    side = plan.add(Shift(y=1), full(0), own_kv)
    right_id = plan.add(Shift(x=1), full(0), own_kv)
    left_id = plan.add(Shift(x=-1), full(0), own_kv)
    plan.add(None, full(0), own_kv)
    relay_tokens = plan.gather_tokens(1, 5, tokens)
    relays = [plan.weights(2, 6, part, ff, 0), plan.weights(3, 6, part, ff, ff)]
    side_right = plan.add(Shift(x=1), side_kv, side_kv, needs=[side])
    side_left = plan.add(Shift(x=-1), side_kv, side_kv, needs=[side])
    plan.add(Shift(x=1), left(upper, 0), left(upper, 0), needs=[right_id])
    plan.add(Shift(x=-1), right(lower, 0), right(lower, 0), needs=[left_id])
    relay_tokens()
    plan.add(Shift(x=1), left(upper, 1), left(upper, 1), needs=[side_right])
    plan.add(Shift(x=-1), right(lower, 1), right(lower, 1), needs=[side_left])
    for relay in relays:
        relay()
    kv_all, cot_all, w_gu = exchange(
        plan, 2, (((8 * KV_ROWS, 256), BF), ((group, width), BF), ((width, 2 * ff), BF)),
        kv, cot, gate_weight, up_weight,
    )
    order = kv_all.reshape(8, KV_ROWS, 256)[:, 8 * RUN, :8].reshape(64).astype(jnp.int32)
    attention, log_total = attention_forward(order, own, queries, kv_all)
    mixed = attention.astype(BF)
    branch_part = dot(mixed, output_weight).astype(BF)

    plan = Plan()
    plan.return_tokens(0, 1, tokens)
    (branch,) = exchange(plan, 3, (((group, width), BF),), branch_part)
    residual = hidden.astype(F32)
    middle = residual + summed(branch, 8)
    mlp_inverse = inverse_rms(middle)
    norm_two_own = (middle * mlp_inverse * mlp_scale).astype(BF)
    plan = Plan()
    plan.gather_tokens(0, 1, tokens)()
    (norm_two,) = exchange(plan, 4, (((group, width), BF),), norm_two_own)

    gate_up = dot(norm_two, w_gu)
    gate, up = gate_up[:, :ff], gate_up[:, ff:]
    sigma = jax.nn.sigmoid(gate)
    swish = gate * sigma
    inner = (swish * up).astype(BF)
    inner_grad = lax.dot_general(cot_all, down_weight, NT, preferred_element_type=F32)
    gate_up_grad = jnp.concatenate(
        [
            (inner_grad * up * sigma * (1.0 + gate * (1.0 - sigma))).astype(BF),
            (inner_grad * swish).astype(BF),
        ],
        axis=1,
    )
    norm_two_part = lax.dot_general(gate_up_grad, w_gu, NT, preferred_element_type=F32).astype(BF)
    gate_up_wgrad = dot_t(norm_two, gate_up_grad).astype(BF).reshape(8, part, 2 * ff)
    down_wgrad = dot_t(inner, cot_all).astype(BF)

    def theirs(ref, size):
        def pick(io, at):
            cut = pl.ds(pl.multiple_of((1 - at.c) * size, size), size)
            return io[ref].at[..., cut]

        return pick

    def my_half(both, got):
        size = got.shape[-1]
        mine = lax.dynamic_slice_in_dim(both, core * size, size, axis=both.ndim - 1)
        return (mine.astype(F32) + got.astype(F32)).astype(BF)

    plan = Plan()
    plan.return_tokens(0, 3, tokens)
    plan.add(Shift(c=1), theirs(1, ff), full(4))
    plan.add(Shift(c=1), theirs(2, width // 2), full(5))
    norm_two_parts, gate_up_got, down_got = exchange(
        plan, 5, (((group, width), BF), ((8, part, ff), BF), ((ff, width // 2), BF)),
        norm_two_part, gate_up_wgrad, down_wgrad,
    )
    norm_two_grad = summed(norm_two_parts, 8)
    middle_grad = cot.astype(F32) + norm_back(middle, mlp_inverse, mlp_scale, norm_two_grad)
    mlp_gain_part = jnp.sum(norm_two_grad * middle * mlp_inverse, axis=0)
    branch_grad_own = middle_grad.astype(BF)
    gate_up_half = my_half(gate_up_wgrad, gate_up_got)
    down_half = my_half(down_wgrad, down_got)

    plan = Plan()
    plan.gather_tokens(0, 3, tokens)()
    plan.scatter_chips(
        lambda io, n: io[1].at[:, pl.ds(pl.multiple_of(n * 16, 16), 16)], lambda io, n: io[4].at[n]
    )
    plan.scatter_chips(rows(ff // 8)(2), lambda io, n: io[5].at[n])
    branch_grad, gate_up_pieces, down_pieces = exchange(
        plan, 6, (((group, width), BF), ((8, 8, 16, ff), BF), ((8, ff // 8, width // 2), BF)),
        branch_grad_own, gate_up_half, down_half,
    )
    mixed_grad = lax.dot_general(branch_grad, output_weight, NT, preferred_element_type=F32).astype(BF)
    output_wgrad = dot_t(mixed, branch_grad).astype(BF)
    down_part = dot(inner, down_weight).astype(BF)
    gate_up_sum = jnp.sum(gate_up_pieces.astype(F32), axis=0).astype(BF)
    down_sum = jnp.sum(down_pieces.astype(F32), axis=0).astype(BF)

    plan = Plan()
    pair = 2 * tokens
    for k in (1, 3, 2):
        plan.add(
            Shift(z=k),
            block(0, lambda at, k=k: (at.z + k) % 4, pair),
            block(4, lambda at: at.z, pair),
        )
    plan.add(None, block(0, lambda at: at.z, pair), block(4, lambda at: at.z, pair))
    plan.add(Shift(c=1), theirs(1, width // 2), full(5))
    plan.scatter_group(
        lambda io, n: io[2].at[n],
        lambda io, n: io[6].at[:, pl.ds(pl.multiple_of(n * ff, ff), ff)],
    )
    n_rows = output_wgrad.shape[0]
    kv_parts, down_parts, output_got, gate_up_own, query_turn = exchange(
        plan, 7,
        (
            ((8, group, 256), BF), ((group, width), BF), ((n_rows, width // 2), BF),
            ((16, 8 * ff), BF),
        ),
        down_part, output_wgrad, gate_up_sum,
        work=attention_backward(order, own, queries, mixed_grad, attention, log_total, kv_all),
    )
    down_pair = summed(down_parts, 4).astype(BF)
    output_half = my_half(output_wgrad, output_got)
    qkv_grad, norm_one_part, gain_parts = unproject(
        kv_parts, query_turn, pre, x_all, w_qkv, head_scale, cos, sin,
        mlp_gain_part.reshape(1, width),
    )
    qkv_wgrad = dot_t(norm_one, qkv_grad).astype(BF).reshape(8, part, 512)

    plan = Plan()
    plan.return_tokens(0, 4, tokens)

    def wgrad_piece(io, chip, c):
        return io[1].at[
            :, pl.ds(pl.multiple_of(chip * 16, 16), 16), pl.ds(pl.multiple_of(c * 256, 256), 256)
        ]

    for shift in [Shift(c=1)] + [
        Shift(s.by[0], s.by[1], c) for s in plan.chip_shifts() for c in (0, 1)
    ]:
        plan.add(
            shift,
            lambda io, at, s=shift: wgrad_piece(io, s.to(at).chip(), s.to(at).c),
            lambda io, at: io[5].at[at.chip() * 2 + at.c],
        )
    plan.add(
        None,
        lambda io, at: wgrad_piece(io, at.chip(), at.c),
        lambda io, at: io[5].at[at.chip() * 2 + at.c],
    )
    plan.scatter_chips(rows(n_rows // 8)(2), lambda io, n: io[6].at[n])
    plan.scatter_group(rows(8)(3), rows(8)(7))

    def stacked_rows(ref, size, total):
        def land(io, chip, c):
            return io[ref].at[pl.ds(pl.multiple_of(c * total + chip * size, size), size)]

        return land, lambda io, c: io[ref].at[pl.ds(pl.multiple_of(c * total, total), total)]

    def side_columns(ref, size):
        def at_core(c):
            return pl.ds(pl.multiple_of(c * (width // 2), width // 2), width // 2)

        def land(io, chip, c):
            return io[ref].at[pl.ds(pl.multiple_of(chip * size, size), size), at_core(c)]

        return land, lambda io, c: io[ref].at[:, at_core(c)]

    norm_one_parts, qkv_pieces, output_pieces, gain_sums = exchange(
        plan, 8,
        (
            ((group, width), BF), ((16, 8, 16, 256), BF), ((8, n_rows // 8, width // 2), BF),
            ((64, 128), F32),
        ),
        norm_one_part, qkv_wgrad, output_half, gain_parts,
    )
    qkv_sum = jnp.sum(qkv_pieces.astype(F32), axis=0).astype(BF)
    output_sum = jnp.sum(output_pieces.astype(F32), axis=0).astype(BF)
    gain_sum = summed(gain_sums, 8)

    plan = Plan()
    to_group = plan.scatter_group(
        lambda io, n: io[0].at[n],
        lambda io, n: io[6].at[:, pl.ds(pl.multiple_of(n * 256, 256), 256)],
    )
    later = [
        plan.gather_chips(full(4), *stacked_rows(11, 16, part)),
        plan.gather_chips(full(5), *side_columns(12, ff // 8)),
        plan.gather_chips(full(1), *side_columns(8, n_rows // 8)),
    ]
    plan.gather_context(2, 9, 8)
    own_block = block(3, lambda at: at.c, tokens)
    other_block = block(3, lambda at: 1 - at.c, tokens)

    def landed(n):
        return lambda io, at: io[10].at[pl.ds(n * tokens, tokens)]

    plan.add(Shift(d=1), own_block, landed(1), away)
    plan.add(Shift(d=1, c=1), other_block, landed(1), away)
    plan.add(None, own_block, landed(0), home)
    plan.add(Shift(c=1), other_block, landed(0), home)
    later.append(plan.gather_chips(full(6), *stacked_rows(7, 16, part), needs=to_group))
    for relay, _ in later:
        relay()
    for _, share in later:
        share()
    _, qkv_final, output_final, gain_all, down_last, gate_up_final, down_final = exchange(
        plan, 9,
        (
            ((16, 2048), BF), ((2 * part, 2048), BF), ((n_rows, width), BF), ((128, 128), F32),
            ((2 * tokens, width), BF), ((2 * part, 8 * ff), BF), ((ff, width), BF),
        ),
        qkv_sum, output_sum, gain_sum, down_pair, gate_up_own, down_sum,
    )
    layer_out, input_grad, query_wgrad, key_wgrad, value_wgrad, output_wgrad, gate_wgrad, up_wgrad, down_wgrad = finish(
        gate_up_final, down_final, output_final, qkv_final, norm_one_parts.reshape(8, tokens, width),
        middle_grad, hidden, attn_scale, middle, down_last.reshape(2, tokens, width),
    )
    gain_total = summed(gain_all, 16)
    head = lax.axis_index("dp") * 4 + lax.axis_index("fsdp")
    return (
        layer_out[None],
        input_grad[None],
        gain_total[0],
        query_wgrad,
        key_wgrad,
        value_wgrad,
        output_wgrad,
        lax.dynamic_slice_in_dim(gain_total[2], head * 16, 16),
        lax.dynamic_slice_in_dim(gain_total[3], head * 16, 16),
        gain_total[1],
        gate_wgrad,
        up_wgrad,
        down_wgrad,
    )


def solution(mesh):
    tokens = P("dp", ("ctx", "fsdp"), None)
    places = P("dp", ("ctx", "fsdp"))
    vector = P(("dp", "fsdp"))
    matrix = P(("dp", "fsdp"), None)
    in_specs = (
        tokens, places, vector, matrix, matrix, matrix, matrix,
        vector, vector, vector, matrix, matrix, matrix, tokens,
    )
    out_specs = (
        tokens, tokens, vector, matrix, matrix, matrix, matrix,
        vector, vector, vector, matrix, matrix, matrix,
    )
    return jax.shard_map(local, mesh=mesh, in_specs=in_specs, out_specs=out_specs, check_vma=False)
```

```python
import jax
import jax.numpy as jnp
from jax import lax
from jax.experimental import pallas as pl
from jax.experimental.pallas import tpu as pltpu
from jax.sharding import PartitionSpec as P

HEAD = 128
EPS = 1e-06
THETA = 1000000.0
SCALE = HEAD ** (-0.5)
LOG2E = 1.4426950408889634
RUN = 128
CHUNK = 512
VMEM = 60 * 2**20
UNROLL = 4
SLOTS = 2
TAG = 16
X_ROWS = RUN + TAG
KV_ROWS = 8 * RUN + TAG
BF = jnp.bfloat16
F32 = jnp.float32
MESH = pl.DeviceIdType.MESH


class At:
    def __init__(self, x, y, c, d, z):
        self.x, self.y, self.c, self.d, self.z = x, y, c, d, z

    def but(self, **new):
        return At(**{**self.__dict__, **new})

    def chip(self):
        return self.x * 2 + self.y

    def head(self):
        return self.d * 4 + self.z

    def slot(self):
        return self.z * 2 + self.c

    def device(self):
        return ((self.x * 2 + self.y) * 2 + self.c, self.d, self.z)


def here():
    ctx = lax.axis_index("ctx")
    return At(ctx // 4, ctx // 2 % 2, ctx % 2, lax.axis_index("dp"), lax.axis_index("fsdp"))


class Shift:
    def __init__(self, x=0, y=0, c=0, d=0, z=0):
        self.by = (x, y, c, d, z)

    def move(self, at, sign):
        x, y, c, d, z = self.by
        return At(
            (at.x + 4 + sign * x) % 4 if x else at.x,
            1 - at.y if y else at.y,
            1 - at.c if c else at.c,
            1 - at.d if d else at.d,
            (at.z + 4 + sign * z) % 4 if z else at.z,
        )

    def to(self, at):
        return self.move(at, 1)

    def back(self, at):
        return self.move(at, -1)

    def key(self):
        return self.by


class Op:
    def __init__(self, shift, src, dst, cond=None, needs=(), stage=0):
        self.shift, self.src, self.dst, self.cond, self.needs = shift, src, dst, cond, needs
        self.stage = stage


class Work:
    def __init__(self, inputs, outs, scratch, greets, body):
        self.inputs, self.outs, self.scratch, self.greets, self.body = inputs, outs, scratch, greets, body


def exchange(ops, collective_id, out_shapes, *arrays, work=None):
    n_in, n_out, n_ops = len(arrays), len(out_shapes), len(ops)
    work = work or Work([], [], [], [], None)
    n_more, n_made = len(work.inputs), len(work.outs)

    def kernel(*refs):
        refs = list(refs)
        ins, more = refs[:n_in], refs[n_in : n_in + n_more]
        refs = refs[n_in + n_more :]
        outs, made = refs[:n_out], refs[n_out : n_out + n_made]
        send_sem, recv_sem = refs[n_out + n_made : n_out + n_made + 2]
        scratch = refs[n_out + n_made + 2 :]
        io = ins + outs + made + scratch
        me = here()

        def when(cond, act):
            if cond is None:
                act()
            else:
                pl.when(cond)(act)

        barrier = pltpu.get_barrier_semaphore()
        seen, count = set(), 0
        for op in ops:
            if op.shift is None or (op.shift.key(), op.cond) in seen:
                continue
            seen.add((op.shift.key(), op.cond))
            source = op.shift.back(me)

            def greet(source=source):
                pl.semaphore_signal(barrier, inc=1, device_id=source.device(), device_id_type=MESH)

            when(op.cond and op.cond(source), greet)
            count = count + (1 if op.cond is None else jnp.where(op.cond(me), 1, 0))
        for shift in work.greets:
            source = shift.back(me)
            pl.semaphore_signal(barrier, inc=1, device_id=source.device(), device_id_type=MESH)
            count = count + 1
        pl.semaphore_wait(barrier, count)

        def copy(t, sender):
            op = ops[t]
            return pltpu.make_async_remote_copy(
                src_ref=op.src(io, sender),
                dst_ref=op.dst(io, sender),
                send_sem=send_sem.at[t],
                recv_sem=recv_sem.at[t],
                device_id=op.shift.to(me).device(),
                device_id_type=MESH,
            )

        local = [t for t in range(n_ops) if ops[t].shift is None]
        views = [ops[t].src(io, me) for t in local]

        def run(*buffers):
            held = dict(zip(local, buffers))

            def fetch(t):
                return pltpu.make_async_copy(ops[t].src(io, me), held[t], send_sem.at[t])

            def store(t):
                return pltpu.make_async_copy(held[t], ops[t].dst(io, me), recv_sem.at[t])

            arrived, fetched = set(), set()

            def pass_on(t):
                if t in fetched:
                    return
                fetched.add(t)

                def act():
                    fetch(t).wait()
                    store(t).start()

                when(ops[t].cond and ops[t].cond(me), act)

            def arrive(t):
                if t in arrived:
                    return
                arrived.add(t)
                op = ops[t]
                if op.shift is None:
                    pass_on(t)
                    when(op.cond and op.cond(me), lambda: store(t).wait())
                else:
                    source = op.shift.back(me)
                    when(op.cond and op.cond(source), lambda: copy(t, source).wait_recv())

            def start(t):
                if ops[t].shift is None:
                    fetch(t).start()
                else:
                    copy(t, me).start()

            def begin(stage):
                for t, op in enumerate(ops):
                    if op.stage != stage:
                        continue
                    if op.needs:
                        for early in local:
                            if early < t and ops[early].stage <= stage:
                                pass_on(early)
                    for need in op.needs:
                        arrive(need)
                    when(op.cond and op.cond(me), lambda t=t: start(t))
                for t in local:
                    if ops[t].stage == stage:
                        pass_on(t)

            begin(0)
            if work.body is not None:
                work.body(me, more, outs, made, scratch, begin, arrive)
            for t, op in enumerate(ops):
                arrive(t)
                if op.shift is not None:
                    when(op.cond and op.cond(me), lambda t=t: copy(t, me).wait_send())

        pl.run_scoped(run, *(pltpu.VMEM(v.shape, v.dtype) for v in views))

    anywhere = pl.BlockSpec(memory_space=pl.ANY)
    return pl.pallas_call(
        kernel,
        out_shape=tuple(jax.ShapeDtypeStruct(s, d) for s, d in out_shapes)
        + tuple(jax.ShapeDtypeStruct(s, d) for s, d in work.outs),
        in_specs=[anywhere] * n_in + [pl.BlockSpec(memory_space=m) for _, m in work.inputs],
        out_specs=tuple([anywhere] * n_out + [pl.BlockSpec(memory_space=pltpu.VMEM)] * n_made),
        scratch_shapes=[
            pltpu.SemaphoreType.DMA((n_ops,)),
            pltpu.SemaphoreType.DMA((n_ops,)),
        ]
        + work.scratch,
        compiler_params=pltpu.CompilerParams(
            collective_id=collective_id,
            has_side_effects=True,
            vmem_limit_bytes=VMEM if work.body else None,
        ),
        name="exchange_%d" % collective_id,
    )(*arrays, *(a for a, _ in work.inputs))


def home(at):
    return at.c == at.d


def away(at):
    return at.c != at.d


def block(index, start, size):
    return lambda io, at: io[index].at[pl.ds(pl.multiple_of(start(at) * size, size), size)]


def full(index):
    return lambda io, at: io[index]


class Plan(list):
    def add(self, *args, **named):
        self.append(Op(*args, **named))
        return len(self) - 1

    def gather_tokens(self, src, dst, size):
        mine = block(dst, At.slot, size)
        self.add(None, full(src), mine, home)
        got = {}
        for name, by in (("side", {"d": 1}), ("up", {"z": 1}), ("down", {"z": -1})):
            got[name] = [
                self.add(Shift(**by), full(src), mine, home),
                self.add(Shift(c=1, **by), full(src), mine, away),
            ]
        self.add(Shift(c=1), full(src), mine, away)

        def relays():
            both = block(dst, lambda at: at.z, 2 * size)
            below = block(dst, lambda at: (at.z + 3) % 4 * 2, size)
            above = block(dst, lambda at: (at.z + 1) % 4 * 2 + 1, size)
            up = self.add(Shift(z=1), both, both, away, got["side"])
            down = self.add(Shift(z=-1), both, both, away, got["side"])
            self.add(Shift(z=1), below, below, home, got["up"])
            self.add(Shift(z=-1), above, above, home, got["down"])
            self.add(Shift(z=1), below, below, away, [up])
            self.add(Shift(z=-1), above, above, away, [down])

        return relays

    def return_tokens(self, src, dst, size):
        land = block(dst, At.head, size)
        for k in (0, 1, 3, 2):
            for c in (0, 1):
                for d, cond in ((0, home), (1, away)):
                    shift = Shift(z=k, c=c, d=d)
                    if not (k or c or d):
                        self.add(None, block(src, At.slot, size), land, cond)
                    else:
                        self.add(shift, block(src, lambda at, s=shift: s.to(at).slot(), size), land, cond)

    def group_shifts(self):
        return [Shift(d=d, z=z) for z in (1, 3, 0, 2) for d in (0, 1) if d or z]

    def chip_shifts(self):
        return [Shift(x=x, y=y) for x in (1, 3, 2, 0) for y in (0, 1) if x or y]

    def weights(self, src, dst, rows, width, start):
        half = rows // 2

        def cut(at, to):
            return lambda io: io[src].at[
                pl.ds(pl.multiple_of(at.c * half, half), half),
                pl.ds(pl.multiple_of(to.head() * width, width), width),
            ]

        def land(io, at):
            first = pl.multiple_of(at.head() * rows + at.c * half, half)
            return io[dst].at[pl.ds(first, half), pl.ds(start, width)]

        got = []
        for shift in self.group_shifts():
            got.append(
                (shift, self.add(shift, lambda io, at, s=shift: cut(at, s.to(at))(io), land))
            )
        self.add(
            None,
            lambda io, at: io[src].at[:, pl.ds(pl.multiple_of(at.head() * width, width), width)],
            lambda io, at: io[dst].at[pl.ds(pl.multiple_of(at.head() * rows, rows), rows), pl.ds(start, width)],
        )

        def relays():
            for shift, need in got:
                piece = lambda io, at, s=shift: land(io, s.back(at))
                self.add(Shift(c=1), piece, piece, needs=[need])

        return relays

    def gather_group(self, src, dst, size):
        for shift in self.group_shifts():
            self.add(shift, full(src), block(dst, At.head, size))
        self.add(None, full(src), block(dst, At.head, size))

    def gather_context(self, src, dst, size):
        land = block(dst, lambda at: at.chip() * 2 + at.c, size)
        for shift in self.chip_shifts():
            for c in (0, 1):
                self.add(Shift(shift.by[0], shift.by[1], c), full(src), land)
        self.add(Shift(c=1), full(src), land)
        self.add(None, full(src), land)

    def scatter_group(self, src, dst):
        ids = []
        for shift in self.group_shifts():
            ids.append(
                self.add(
                    shift,
                    lambda io, at, s=shift: src(io, s.to(at).head()),
                    lambda io, at: dst(io, at.head()),
                )
            )
        ids.append(
            self.add(None, lambda io, at: src(io, at.head()), lambda io, at: dst(io, at.head()))
        )
        return ids

    def scatter_chips(self, src, dst, stage=0):
        for shift in self.chip_shifts():
            self.add(
                shift,
                lambda io, at, s=shift: src(io, s.to(at).chip()),
                lambda io, at: dst(io, at.chip()),
                stage=stage,
            )
        self.add(
            None, lambda io, at: src(io, at.chip()), lambda io, at: dst(io, at.chip()), stage=stage
        )

    def gather_chips(self, src, land, whole, needs=()):
        at_own = lambda io, at: land(io, at.chip(), at.c)
        ids = [self.add(None, src, at_own, needs=needs)]
        side = self.add(Shift(y=1), src, at_own, needs=needs)
        ids.append(side)
        for x in (1, 3, 2):
            ids.append(self.add(Shift(x=x), src, at_own, needs=needs))

        def relays():
            other = lambda io, at: land(io, at.but(y=1 - at.y).chip(), at.c)
            for x in (1, 3, 2):
                ids.append(self.add(Shift(x=x), other, other, needs=[side]))

        def share():
            mine = lambda io, at: whole(io, at.c)
            self.add(Shift(c=1), mine, mine, needs=list(ids))

        return relays, share


NT = (((1,), (1,)), ((), ()))
NN = (((1,), (0,)), ((), ()))
TN = (((0,), (0,)), ((), ()))


def mm(a, b, dims=NN):
    return lax.dot_general(a, b, dims, preferred_element_type=F32)


def stacked(ref):
    return jnp.concatenate([ref[:, :HEAD], ref[:, HEAD:]], axis=0)


def forward_kernel(order, own, q_ref, kv_ref, o_ref, l_ref, keys, vals, acc):
    step = pl.program_id(0)
    n_runs = order.shape[0]

    @pl.when(step == 0)
    def _():
        def place(r, _):
            src = pl.ds(pl.multiple_of(r // 8 * KV_ROWS + r % 8 * RUN, 16), RUN)
            dst = pl.ds(pl.multiple_of(order[r] * RUN, RUN), RUN)
            keys[dst, :] = kv_ref[src, :HEAD]
            vals[dst, :HEAD] = kv_ref[src, HEAD:]
            vals[dst, HEAD:] = jnp.ones((RUN, HEAD), BF)
            return 0

        lax.fori_loop(0, n_runs, place, 0, unroll=8)

    run = own[step]
    query = stacked(q_ref)
    acc[...] = jnp.zeros_like(acc)

    def visit(j, masked):
        at = pl.ds(pl.multiple_of(j * CHUNK, CHUNK), CHUNK)
        s = mm(query, keys[at, :], NT)
        p = jnp.exp2(s * (SCALE * LOG2E))
        if masked:
            row = lax.broadcasted_iota(jnp.int32, p.shape, 0) % RUN + run * RUN
            col = lax.broadcasted_iota(jnp.int32, p.shape, 1) + j * CHUNK
            p = jnp.where(col <= row, p, 0.0)
        acc[...] += mm(p.astype(BF), vals[at, :])

    last = run // (CHUNK // RUN)

    def plain(j, _):
        for u in range(UNROLL):
            visit(j * UNROLL + u, False)
        return 0

    def single(j, _):
        visit(j, False)
        return 0

    lax.fori_loop(0, last // UNROLL, plain, 0)
    lax.fori_loop(last // UNROLL * UNROLL, last, single, 0)
    visit(last, True)
    total = acc[:, HEAD:]
    out = acc[:, :HEAD] / total
    log = jnp.log2(total)
    o_ref[:, :HEAD] = out[:RUN]
    o_ref[:, HEAD:] = out[RUN:]
    l_ref[:, :HEAD] = log[:RUN]
    l_ref[:, HEAD:] = log[RUN:]


def attention_forward(order, own, q, kv):
    length = order.shape[0] * RUN
    tokens = q.shape[0]
    block = pl.BlockSpec((RUN, 2 * HEAD), lambda i, *_: (i, 0))
    return pl.pallas_call(
        forward_kernel,
        grid_spec=pltpu.PrefetchScalarGridSpec(
            num_scalar_prefetch=2,
            grid=(tokens // RUN,),
            in_specs=[block, pl.BlockSpec(kv.shape, lambda i, *_: (0, 0))],
            out_specs=[block, block],
            scratch_shapes=[
                pltpu.VMEM((length, HEAD), BF),
                pltpu.VMEM((length, 2 * HEAD), BF),
                pltpu.VMEM((2 * RUN, 2 * HEAD), F32),
            ],
        ),
        out_shape=(jax.ShapeDtypeStruct(q.shape, F32), jax.ShapeDtypeStruct(q.shape, F32)),
        compiler_params=pltpu.CompilerParams(
            dimension_semantics=("arbitrary",), vmem_limit_bytes=VMEM
        ),
        name="attention_forward",
    )(order, own, q, kv)


def attention_backward(order, own, q, g, o, log, kv):
    tokens = q.shape[0]
    runs = tokens // RUN
    half = tokens // 2
    chips = order.shape[0] // runs

    def body(me, more, outs, made, scratch, begin, arrive):
        order_ref, own_ref, q_ref, g_ref, o_ref, l_ref, kv_ref = more
        (landed,) = outs[:1]
        (dq_ref,) = made
        q2, g2, q_t, g_t, rows, dq_t, dk, dv, keys_t, send, send_sem, recv_sem, own_sem = scratch
        mine = me.chip()

        def prepare(i, _):
            at = pl.ds(pl.multiple_of(i * RUN, RUN), RUN)
            cut = pl.ds(pl.multiple_of(i % 2 * 2 * RUN, 2 * RUN), 2 * RUN)
            query, grad = stacked(q_ref.at[at]), stacked(g_ref.at[at])
            j = i // 2
            q2[j, cut, :] = query
            g2[j, cut, :] = grad
            q_t[j, :, cut] = query.T
            g_t[j, :, cut] = grad.T
            rows[j, 0:1, cut] = jnp.sum((grad.astype(F32) * stacked(o_ref.at[at])).T, axis=0, keepdims=True)
            rows[j, 1:2, cut] = stacked(l_ref.at[at]).T[:1]
            return 0

        lax.fori_loop(0, runs, prepare, 0)
        dq_t[...] = jnp.zeros_like(dq_t)

        def per_run(j, value):
            return jnp.concatenate(
                [jnp.broadcast_to(value(own_ref[j * 2 + u]), (1, 2 * RUN)) for u in (0, 1)], axis=1
            )

        def remote(step, chip, slot):
            return pltpu.make_async_remote_copy(
                src_ref=send.at[step],
                dst_ref=landed.at[slot],
                send_sem=send_sem.at[step],
                recv_sem=recv_sem.at[slot],
                device_id=(chip * 2 + me.c, me.d, me.z),
                device_id_type=MESH,
            )

        def one_chip(step, chip, diagonal):
            base = chip * KV_ROWS
            for r in range(runs):
                cut = slice(r * RUN, (r + 1) * RUN)
                keys_t[:, cut] = kv_ref[pl.ds(pl.multiple_of(base + r * RUN, 16), RUN), :HEAD].T
            dk[...] = jnp.zeros_like(dk)
            dv[...] = jnp.zeros_like(dv)

            def visit(j, part):
                at = pl.ds(pl.multiple_of(base + part * half, 16), half)
                cut = slice(part * half, (part + 1) * half)
                s = mm(kv_ref[at, :HEAD], q_t[j]) * (SCALE * LOG2E)
                log = rows[j, 1:2, :]
                pieces = []
                for r in range(runs // 2):
                    run = order_ref[chip * runs + part * (runs // 2) + r]
                    piece = s[r * RUN : (r + 1) * RUN]
                    if diagonal:
                        ahead = lax.broadcasted_iota(jnp.int32, piece.shape, 0) - (
                            lax.broadcasted_iota(jnp.int32, piece.shape, 1) % RUN
                        )
                        seen = ahead <= per_run(j, lambda mine: (mine - run) * RUN)
                        pieces.append(jnp.where(seen, jnp.exp2(piece - log), 0.0))
                    else:
                        hide = per_run(j, lambda mine: jnp.where(run <= mine, 0.0, 1e30))
                        pieces.append(jnp.exp2(piece - (log + hide)))
                p = jnp.concatenate(pieces, axis=0)
                dp = mm(kv_ref[at, HEAD:], g_t[j])
                ds = (p * (dp - rows[j, 0:1, :])).astype(BF)
                dv[cut, :] += mm(p.astype(BF), g2[j])
                dk[cut, :] += mm(ds, q2[j])
                dq_t[j] += mm(keys_t[:, cut], ds)

            def two_runs(j, _):
                visit(j, 0)
                visit(j, 1)
                return 0

            lax.fori_loop(0, runs // 2, two_runs, 0)
            send[step, :, :HEAD] = (dk[...] * SCALE).astype(BF)
            send[step, :, HEAD:] = dv[...].astype(BF)

        def other_chip(step, _):
            chip = (mine + 1 + step) % chips
            one_chip(step, chip, False)
            remote(step, chip, mine).start()
            return 0

        lax.fori_loop(0, chips - 1, other_chip, 0)
        one_chip(chips - 1, mine, True)
        keep = pltpu.make_async_copy(send.at[chips - 1], landed.at[mine], own_sem)
        keep.start()

        def give(i, _):
            at = pl.ds(pl.multiple_of(i * RUN, RUN), RUN)
            cut = pl.ds(pl.multiple_of(i % 2 * 2 * RUN, 2 * RUN), 2 * RUN)
            out = dq_t[i // 2, :, cut].T * SCALE
            dq_ref[at, :HEAD] = out[:RUN]
            dq_ref[at, HEAD:] = out[RUN:]
            return 0

        lax.fori_loop(0, runs, give, 0)
        keep.wait()
        for step in range(chips - 1):
            remote(step, (mine + 1 + step) % chips, mine).wait_send()
            remote(step, (mine + 1 + step) % chips, (mine + 1 + step) % chips).wait_recv()

    smem, vmem = pltpu.SMEM, pltpu.VMEM
    return Work(
        inputs=[(order, smem), (own, smem), (q, vmem), (g, vmem), (o, vmem), (log, vmem), (kv, vmem)],
        outs=[(q.shape, F32)],
        scratch=[
            pltpu.VMEM((runs // 2, 4 * RUN, HEAD), BF),
            pltpu.VMEM((runs // 2, 4 * RUN, HEAD), BF),
            pltpu.VMEM((runs // 2, HEAD, 4 * RUN), BF),
            pltpu.VMEM((runs // 2, HEAD, 4 * RUN), BF),
            pltpu.VMEM((runs // 2, 8, 4 * RUN), F32),
            pltpu.VMEM((runs // 2, HEAD, 4 * RUN), F32),
            pltpu.VMEM((tokens, HEAD), F32),
            pltpu.VMEM((tokens, HEAD), F32),
            pltpu.VMEM((HEAD, tokens), BF),
            pltpu.VMEM((chips, tokens, 2 * HEAD), BF),
            pltpu.SemaphoreType.DMA((chips,)),
            pltpu.SemaphoreType.DMA((chips,)),
            pltpu.SemaphoreType.DMA(()),
        ],
        greets=Plan().chip_shifts(),
        body=body,
    )


def inverse_rms(value):
    return lax.rsqrt(jnp.mean(value * value, axis=-1, keepdims=True) + EPS)


def norm_back(value, inverse, gain, grad):
    scaled = grad * gain
    inner = jnp.sum(scaled * value, axis=-1, keepdims=True)
    return inverse * scaled - value * inverse * inverse * inverse * inner / value.shape[-1]


def finish_kernel(
    gate_ref, up_ref, down_ref, out_ref, query_ref, pair_ref, parts_ref, grad_ref, x_ref, scale_ref,
    middle_ref, last_ref,
    layer_o, input_o, query_o, key_o, value_o, out_o, gate_o, up_o, down_o,
):
    for source, target in (
        (gate_ref, gate_o), (up_ref, up_o), (down_ref, down_o), (out_ref, out_o), (query_ref, query_o)
    ):
        target[...] = source[...].astype(F32)
    for i in range(8):
        to = slice(i * HEAD, (i + 1) * HEAD)
        key_o[:, to] = pair_ref[:, 2 * i * HEAD : (2 * i + 1) * HEAD].astype(F32)
        value_o[:, to] = pair_ref[:, (2 * i + 1) * HEAD : (2 * i + 2) * HEAD].astype(F32)
    x = x_ref[...].astype(F32)
    grad = jnp.sum(parts_ref[...].astype(F32), axis=0)
    input_o[...] = grad_ref[...] + norm_back(x, inverse_rms(x), scale_ref[...], grad)
    last = jnp.sum(last_ref[...].astype(F32), axis=0)
    layer_o[...] = (middle_ref[...] + last).astype(BF)


def finish(gate_up, down, out, qkv, parts, grad, x, scale, middle, last):
    steps = 4
    tokens, width = x.shape

    def rows_of(a, n, offset=0):
        return pl.BlockSpec((n // steps, a.shape[-1]), lambda i: (i + offset, 0))

    def deep(a):
        return pl.BlockSpec((a.shape[0], tokens // steps, width), lambda i: (0, i, 0))

    part = qkv.shape[0] // 2
    specs = [
        rows_of(gate_up, part), rows_of(gate_up, part, steps), rows_of(down, down.shape[0]),
        rows_of(out, out.shape[0]), rows_of(qkv, part), rows_of(qkv, part, steps), deep(parts),
        rows_of(grad, tokens), rows_of(x, tokens), pl.BlockSpec(scale.shape, lambda i: (0, 0)),
        rows_of(middle, tokens), deep(last),
    ]
    shapes = [
        ((tokens, width), BF), ((tokens, width), F32), ((part, 2 * width), F32), ((part, width), F32),
        ((part, width), F32), (out.shape, F32), ((part, gate_up.shape[1]), F32),
        ((part, gate_up.shape[1]), F32), (down.shape, F32),
    ]
    return pl.pallas_call(
        finish_kernel,
        grid=(steps,),
        in_specs=specs,
        out_specs=[pl.BlockSpec((s[0] // steps, s[1]), lambda i: (i, 0)) for s, _ in shapes],
        out_shape=tuple(jax.ShapeDtypeStruct(s, d) for s, d in shapes),
        compiler_params=pltpu.CompilerParams(
            dimension_semantics=("arbitrary",), vmem_limit_bytes=VMEM
        ),
        name="finish",
    )(gate_up, gate_up, down, out, qkv, qkv, parts, grad, x, scale, middle, last)


def dot(a, b):
    return jnp.dot(a, b, preferred_element_type=F32)


def dot_t(a, b):
    return lax.dot_general(a, b, (((0,), (0,)), ((), ())), preferred_element_type=F32)


def summed(parts, count):
    return jnp.sum(parts.reshape((count, -1) + parts.shape[1:]).astype(F32), axis=0)


def row_of(vector):
    return jnp.pad(vector.reshape(1, -1), ((0, 0), (0, 128 - vector.shape[-1])))


def project_kernel(x_ref, w_ref, scale_ref, head_ref, cos_ref, sin_ref, tag_ref, n_ref, p_ref, q_ref, kv_ref):
    step = pl.program_id(0)
    x = jnp.concatenate([x_ref[n, :RUN, :] for n in range(SLOTS)], axis=0).astype(F32)
    low = (x * inverse_rms(x) * scale_ref[...]).astype(BF)
    n_ref[...] = low
    out = mm(low, w_ref[...])
    p_ref[...] = out[:, : 3 * HEAD]
    turned = []
    for h in range(3):
        v = out[:, h * HEAD : (h + 1) * HEAD]
        v = v * inverse_rms(v) * head_ref[h : h + 1, :]
        turned.append((v * cos_ref[...] + pltpu.roll(v, HEAD // 2, 1) * sin_ref[...]).astype(BF))
    q_ref[:, :HEAD] = turned[0]
    q_ref[:, HEAD:] = turned[1]
    at = pl.ds(pl.multiple_of(step * SLOTS * RUN, SLOTS * RUN), SLOTS * RUN)
    kv_ref[at, :HEAD] = turned[2]
    kv_ref[at, HEAD:] = out[:, 3 * HEAD :].astype(BF)

    @pl.when(step == 0)
    def _():
        kv_ref[pl.ds(8 * RUN, TAG), :] = tag_ref[...]


def project(x, w, scale, head_scale, cos, sin, tag):
    width = x.shape[-1]
    group = 8 * RUN

    def fixed(a):
        return pl.BlockSpec(a.shape, lambda i: (0,) * a.ndim)

    def moving(n):
        return pl.BlockSpec((SLOTS * RUN, n), lambda i: (i, 0))

    return pl.pallas_call(
        project_kernel,
        grid=(8 // SLOTS,),
        in_specs=[
            pl.BlockSpec((SLOTS, X_ROWS, width), lambda i: (i, 0, 0)),
            fixed(w), fixed(scale), fixed(head_scale), moving(HEAD), moving(HEAD), fixed(tag),
        ],
        out_specs=[
            moving(width), moving(3 * HEAD), moving(2 * HEAD),
            pl.BlockSpec((KV_ROWS, 2 * HEAD), lambda i: (0, 0)),
        ],
        out_shape=(
            jax.ShapeDtypeStruct((group, width), BF),
            jax.ShapeDtypeStruct((group, 3 * HEAD), F32),
            jax.ShapeDtypeStruct((group, 2 * HEAD), BF),
            jax.ShapeDtypeStruct((KV_ROWS, 2 * HEAD), BF),
        ),
        compiler_params=pltpu.CompilerParams(
            dimension_semantics=("arbitrary",), vmem_limit_bytes=VMEM
        ),
        name="project",
    )(x, w, scale, head_scale, cos, sin, tag)


def unproject_kernel(
    kv_ref, t_ref, p_ref, x_ref, w_ref, head_ref, cos_ref, sin_ref, mlp_ref,
    g_ref, n_ref, tile_ref, attn_acc, head_acc,
):
    step = pl.program_id(0)

    @pl.when(step == 0)
    def _():
        attn_acc[...] = jnp.zeros_like(attn_acc)
        head_acc[...] = jnp.zeros_like(head_acc)

    kv = kv_ref[0].astype(F32)
    for chip in range(1, 8):
        kv = kv + kv_ref[chip].astype(F32)
    for h in range(3):
        turn = kv[:, :HEAD] if h == 2 else t_ref[:, h * HEAD : (h + 1) * HEAD]
        grad = turn * cos_ref[...] - pltpu.roll(turn, HEAD // 2, 1) * sin_ref[...]
        v = p_ref[:, h * HEAD : (h + 1) * HEAD]
        inverse = inverse_rms(v)
        back = norm_back(v, inverse, head_ref[h : h + 1, :], grad)
        g_ref[:, h * HEAD : (h + 1) * HEAD] = back.astype(BF)
        head_acc[h // 2 : h // 2 + 1, :] += jnp.sum(grad * v * inverse, axis=0, keepdims=True)
    g_ref[:, 3 * HEAD :] = kv[:, HEAD:].astype(BF)
    wide = mm(g_ref[...], w_ref[...], NT)
    n_ref[...] = wide.astype(BF)
    x = jnp.concatenate([x_ref[n, :RUN, :] for n in range(SLOTS)], axis=0).astype(F32)
    attn_acc[...] += jnp.sum(wide * x * inverse_rms(x), axis=0, keepdims=True)

    @pl.when(step == pl.num_programs(0) - 1)
    def _():
        tile_ref[...] = jnp.zeros_like(tile_ref)
        for j in range(8):
            tile_ref[j * 8 : j * 8 + 1, :] = attn_acc[:, j * 128 : (j + 1) * 128]
            tile_ref[j * 8 + 1 : j * 8 + 2, :] = mlp_ref[:, j * 128 : (j + 1) * 128]
            tile_ref[j * 8 + 2 : j * 8 + 4, :] = head_acc[...]


def unproject(kv_parts, turn, pre, x, w, head_scale, cos, sin, mlp_part):
    width = x.shape[-1]
    group = 8 * RUN

    def fixed(a):
        return pl.BlockSpec(a.shape, lambda i: (0,) * a.ndim)

    def moving(n):
        return pl.BlockSpec((SLOTS * RUN, n), lambda i: (i, 0))

    return pl.pallas_call(
        unproject_kernel,
        grid=(8 // SLOTS,),
        in_specs=[
            pl.BlockSpec((8, SLOTS * RUN, 2 * HEAD), lambda i: (0, i, 0)),
            moving(2 * HEAD), moving(3 * HEAD),
            pl.BlockSpec((SLOTS, X_ROWS, width), lambda i: (i, 0, 0)),
            fixed(w), fixed(head_scale), moving(HEAD), moving(HEAD), fixed(mlp_part),
        ],
        out_specs=[moving(4 * HEAD), moving(width), pl.BlockSpec((64, 128), lambda i: (0, 0))],
        out_shape=(
            jax.ShapeDtypeStruct((group, 4 * HEAD), BF),
            jax.ShapeDtypeStruct((group, width), BF),
            jax.ShapeDtypeStruct((64, 128), F32),
        ),
        scratch_shapes=[pltpu.VMEM((1, width), F32), pltpu.VMEM((2, HEAD), F32)],
        compiler_params=pltpu.CompilerParams(
            dimension_semantics=("arbitrary",), vmem_limit_bytes=VMEM
        ),
        name="unproject",
    )(kv_parts, turn, pre, x, w, head_scale, cos, sin, mlp_part)


def local(
    hidden_in, positions, attn_gain, query_weight, key_matrix, value_matrix, output_weight,
    query_norm_gain, key_gain, mlp_gain, gate_weight, up_weight, down_weight, cotangent,
):
    hidden = hidden_in[0]
    cot = cotangent[0]
    tokens, width = hidden.shape
    group = 8 * tokens
    ff = gate_weight.shape[1] // 8
    part = width // 8
    core = lax.axis_index("ctx") % 2
    def rows(size):
        return lambda ref: (lambda io, n: io[ref].at[pl.ds(pl.multiple_of(n * size, size), size)])

    gain_tile = jnp.concatenate(
        [row_of(g.astype(F32)) for g in (attn_gain, mlp_gain, query_norm_gain, key_gain)]
        + [jnp.zeros((4, 128), F32)],
        axis=0,
    )
    own_run = (positions[:, :1] // RUN).astype(BF)
    tagged = jnp.concatenate([hidden, jnp.broadcast_to(own_run, (TAG, width))], axis=0)
    plan = Plan()
    relays = [plan.gather_tokens(0, 5, X_ROWS)]
    plan.gather_group(1, 6, 8)
    relays += [
        plan.weights(2, 7, part, 256, 0),
        plan.weights(3, 7, part, 128, 256),
        plan.weights(4, 7, part, 128, 384),
    ]
    for relay in relays:
        relay()
    x_all, gains, w_qkv = exchange(
        plan, 1, (((8 * X_ROWS, width), BF), ((64, 128), F32), ((width, 512), BF)),
        tagged, gain_tile, query_weight, key_matrix, value_matrix,
    )
    gains = gains.reshape(8, 8, 128)
    attn_scale = gains[:, 0].reshape(1, width)
    mlp_scale = gains[:, 1].reshape(1, width)
    query_scale = gains[:, 2, :16].reshape(1, HEAD)
    key_scale = gains[:, 3, :16].reshape(1, HEAD)
    x_all = x_all.reshape(8, X_ROWS, width)
    own_bf = x_all[:, RUN, 0]
    own = own_bf.astype(jnp.int32)
    head_scale = jnp.concatenate([query_scale, query_scale, key_scale], axis=0)
    place_rows = (own[:, None] * RUN + jnp.arange(RUN, dtype=jnp.int32)[None, :]).reshape(group)
    frequency = 1.0 / THETA ** (jnp.arange(0, HEAD, 2, dtype=F32) / HEAD)
    angle = place_rows.astype(F32)[:, None] * jnp.tile(frequency, 2)[None, :]
    sign = jnp.where(jnp.arange(HEAD) < HEAD // 2, -1.0, 1.0).astype(F32)
    cos, sin = jnp.cos(angle), jnp.sin(angle) * sign[None, :]
    tag = jnp.pad(jnp.broadcast_to(own_bf[None, :], (TAG, 8)), ((0, 0), (0, 2 * HEAD - 8)))
    norm_one, pre, queries, kv = project(x_all, w_qkv, attn_scale, head_scale, cos, sin, tag)

    plan = Plan()
    own_kv = block(4, At.chip, KV_ROWS)
    side_kv = block(4, lambda at: at.but(y=1 - at.y).chip(), KV_ROWS)
    half = group // 2

    def upper(io, at):
        return io[4].at[pl.ds(pl.multiple_of(at.chip() * KV_ROWS, 16), half)]

    def lower(io, at):
        return io[4].at[pl.ds(pl.multiple_of(at.chip() * KV_ROWS + half, 16), KV_ROWS - half)]

    def left(of, flip):
        return lambda io, at: of(io, at.but(x=(at.x + 3) % 4, y=1 - at.y if flip else at.y))

    def right(of, flip):
        return lambda io, at: of(io, at.but(x=(at.x + 1) % 4, y=1 - at.y if flip else at.y))

    side = plan.add(Shift(y=1), full(0), own_kv)
    right_id = plan.add(Shift(x=1), full(0), own_kv)
    left_id = plan.add(Shift(x=-1), full(0), own_kv)
    plan.add(None, full(0), own_kv)
    relay_tokens = plan.gather_tokens(1, 5, tokens)
    relays = [plan.weights(2, 6, part, ff, 0), plan.weights(3, 6, part, ff, ff)]
    side_right = plan.add(Shift(x=1), side_kv, side_kv, needs=[side])
    side_left = plan.add(Shift(x=-1), side_kv, side_kv, needs=[side])
    plan.add(Shift(x=1), left(upper, 0), left(upper, 0), needs=[right_id])
    plan.add(Shift(x=-1), right(lower, 0), right(lower, 0), needs=[left_id])
    relay_tokens()
    plan.add(Shift(x=1), left(upper, 1), left(upper, 1), needs=[side_right])
    plan.add(Shift(x=-1), right(lower, 1), right(lower, 1), needs=[side_left])
    for relay in relays:
        relay()
    kv_all, cot_all, w_gu = exchange(
        plan, 2, (((8 * KV_ROWS, 256), BF), ((group, width), BF), ((width, 2 * ff), BF)),
        kv, cot, gate_weight, up_weight,
    )
    order = kv_all.reshape(8, KV_ROWS, 256)[:, 8 * RUN, :8].reshape(64).astype(jnp.int32)
    attention, log_total = attention_forward(order, own, queries, kv_all)
    mixed = attention.astype(BF)
    branch_part = dot(mixed, output_weight).astype(BF)

    plan = Plan()
    plan.return_tokens(0, 1, tokens)
    (branch,) = exchange(plan, 3, (((group, width), BF),), branch_part)
    residual = hidden.astype(F32)
    middle = residual + summed(branch, 8)
    mlp_inverse = inverse_rms(middle)
    norm_two_own = (middle * mlp_inverse * mlp_scale).astype(BF)
    plan = Plan()
    plan.gather_tokens(0, 1, tokens)()
    (norm_two,) = exchange(plan, 4, (((group, width), BF),), norm_two_own)

    gate_up = dot(norm_two, w_gu)
    gate, up = gate_up[:, :ff], gate_up[:, ff:]
    sigma = jax.nn.sigmoid(gate)
    swish = gate * sigma
    inner = (swish * up).astype(BF)
    inner_grad = lax.dot_general(cot_all, down_weight, NT, preferred_element_type=F32)
    gate_up_grad = jnp.concatenate(
        [
            (inner_grad * up * sigma * (1.0 + gate * (1.0 - sigma))).astype(BF),
            (inner_grad * swish).astype(BF),
        ],
        axis=1,
    )
    norm_two_part = lax.dot_general(gate_up_grad, w_gu, NT, preferred_element_type=F32).astype(BF)
    gate_up_wgrad = dot_t(norm_two, gate_up_grad).astype(BF).reshape(8, part, 2 * ff)
    down_wgrad = dot_t(inner, cot_all).astype(BF)

    def theirs(ref, size):
        def pick(io, at):
            cut = pl.ds(pl.multiple_of((1 - at.c) * size, size), size)
            return io[ref].at[..., cut]

        return pick

    def my_half(both, got):
        size = got.shape[-1]
        mine = lax.dynamic_slice_in_dim(both, core * size, size, axis=both.ndim - 1)
        return (mine.astype(F32) + got.astype(F32)).astype(BF)

    plan = Plan()
    plan.return_tokens(0, 3, tokens)
    plan.add(Shift(c=1), theirs(1, ff), full(4))
    plan.add(Shift(c=1), theirs(2, width // 2), full(5))
    norm_two_parts, gate_up_got, down_got = exchange(
        plan, 5, (((group, width), BF), ((8, part, ff), BF), ((ff, width // 2), BF)),
        norm_two_part, gate_up_wgrad, down_wgrad,
    )
    norm_two_grad = summed(norm_two_parts, 8)
    middle_grad = cot.astype(F32) + norm_back(middle, mlp_inverse, mlp_scale, norm_two_grad)
    mlp_gain_part = jnp.sum(norm_two_grad * middle * mlp_inverse, axis=0)
    branch_grad_own = middle_grad.astype(BF)
    gate_up_half = my_half(gate_up_wgrad, gate_up_got)
    down_half = my_half(down_wgrad, down_got)

    plan = Plan()
    plan.gather_tokens(0, 3, tokens)()
    plan.scatter_chips(
        lambda io, n: io[1].at[:, pl.ds(pl.multiple_of(n * 16, 16), 16)], lambda io, n: io[4].at[n]
    )
    plan.scatter_chips(rows(ff // 8)(2), lambda io, n: io[5].at[n])
    branch_grad, gate_up_pieces, down_pieces = exchange(
        plan, 6, (((group, width), BF), ((8, 8, 16, ff), BF), ((8, ff // 8, width // 2), BF)),
        branch_grad_own, gate_up_half, down_half,
    )
    mixed_grad = lax.dot_general(branch_grad, output_weight, NT, preferred_element_type=F32).astype(BF)
    output_wgrad = dot_t(mixed, branch_grad).astype(BF)
    down_part = dot(inner, down_weight).astype(BF)
    gate_up_sum = jnp.sum(gate_up_pieces.astype(F32), axis=0).astype(BF)
    down_sum = jnp.sum(down_pieces.astype(F32), axis=0).astype(BF)

    plan = Plan()
    pair = 2 * tokens
    for k in (1, 3, 2):
        plan.add(
            Shift(z=k),
            block(0, lambda at, k=k: (at.z + k) % 4, pair),
            block(4, lambda at: at.z, pair),
        )
    plan.add(None, block(0, lambda at: at.z, pair), block(4, lambda at: at.z, pair))
    plan.add(Shift(c=1), theirs(1, width // 2), full(5))
    plan.scatter_group(
        lambda io, n: io[2].at[n],
        lambda io, n: io[6].at[:, pl.ds(pl.multiple_of(n * ff, ff), ff)],
    )
    n_rows = output_wgrad.shape[0]
    kv_parts, down_parts, output_got, gate_up_own, query_turn = exchange(
        plan, 7,
        (
            ((8, group, 256), BF), ((group, width), BF), ((n_rows, width // 2), BF),
            ((16, 8 * ff), BF),
        ),
        down_part, output_wgrad, gate_up_sum,
        work=attention_backward(order, own, queries, mixed_grad, attention, log_total, kv_all),
    )
    down_pair = summed(down_parts, 4).astype(BF)
    output_half = my_half(output_wgrad, output_got)
    qkv_grad, norm_one_part, gain_parts = unproject(
        kv_parts, query_turn, pre, x_all, w_qkv, head_scale, cos, sin,
        mlp_gain_part.reshape(1, width),
    )

    plan = Plan()
    plan.return_tokens(0, 3, tokens)
    plan.scatter_chips(rows(n_rows // 8)(1), lambda io, n: io[5].at[n])
    plan.scatter_group(rows(8)(2), rows(8)(6))
    swap = plan.add(Shift(c=1), theirs(7, 256), full(8), stage=1)
    plan.scatter_chips(
        lambda io, n: io[9].at[:, pl.ds(pl.multiple_of(n * 16, 16), 16)],
        lambda io, n: io[4].at[n],
        stage=2,
    )

    def weight_grads(me, more, outs, made, scratch, begin, arrive):
        norm_ref, grad_ref = more
        both, got, total = scratch
        mine = pl.ds(pl.multiple_of(me.c * 256, 256), 256)

        def some_rows(j, _):
            cut = pl.ds(pl.multiple_of(j * part, part), part)
            both[j] = mm(norm_ref[:, cut], grad_ref[...], TN).astype(BF)
            return 0

        def add(j, _):
            total[j] = (both[j, :, mine].astype(F32) + got[j].astype(F32)).astype(BF)
            return 0

        lax.fori_loop(0, 8, some_rows, 0)
        begin(1)
        arrive(swap)
        lax.fori_loop(0, 8, add, 0)
        begin(2)

    def stacked_rows(ref, size, total):
        def land(io, chip, c):
            return io[ref].at[pl.ds(pl.multiple_of(c * total + chip * size, size), size)]

        return land, lambda io, c: io[ref].at[pl.ds(pl.multiple_of(c * total, total), total)]

    def side_columns(ref, size):
        def at_core(c):
            return pl.ds(pl.multiple_of(c * (width // 2), width // 2), width // 2)

        def land(io, chip, c):
            return io[ref].at[pl.ds(pl.multiple_of(chip * size, size), size), at_core(c)]

        return land, lambda io, c: io[ref].at[:, at_core(c)]

    norm_one_parts, qkv_pieces, output_pieces, gain_sums = exchange(
        plan, 8,
        (
            ((group, width), BF), ((8, 8, 16, 256), BF), ((8, n_rows // 8, width // 2), BF),
            ((64, 128), F32),
        ),
        norm_one_part, output_half, gain_parts,
        work=Work(
            [(norm_one, pltpu.VMEM), (qkv_grad, pltpu.VMEM)], [],
            [
                pltpu.VMEM((8, part, 512), BF), pltpu.VMEM((8, part, 256), BF),
                pltpu.VMEM((8, part, 256), BF),
            ],
            [], weight_grads,
        ),
    )
    qkv_sum = jnp.sum(qkv_pieces.astype(F32), axis=0).astype(BF)
    output_sum = jnp.sum(output_pieces.astype(F32), axis=0).astype(BF)
    gain_sum = summed(gain_sums, 8)

    plan = Plan()
    to_group = plan.scatter_group(
        lambda io, n: io[0].at[n],
        lambda io, n: io[6].at[:, pl.ds(pl.multiple_of(n * 256, 256), 256)],
    )
    later = [
        plan.gather_chips(full(4), *stacked_rows(11, 16, part)),
        plan.gather_chips(full(5), *side_columns(12, ff // 8)),
        plan.gather_chips(full(1), *side_columns(8, n_rows // 8)),
    ]
    plan.gather_context(2, 9, 8)
    own_block = block(3, lambda at: at.c, tokens)
    other_block = block(3, lambda at: 1 - at.c, tokens)

    def landed(n):
        return lambda io, at: io[10].at[pl.ds(n * tokens, tokens)]

    plan.add(Shift(d=1), own_block, landed(1), away)
    plan.add(Shift(d=1, c=1), other_block, landed(1), away)
    plan.add(None, own_block, landed(0), home)
    plan.add(Shift(c=1), other_block, landed(0), home)
    later.append(plan.gather_chips(full(6), *stacked_rows(7, 16, part), needs=to_group))
    for relay, _ in later:
        relay()
    for _, share in later:
        share()
    _, qkv_final, output_final, gain_all, down_last, gate_up_final, down_final = exchange(
        plan, 9,
        (
            ((16, 2048), BF), ((2 * part, 2048), BF), ((n_rows, width), BF), ((128, 128), F32),
            ((2 * tokens, width), BF), ((2 * part, 8 * ff), BF), ((ff, width), BF),
        ),
        qkv_sum, output_sum, gain_sum, down_pair, gate_up_own, down_sum,
    )
    layer_out, input_grad, query_wgrad, key_wgrad, value_wgrad, output_wgrad, gate_wgrad, up_wgrad, down_wgrad = finish(
        gate_up_final, down_final, output_final, qkv_final, norm_one_parts.reshape(8, tokens, width),
        middle_grad, hidden, attn_scale, middle, down_last.reshape(2, tokens, width),
    )
    gain_total = summed(gain_all, 16)
    head = lax.axis_index("dp") * 4 + lax.axis_index("fsdp")
    return (
        layer_out[None],
        input_grad[None],
        gain_total[0],
        query_wgrad,
        key_wgrad,
        value_wgrad,
        output_wgrad,
        lax.dynamic_slice_in_dim(gain_total[2], head * 16, 16),
        lax.dynamic_slice_in_dim(gain_total[3], head * 16, 16),
        gain_total[1],
        gate_wgrad,
        up_wgrad,
        down_wgrad,
    )


def solution(mesh):
    tokens = P("dp", ("ctx", "fsdp"), None)
    places = P("dp", ("ctx", "fsdp"))
    vector = P(("dp", "fsdp"))
    matrix = P(("dp", "fsdp"), None)
    in_specs = (
        tokens, places, vector, matrix, matrix, matrix, matrix,
        vector, vector, vector, matrix, matrix, matrix, tokens,
    )
    out_specs = (
        tokens, tokens, vector, matrix, matrix, matrix, matrix,
        vector, vector, vector, matrix, matrix, matrix,
    )
    return jax.shard_map(local, mesh=mesh, in_specs=in_specs, out_specs=out_specs, check_vma=False)
```
